32 devices in a mesh: seq: 32 (over z, y, x, core).
Axes of the slice: x: 2, y: 2, z: 4, core: 2. Of those that a mesh axis runs over, the one named last changes fastest.
Arguments:
- tokens: bfloat16 [4096, 1600], P('seq'), may hold values from -6 to 6
- seg_ids: int32 [4096], P('seq'), may hold values from 0 to 8, as said below
- meta_index: int32 [4096], P('seq'), may hold values from 0 to 128, as said below
- meta_table: bfloat16 [128, 1600], replicated, may hold values from -6 to 6
- mixer_gain: float32 [1600], replicated, may hold values from 0.5 to 1.5
- attn_weight: bfloat16 [1600, 3840], replicated, may hold values from -0.15625 to 0.15625
- ssm_weight: bfloat16 [1600, 6400], replicated, may hold values from -0.15625 to 0.15625
- select_weight: bfloat16 [1600, 82], replicated, may hold values from -0.15625 to 0.15625
- conv_weight: float32 [4, 3200], replicated, may hold values from -4 to 4
- step_bias: float32 [50], replicated, may hold values from -1 to 1
- decay_log: float32 [50], replicated, may hold values from -9 to -3
- skip_gain: float32 [50], replicated, may hold values from 0.5 to 1.5
- ssm_down: bfloat16 [3200, 1600], replicated, may hold values from -0.109375 to 0.109375
- attn_beta: float32 [1600], replicated, may hold values from 0.5 to 1.5
- ssm_beta: float32 [1600], replicated, may hold values from 0.5 to 1.5
- ffn_gain: float32 [1600], replicated, may hold values from 0.5 to 1.5
- gate_up: bfloat16 [1600, 11008], replicated, may hold values from -0.15625 to 0.15625
- ffn_down: bfloat16 [5504, 1600], replicated, may hold values from -0.078125 to 0.078125
- cotangent: bfloat16 [4096, 1600], P('seq'), may hold values from -6 to 6
Outputs:
- layer_out: bfloat16 [4096, 1600], P('seq')
- grad_tokens: bfloat16 [4096, 1600], P('seq')
- grad_meta: float32 [128, 1600], replicated
- grad_mixer_gain: float32 [1600], replicated
- grad_attn: float32 [1600, 3840], P(None, 'seq')
- grad_ssm: float32 [1600, 6400], P(None, 'seq')
- grad_select: float32 [1600, 82], replicated
- grad_conv: float32 [4, 3200], replicated
- grad_step_bias: float32 [50], replicated
- grad_decay: float32 [50], replicated
- grad_skip: float32 [50], replicated
- grad_ssm_down: float32 [3200, 1600], P('seq')
- grad_attn_beta: float32 [1600], replicated
- grad_ssm_beta: float32 [1600], replicated
- grad_ffn_gain: float32 [1600], replicated
- grad_gate_up: float32 [1600, 11008], P(None, 'seq')
- grad_ffn_down: float32 [5504, 1600], P('seq')
The draws below stay inside these ranges and needn't reach their ends.
Inputs may be any that keep to these rules, and one draw needn't show every extreme that they name: `seg_ids`: item numbers never fall along the tokens. Tokens 4 * 128 up to 2560 hold items of exactly 2048 tokens, each starting 2048 tokens after the one before; every other item holds more than 128 tokens and fewer than 384. No token lies 2048 or more positions after the first token of its item. `meta_index`: A token's place in its item where that is below 128, else 128.
All inputs are finite; a program needn't handle non-finite values.
Results may differ from the reference program's by a relative error of at most 0.018.
Values may be sent and summed in bfloat16 or wider, within the bound.
A program may use at most 512 MiB of HBM per device.

```python
import math
import jax
import jax.numpy as jnp
from jax import lax

D = 1600
HEADS = 25
GROUPS = 5
HEAD = 64
INNER = 3200
STATE = 16
CONV = 4
FF = 5504
META = 128
SHEAD = 64
TOK_DEV = 128
TOKENS = 4096
LONG = 2048


def item_layout(key):
    half_tokens = TOKENS // 2
    pair_length = 4 * TOK_DEV
    pair_count = half_tokens // pair_length
    long_start = 4 * TOK_DEV
    long_count = half_tokens // LONG
    jitter = jax.random.randint(jax.random.fold_in(key, 11), (pair_count,), 0, TOK_DEV // 2 + 1)
    position = jnp.arange(TOKENS, dtype=jnp.int32)
    in_long = (position >= long_start) & (position < long_start + half_tokens)
    after_long = position >= long_start + half_tokens
    short_pos = jnp.where(position < long_start, position, position - half_tokens)
    pair_index = jnp.clip(short_pos // pair_length, 0, pair_count - 1)
    within = short_pos - pair_index * pair_length
    first_length = 2 * TOK_DEV - jitter[pair_index]
    second = (within >= first_length).astype(jnp.int32)
    short_seg = 2 * pair_index + second + jnp.where(after_long, long_count, 0)
    short_place = within - second * first_length
    long_off = position - long_start
    segment = jnp.where(in_long, 2 + long_off // LONG, short_seg)
    item_place = jnp.where(in_long, long_off % LONG, short_place)
    return (segment.astype(jnp.int32), jnp.minimum(item_place, META).astype(jnp.int32))


def draw_seg_ids(key, part):
    return item_layout(key)[0]


def draw_meta_index(key, part):
    return item_layout(key)[1]


def level_of(own_key, extent, split, smallest, largest):
    gain = 1.0
    for axis_at, shards_of in split:
        steps = jax.random.uniform(jax.random.fold_in(jax.random.fold_in(own_key, 6), axis_at), (shards_of,), jnp.float32, smallest / len(split), largest / len(split))
        gain = gain * jnp.repeat(jnp.exp(steps), extent[axis_at] // shards_of).reshape((-1,) + (1,) * (len(extent) - 1 - axis_at))
    return gain


def gaussian(own_key, shape, scale, limit, cuts=(), kind=jnp.bfloat16):
    values = jax.random.normal(own_key, shape, jnp.float32) * scale
    if len(cuts) > 0:
        values = level_of(own_key, shape, cuts, -0.22, 0.18) * values
    return jnp.clip(values, min=-limit, max=limit).astype(kind)


def setup_inputs(seed: int = 0) -> dict:
    key_of = jax.random.split(jax.random.key(seed), 20)
    return {
        "tokens": gaussian(key_of[0], (TOKENS, D), 1.0, 6.0, ((0, 32),)),
        "seg_ids": draw_seg_ids(jax.random.fold_in(key_of[19], 71), 0),
        "meta_index": draw_meta_index(jax.random.fold_in(key_of[19], 71), 0),
        "meta_table": gaussian(key_of[3], (META, D), 1.0, 6.0),
        "mixer_gain": jnp.clip(1.0 + 0.1 * jax.random.normal(key_of[4], (D,), jnp.float32), 0.5, 1.5),
        "attn_weight": gaussian(key_of[5], (D, 2 * D + 2 * GROUPS * HEAD), D ** -0.5, 0.15625),
        "ssm_weight": gaussian(key_of[6], (D, 2 * INNER), D ** -0.5, 0.15625),
        "select_weight": gaussian(key_of[7], (D, 2 * STATE + INNER // SHEAD), D ** -0.5, 0.15625),
        "conv_weight": gaussian(key_of[8], (CONV, INNER), 1.0, 4.0, (), jnp.float32),
        "step_bias": jnp.clip(jax.random.uniform(key_of[9], (INNER // SHEAD,), jnp.float32, -1.0, 1.0), -1.0, 1.0),
        "decay_log": jnp.clip(jax.random.uniform(key_of[10], (INNER // SHEAD,), jnp.float32, -9.0, -3.0), -9.0, -3.0),
        "skip_gain": jnp.clip(jax.random.uniform(key_of[11], (INNER // SHEAD,), jnp.float32, 0.5, 1.5), 0.5, 1.5),
        "ssm_down": gaussian(key_of[12], (INNER, D), INNER ** -0.5, 0.109375),
        "attn_beta": jnp.clip(1.0 + 0.1 * jax.random.normal(key_of[13], (D,), jnp.float32), 0.5, 1.5),
        "ssm_beta": jnp.clip(1.0 + 0.1 * jax.random.normal(key_of[14], (D,), jnp.float32), 0.5, 1.5),
        "ffn_gain": jnp.clip(1.0 + 0.1 * jax.random.normal(key_of[15], (D,), jnp.float32), 0.5, 1.5),
        "gate_up": gaussian(key_of[16], (D, 2 * FF), D ** -0.5, 0.15625),
        "ffn_down": gaussian(key_of[17], (FF, D), FF ** -0.5, 0.078125),
        "cotangent": gaussian(key_of[18], (TOKENS, D), 1.0, 6.0, ((0, 32),)),
    }


@jax.custom_vjp
def low(v):
    return lax.optimization_barrier(v.astype(jnp.bfloat16)).astype(jnp.float32)

@jax.custom_vjp
def low_back(v):
    return v

def low_keep(v):
    return (low(v), None)

def low_pass(kept, grad):
    return (grad,)

def back_keep(v):
    return (v, None)

def back_low(kept, grad):
    return (low(grad),)
low.defvjp(low_keep, low_pass)
low_back.defvjp(back_keep, back_low)
eps = 1e-05
highest = lax.Precision.HIGHEST

def matmul(left, right):
    return jnp.dot(left, right, precision=highest)

def rms_scale(entries):
    return entries * lax.rsqrt(lax.optimization_barrier(jnp.mean(entries * entries, axis=-1, keepdims=True)) + eps)

def attention_all(queries, keys, values, seg_ids):
    block = min(512, TOKENS)
    kv_width = GROUPS * HEAD
    per_group = HEADS // GROUPS
    score_scale = 1.0 / math.sqrt(HEAD)
    keys_pad = jnp.concatenate([jnp.zeros((LONG, kv_width), jnp.float32), keys], 0)
    values_pad = jnp.concatenate([jnp.zeros((LONG, kv_width), jnp.float32), values], 0)
    seg_pad = jnp.concatenate([jnp.full((LONG,), -1, jnp.int32), seg_ids], 0)

    def one_block(block_index):
        start = (block_index * block).astype(jnp.int32)
        query_rows = lax.dynamic_slice_in_dim(queries, start, block, 0).reshape(block, GROUPS, per_group, HEAD)
        key_rows = lax.dynamic_slice_in_dim(keys_pad, start, LONG + block, 0).reshape(LONG + block, GROUPS, HEAD)
        value_rows = lax.dynamic_slice_in_dim(values_pad, start, LONG + block, 0).reshape(LONG + block, GROUPS, HEAD)
        query_seg = lax.dynamic_slice_in_dim(seg_ids, start, block, 0)
        key_seg = lax.dynamic_slice_in_dim(seg_pad, start, LONG + block, 0)
        query_pos = jnp.arange(block, dtype=jnp.int32) + LONG
        key_pos = jnp.arange(LONG + block, dtype=jnp.int32)
        allowed = (query_seg[:, None] == key_seg[None, :]) & (key_pos[None, :] <= query_pos[:, None])
        scores = low_back(jnp.einsum('tgjd,rgd->gjtr', query_rows, key_rows, precision=highest) * score_scale)
        scores = jnp.where(allowed, scores, -1e+30)
        probs = jax.nn.softmax(scores, axis=-1)
        mixed = jnp.einsum('gjtr,rgd->tgjd', low(probs), value_rows, precision=highest)
        return mixed.reshape(block, HEADS * HEAD)
    outputs = lax.map(jax.checkpoint(one_block), jnp.arange(TOKENS // block, dtype=jnp.int32))
    return outputs.reshape(TOKENS, HEADS * HEAD)

def conv_all(conv_in, conv_weight, seg_ids):
    summed = conv_weight[0] * conv_in
    for tap_lag in range(1, CONV):
        lagged = jnp.concatenate([jnp.zeros((tap_lag, INNER), jnp.float32), conv_in[:TOKENS - tap_lag]], 0)
        lag_seg = jnp.concatenate([jnp.full((tap_lag,), -1, jnp.int32), seg_ids[:TOKENS - tap_lag]], 0)
        summed = summed + conv_weight[tap_lag] * jnp.where((lag_seg == seg_ids)[:, None], lagged, 0.0)
    return jax.nn.silu(summed)

def scan_all(conv_out, b_proj, c_proj, step_size, log_decay, skip_gain, seg_ids):
    block = min(512, TOKENS)
    count = TOKENS // block
    sheads = INNER // SHEAD
    lower_tri = (jnp.arange(block)[:, None] >= jnp.arange(block)[None, :]).astype(jnp.float32)

    def one_block(carry, pieces):
        held_state, seg_prev = carry
        x_block, b_block, c_block, step_block, decay_block, seg_block = pieces
        cum_decay = matmul(lower_tri, decay_block)
        same_item = (seg_block[:, None] == seg_block[None, :]) & (lower_tri > 0)
        exponent = jnp.where(same_item[None], cum_decay.T[:, :, None] - cum_decay.T[:, None, :], -1e+30)
        weights = jnp.exp(exponent) * matmul(c_block, b_block.T)[None]
        heads_x = x_block.reshape(block, sheads, SHEAD)
        scaled_x = heads_x * step_block[:, :, None]
        local_part = jnp.einsum('htr,rhp->thp', weights, scaled_x, precision=highest)
        follow = (seg_block == seg_prev).astype(jnp.float32)
        carry_weight = jnp.exp(cum_decay) * follow[:, None]
        carried = jnp.einsum('th,hpn,tn->thp', carry_weight, held_state, c_block, precision=highest)
        outputs = local_part + carried + skip_gain[None, :, None] * heads_x
        last_same = (seg_block == seg_block[-1]).astype(jnp.float32)
        last_weight = jnp.exp(cum_decay[-1][None, :] - cum_decay) * last_same[:, None]
        fresh_state = jnp.einsum('rh,rhp,rn->hpn', last_weight, scaled_x, b_block, precision=highest)
        held_state = fresh_state + (jnp.exp(cum_decay[-1]) * follow[-1])[:, None, None] * held_state
        return ((held_state, seg_block[-1]), outputs.reshape(block, INNER))
    start_state = (jnp.zeros((sheads, SHEAD, STATE), jnp.float32), jnp.array(-1, dtype=jnp.int32))
    pieces = (conv_out.reshape(count, block, INNER), b_proj.reshape(count, block, STATE), c_proj.reshape(count, block, STATE), step_size.reshape(count, block, sheads), log_decay.reshape(count, block, sheads), seg_ids.reshape(count, block))
    finals, scanned = lax.scan(jax.checkpoint(one_block), start_state, pieces)
    return scanned.reshape(TOKENS, INNER)

def reference(tokens, seg_ids, meta_index, meta_table, mixer_gain, attn_weight, ssm_weight, select_weight, conv_weight, step_bias, decay_log, skip_gain, ssm_down, attn_beta, ssm_beta, ffn_gain, gate_up, ffn_down, cotangent):
    kv_width = GROUPS * HEAD
    is_meta = (meta_index < META)[:, None]
    one_hot = (meta_index[:, None] == jnp.arange(META, dtype=jnp.int32)[None, :]).astype(jnp.float32)

    def forward(tokens, meta_table, mixer_gain, attn_weight, ssm_weight, select_weight, conv_weight, step_bias, decay_log, skip_gain, ssm_down, attn_beta, ssm_beta, ffn_gain, gate_up, ffn_down):
        layer_in = jnp.where(is_meta, matmul(one_hot, meta_table), tokens)
        normed = low(rms_scale(layer_in) * mixer_gain)
        proj_qkv = low_back(low(matmul(normed, attn_weight[:, :D + 2 * kv_width])))
        attended = attention_all(proj_qkv[:, :D], proj_qkv[:, D:D + kv_width], proj_qkv[:, D + kv_width:], seg_ids)
        attended = low_back(low(attended))
        attn_proj = low_back(matmul(attended, attn_weight[:, D + 2 * kv_width:].T))
        ssm_proj = low_back(matmul(normed, ssm_weight))
        select = low_back(matmul(normed, select_weight))
        conv_out = conv_all(ssm_proj[:, :INNER], conv_weight, seg_ids)
        step_size = jax.nn.softplus(select[:, 2 * STATE:] + step_bias)
        log_decay = -step_size * jnp.exp(decay_log)
        scanned = scan_all(conv_out, select[:, :STATE], select[:, STATE:2 * STATE], step_size, log_decay, skip_gain, seg_ids)
        gated = low_back(low(scanned * jax.nn.silu(ssm_proj[:, INNER:])))
        ssm_proj_out = low_back(matmul(gated, ssm_down))
        hidden1 = layer_in + attn_beta * rms_scale(attn_proj) + ssm_beta * rms_scale(ssm_proj_out)
        ffn_in = low(rms_scale(hidden1) * ffn_gain)
        gate_vals = low_back(matmul(ffn_in, gate_up))
        hidden = low_back(low(jax.nn.silu(gate_vals[:, :FF]) * gate_vals[:, FF:]))
        return hidden1 + matmul(hidden, ffn_down)
    result, pullback = jax.vjp(forward, tokens.astype(jnp.float32), meta_table.astype(jnp.float32), mixer_gain.astype(jnp.float32), attn_weight.astype(jnp.float32), ssm_weight.astype(jnp.float32), select_weight.astype(jnp.float32), conv_weight.astype(jnp.float32), step_bias.astype(jnp.float32), decay_log.astype(jnp.float32), skip_gain.astype(jnp.float32), ssm_down.astype(jnp.float32), attn_beta.astype(jnp.float32), ssm_beta.astype(jnp.float32), ffn_gain.astype(jnp.float32), gate_up.astype(jnp.float32), ffn_down.astype(jnp.float32))
    grads = pullback(cotangent.astype(jnp.float32))
    return (result.astype(jnp.bfloat16), grads[0].astype(jnp.bfloat16), grads[1], grads[2], grads[3], grads[4], grads[5], grads[6], grads[7], grads[8], grads[9], grads[10], grads[11], grads[12], grads[13], grads[14], grads[15])
```

```python
from functools import partial
import math

import jax
import jax.numpy as jnp
from jax import lax
from jax.experimental import pallas as pl
from jax.experimental.pallas import tpu as pltpu
from jax.sharding import PartitionSpec as P

HEADS = 25
GROUPS = 5
HEAD = 64
INNER = 3200
STATE = 16
CONV = 4
FF = 5504
META = 128
SHEAD = 64


eps = 1e-05
highest = lax.Precision.HIGHEST


MESH = pl.DeviceIdType.MESH
MIB = 2**20


def flipped(v, k):
    bit = 1 << k
    return jnp.where(lax.rem(v // bit, 2) == 0, v + bit, v - bit)


def flips_of(v, bits):
    out = [v]
    for k in bits:
        out = out + [flipped(o, k) for o in out]
    return out


def thirds(rows):
    most = (rows // 3 + 15) // 16 * 16
    return [(0, most), (most, most), (2 * most, rows - 2 * most)]


def greet(partners):
    barrier = pltpu.get_barrier_semaphore()
    for partner in partners:
        pl.semaphore_signal(barrier, inc=1, device_id=(partner,), device_id_type=MESH)
    pl.semaphore_wait(barrier, len(partners))


def remote(src, dst, send, recv, device):
    return pltpu.make_async_remote_copy(
        src_ref=src,
        dst_ref=dst,
        send_sem=send,
        recv_sem=recv,
        device_id=(device,),
        device_id_type=MESH,
    )


def gather_kernel(arrays, half, *refs):
    ins, out = refs[:arrays], refs[arrays]
    send, recv, core_send, core_recv, local_sem = refs[arrays + 1 :]
    me = lax.axis_index("seq")
    place = lax.rem(me, half)
    bits = half.bit_length() - 1
    greet([flipped(me, k) for k in range(bits)])
    parts = thirds(ins[0].shape[0])
    links = bits - 1
    orders = [[1 + (c + s) % links for s in range(links)] for c in range(3)]
    local = [
        pltpu.make_async_copy(ins[a], out.at[a * half + place], local_sem.at[a])
        for a in range(arrays)
    ]
    for copy in local:
        copy.start()
    sent, handed = [], []
    for step in range(links + 1):
        arriving = []
        for c, (first, count) in enumerate(parts):
            rows = pl.ds(first, count)
            held = flips_of(place, orders[c][:step])
            for a in range(arrays):
                if step < links:
                    for i, b in enumerate(held):
                        place_at = out.at[a * half + b, rows]
                        at = (1 << step) - 1 + i
                        copy = remote(
                            ins[a].at[rows] if i == 0 else place_at,
                            place_at,
                            send.at[a, c, at],
                            recv.at[a, c, at],
                            flipped(me, orders[c][step]),
                        )
                        copy.start()
                        arriving.append(copy)
                new = held if step == 0 else held[len(held) // 2 :]
                for i, b in enumerate(new):
                    place_at = out.at[a * half + b, rows]
                    at = 0 if step == 0 else (1 << (step - 1)) + i
                    copy = remote(
                        ins[a].at[rows] if step == 0 else place_at,
                        place_at,
                        core_send.at[a, c, at],
                        core_recv.at[a, c, at],
                        flipped(me, 0),
                    )
                    copy.start()
                    handed.append(copy)
        for copy in arriving:
            copy.wait_recv()
        sent += arriving
    for copy in sent:
        copy.wait_send()
    for copy in handed:
        copy.wait()
    for copy in local:
        copy.wait()


def gather_half(arrays, half, collective_id):
    count = len(arrays)
    shape = arrays[0].shape
    semaphores = pltpu.SemaphoreType.DMA((count, 3, half // 2))
    return pl.pallas_call(
        partial(gather_kernel, count, half),
        out_shape=jax.ShapeDtypeStruct((count * half,) + shape, arrays[0].dtype),
        in_specs=[pl.BlockSpec(memory_space=pl.ANY)] * count,
        out_specs=pl.BlockSpec(memory_space=pl.ANY),
        scratch_shapes=[semaphores] * 4 + [pltpu.SemaphoreType.DMA((count,))],
        compiler_params=pltpu.CompilerParams(collective_id=collective_id, has_side_effects=True),
        name="gather_half",
    )(*arrays)


def sum_kernel(arrays, half, *refs):
    terms, outs = refs[0], refs[1 : 1 + arrays]
    mine, core_in, link_in, load_sem, send, recv, core_send, core_recv = refs[1 + arrays :]
    me = lax.axis_index("seq")
    place = lax.rem(me, half)
    bits = half.bit_length() - 1
    greet([flipped(me, k) for k in range(bits)])
    parts = thirds(terms.shape[1])
    links = bits - 1
    orders = [[1 + (c + s) % links for s in range(links)] for c in range(3)]
    loads = []
    pairs = half // 2
    for a in range(arrays):
        for i in range(pairs):
            block = 2 * i + lax.rem(place, 2)
            copy = pltpu.make_async_copy(
                terms.at[a * half + block], mine.at[a, i], load_sem.at[a, i]
            )
            copy.start()
            loads.append(copy)
    handed = {}
    for wanted in range(2):
        for c, (first, count) in enumerate(parts):
            rows = pl.ds(first, count)
            kept = flips_of(place, orders[c][1:])
            blocks = kept if wanted else [flipped(b, orders[c][0]) for b in kept]
            for a in range(arrays):
                for i, b in enumerate(blocks):
                    at = wanted * (pairs // 2) + i
                    copy = remote(
                        terms.at[a * half + flipped(b, 0), rows],
                        core_in.at[a, at, rows],
                        core_send.at[a, c, at],
                        core_recv.at[a, c, at],
                        flipped(me, 0),
                    )
                    copy.start()
                    handed[a, c, at] = copy
    for copy in loads:
        copy.wait()
    sent = []
    arriving = {}

    def add(ref, slot, rows, other):
        ref[slot, rows] = (
            ref[slot, rows].astype(jnp.float32) + other[...].astype(jnp.float32)
        ).astype(ref.dtype)

    for step in range(links):
        for c, (first, count) in enumerate(parts):
            rows = pl.ds(first, count)
            kept = flips_of(place, orders[c][step + 1 :])
            for a in range(arrays):
                for i, b in enumerate(kept):
                    out_block = flipped(b, orders[c][step])
                    if step == 0:
                        handed[a, c, i].wait_recv()
                        add(mine.at[a], out_block // 2, rows, core_in.at[a, i, rows])
                    at = pairs - (pairs >> step) + i
                    copy = remote(
                        mine.at[a, out_block // 2, rows],
                        link_in.at[a, at, rows],
                        send.at[a, c, at],
                        recv.at[a, c, at],
                        flipped(me, orders[c][step]),
                    )
                    copy.start()
                    arriving[a, c, at] = copy
                    sent.append(copy)
        if step == 0:
            for c, (first, count) in enumerate(parts):
                rows = pl.ds(first, count)
                for a in range(arrays):
                    for i, b in enumerate(flips_of(place, orders[c][1:])):
                        at = pairs // 2 + i
                        handed[a, c, at].wait_recv()
                        add(mine.at[a], b // 2, rows, core_in.at[a, at, rows])
        for c, (first, count) in enumerate(parts):
            rows = pl.ds(first, count)
            kept = flips_of(place, orders[c][step + 1 :])
            for a in range(arrays):
                for i, b in enumerate(kept):
                    at = pairs - (pairs >> step) + i
                    arriving[a, c, at].wait_recv()
                    add(mine.at[a], b // 2, rows, link_in.at[a, at, rows])
    for a in range(arrays):
        outs[a][...] = mine[a, place // 2]
    for copy in sent:
        copy.wait_send()
    for copy in handed.values():
        copy.wait_send()


def sum_half(terms, arrays, half, collective_id):
    rows, columns = terms.shape[1:]
    pairs = half // 2
    block = (rows, columns)
    semaphores = pltpu.SemaphoreType.DMA((arrays, 3, pairs))
    return pl.pallas_call(
        partial(sum_kernel, arrays, half),
        out_shape=[jax.ShapeDtypeStruct(block, terms.dtype)] * arrays,
        in_specs=[pl.BlockSpec(memory_space=pl.ANY)],
        out_specs=[pl.BlockSpec(memory_space=pltpu.VMEM)] * arrays,
        scratch_shapes=[
            pltpu.VMEM((arrays, pairs) + block, terms.dtype),
            pltpu.VMEM((arrays, pairs) + block, terms.dtype),
            pltpu.VMEM((arrays, pairs) + block, terms.dtype),
            pltpu.SemaphoreType.DMA((arrays, pairs)),
        ]
        + [semaphores] * 4,
        compiler_params=pltpu.CompilerParams(
            collective_id=collective_id, has_side_effects=True, vmem_limit_bytes=60 * MIB
        ),
        name="sum_half",
    )(terms)


def masked_block(at, first_ref, device_index, rows):
    key = lax.broadcasted_iota(jnp.int32, (rows, rows), 0) + at * rows
    query = lax.broadcasted_iota(jnp.int32, (rows, rows), 1) + device_index * rows
    seen = ((key >= first_ref[...]) & (key <= query)).astype(jnp.float32)
    return jnp.concatenate([seen] * (HEADS // GROUPS), 1) > 0.0


def side_by_side(ref, g):
    return jnp.concatenate([ref[g, j] for j in range(HEADS // GROUPS)], 1)


def over_shards(steps_ref, body):
    body(0)

    @pl.loop(1, steps_ref[1] + 1)
    def _(hop):
        body(hop)


def attend_kernel(half, steps_ref, q_ref, kv_ref, first_ref, out_ref, log_ref, top, total, acc):
    device_index, newest = steps_ref[0], half + lax.rem(steps_ref[0], half)
    rows = kv_ref.shape[1]
    top[...] = jnp.full_like(top, -1e30)
    total[...] = jnp.zeros_like(total)
    acc[...] = jnp.zeros_like(acc)

    def body(hop):
        block = kv_ref[newest - hop]
        seen = masked_block(device_index - hop, first_ref, device_index, rows)
        for g in range(GROUPS):
            keys = block[:, g * HEAD : (g + 1) * HEAD]
            values = block[:, (GROUPS + g) * HEAD : (GROUPS + g + 1) * HEAD]
            scores = jnp.dot(keys, side_by_side(q_ref, g), preferred_element_type=jnp.float32)
            scores = jnp.where(seen, scores, -1e30)
            now = jnp.maximum(top[g], jnp.max(scores, axis=0, keepdims=True))
            probs = jnp.exp(scores - now)
            fade = jnp.exp(top[g] - now)
            top[g] = now
            total[g] = total[g] * fade + jnp.sum(probs, axis=0, keepdims=True)
            acc[g] = acc[g] * fade + lax.dot_general(
                values,
                probs.astype(jnp.bfloat16),
                (((0,), (0,)), ((), ())),
                preferred_element_type=jnp.float32,
            )

    over_shards(steps_ref, body)
    for g in range(GROUPS):
        done = acc[g] / total[g]
        for j in range(HEADS // GROUPS):
            out_ref[g, j] = done[:, j * rows : (j + 1) * rows]
        log_ref[g] = top[g] + jnp.log(total[g])


def attend(steps, queries, kv, first, half):
    rows = kv.shape[1]
    per_group = HEADS // GROUPS
    wide = per_group * rows
    return pl.pallas_call(
        partial(attend_kernel, half),
        out_shape=[
            jax.ShapeDtypeStruct((GROUPS, per_group, HEAD, rows), jnp.float32),
            jax.ShapeDtypeStruct((GROUPS, 1, wide), jnp.float32),
        ],
        in_specs=[pl.BlockSpec(memory_space=pltpu.SMEM)]
        + [pl.BlockSpec(memory_space=pltpu.VMEM)] * 3,
        out_specs=[pl.BlockSpec(memory_space=pltpu.VMEM)] * 2,
        scratch_shapes=[
            pltpu.VMEM((GROUPS, 1, wide), jnp.float32),
            pltpu.VMEM((GROUPS, 1, wide), jnp.float32),
            pltpu.VMEM((GROUPS, HEAD, wide), jnp.float32),
        ],
        compiler_params=pltpu.CompilerParams(vmem_limit_bytes=56 * MIB),
        name="attend",
    )(steps, queries, kv, first)


def attend_back_kernel(
    half,
    steps_ref,
    q_ref,
    kv_ref,
    first_ref,
    out_ref,
    log_ref,
    grad_ref,
    grad_q_ref,
    grad_kv_ref,
    dots,
    acc,
):
    device_index, newest = steps_ref[0], half + lax.rem(steps_ref[0], half)
    rows = kv_ref.shape[1]
    contract = lambda a, b, i: lax.dot_general(
        a, b, (((i,), (i,)), ((), ())), preferred_element_type=jnp.float32
    )
    for g in range(GROUPS):
        product = side_by_side(out_ref, g) * side_by_side(grad_ref, g).astype(jnp.float32)
        dots[g] = jnp.sum(product, axis=0, keepdims=True)
    acc[...] = jnp.zeros_like(acc)

    @pl.loop(0, 2 * half)
    def _(i):
        grad_kv_ref[i] = jnp.zeros(grad_kv_ref.shape[1:], grad_kv_ref.dtype)

    def body(hop):
        block = kv_ref[newest - hop]
        seen = masked_block(device_index - hop, first_ref, device_index, rows)
        grad_keys, grad_values = [], []
        for g in range(GROUPS):
            keys = block[:, g * HEAD : (g + 1) * HEAD]
            values = block[:, (GROUPS + g) * HEAD : (GROUPS + g + 1) * HEAD]
            queries, grads = side_by_side(q_ref, g), side_by_side(grad_ref, g)
            scores = jnp.dot(keys, queries, preferred_element_type=jnp.float32)
            probs = jnp.where(seen, jnp.exp(scores - log_ref[g]), 0.0)
            grad_probs = jnp.dot(values, grads, preferred_element_type=jnp.float32)
            grad_values.append(contract(probs.astype(jnp.bfloat16), grads, 1))
            grad_scores = (probs * (grad_probs - dots[g])).astype(jnp.bfloat16)
            grad_keys.append(contract(grad_scores, queries, 1))
            acc[g] += contract(keys, grad_scores, 0)
        grad_kv_ref[newest - hop] = jnp.concatenate(grad_keys + grad_values, 1).astype(
            grad_kv_ref.dtype
        )

    over_shards(steps_ref, body)
    for g in range(GROUPS):
        for j in range(HEADS // GROUPS):
            grad_q_ref[g, j] = (acc[g, :, j * rows : (j + 1) * rows] * (HEAD**-0.5)).astype(
                grad_q_ref.dtype
            )


def attend_back(steps, queries, kv, first, out, log_sum, grads, half):
    rows = kv.shape[1]
    wide = HEADS // GROUPS * rows
    return pl.pallas_call(
        partial(attend_back_kernel, half),
        out_shape=[
            jax.ShapeDtypeStruct(queries.shape, jnp.bfloat16),
            jax.ShapeDtypeStruct(kv.shape, jnp.bfloat16),
        ],
        in_specs=[pl.BlockSpec(memory_space=pltpu.SMEM)]
        + [pl.BlockSpec(memory_space=pltpu.VMEM)] * 6,
        out_specs=[pl.BlockSpec(memory_space=pltpu.VMEM)] * 2,
        scratch_shapes=[
            pltpu.VMEM((GROUPS, 1, wide), jnp.float32),
            pltpu.VMEM((GROUPS, HEAD, wide), jnp.float32),
        ],
        compiler_params=pltpu.CompilerParams(vmem_limit_bytes=60 * MIB),
        name="attend_back",
    )(steps, queries, kv, first, out, log_sum, grads)


def from_behind(x, axis, by):
    count = lax.axis_size(axis)
    pairs = [(i, i + by) for i in range(count) if 0 <= i + by < count]
    return lax.ppermute(x, axis, pairs)


def carried_in_2(x, axis, combine, identity, reverse):
    count, place = (lax.axis_size(axis), lax.axis_index(axis))
    everything = jax.tree.map(
        lambda part, kind: lax.all_gather(part.astype(kind), axis),
        x,
        jax.tree.map(lambda a: jnp.bfloat16 if a.dtype == jnp.float32 else a.dtype, x),
    )
    start = jax.tree.map(
        lambda part, zero: jnp.broadcast_to(jnp.asarray(zero, part.dtype), part.shape), x, identity
    )

    def hop(k, before):
        at = count - 1 - k if reverse else k
        reached = at > place if reverse else at < place
        new = combine(
            before, jax.tree.map(lambda part, own: part[at].astype(own.dtype), everything, x)
        )
        return jax.tree.map(lambda a, b: jnp.where(reached, a, b), new, before)

    return lax.fori_loop(0, count, hop, start)


def as_sent(x):
    return jax.tree.map(lambda a: a.astype(jnp.bfloat16) if a.dtype == jnp.float32 else a, x)


def gathered(x, groups):
    return lax.all_gather(x, "seq", axis_index_groups=groups, tiled=True)


def summed_rows(x, groups):
    return lax.psum_scatter(x, "seq", scatter_dimension=0, axis_index_groups=groups, tiled=True)


def halves_summed(first, second, side, half):
    send = jnp.where(side == 0, second, first).astype(jnp.bfloat16)
    keep = jnp.where(side == 0, first, second)
    return keep + lax.ppermute(
        send, "seq", [(d, (d + half) % (2 * half)) for d in range(2 * half)]
    ).astype(jnp.float32)


def swapped(arrays, half, groups):
    widths = [a.shape[1] // (2 * half) for a in arrays]
    rows = arrays[0].shape[0]
    packed = jnp.concatenate([a.reshape(rows, 2, half, -1) for a in arrays], 3)
    packed = jnp.transpose(packed, (2, 0, 1, 3))
    packed = lax.all_to_all(packed, "seq", 0, 0, axis_index_groups=groups, tiled=True)
    packed = packed.reshape(half * rows, 2, -1)
    out, at = [], 0
    for width in widths:
        out.append([packed[:, k, at : at + width] for k in range(2)])
        at += width
    return out


def rms_scale(entries):
    return entries * lax.rsqrt(jnp.mean(entries * entries, axis=-1, keepdims=True) + eps)


def scaled_norm(entries, gain):
    return rms_scale(entries) * gain


def branch_mix(attn_proj, ssm_proj_out, attn_beta, ssm_beta):
    return attn_beta * rms_scale(attn_proj) + ssm_beta * rms_scale(ssm_proj_out)


def silu_slope(entries):
    sigma = jax.nn.sigmoid(entries)
    return sigma * (1.0 + entries * (1.0 - sigma))


def conv_local(conv_in, tail_x, conv_weight, seg_ids, tail_seg):
    row_count = conv_in.shape[0]
    tap_count = conv_weight.shape[0]
    extended = jnp.concatenate([tail_x, conv_in], 0)
    ext_seg = jnp.concatenate([tail_seg, seg_ids], 0)
    summed = conv_weight[0] * conv_in
    for tap_lag in range(1, tap_count):
        first_row = tap_count - 1 - tap_lag
        lagged = extended[first_row : first_row + row_count]
        same_item = (ext_seg[first_row : first_row + row_count] == seg_ids)[:, None]
        summed = summed + conv_weight[tap_lag] * jnp.where(same_item, lagged, 0.0)
    return jax.nn.silu(summed)


def ssm_parts(conv_in, select, tail_x, conv_weight, step_bias, decay_log, seg_ids, tail_seg):
    row_count = conv_in.shape[0]
    conv_out = conv_local(conv_in, tail_x, conv_weight, seg_ids, tail_seg)
    heads_x = conv_out.reshape(row_count, -1, SHEAD)
    b_proj = select[:, :STATE]
    c_proj = select[:, STATE : 2 * STATE]
    step_size = jax.nn.softplus(select[:, 2 * STATE :] + step_bias)
    log_decay = -step_size * jnp.exp(decay_log)
    lower_tri = (jnp.arange(row_count)[:, None] >= jnp.arange(row_count)[None, :]).astype(
        jnp.float32
    )
    cum_decay = jnp.dot(lower_tri, log_decay, precision=highest)
    scaled_x = heads_x * step_size[:, :, None]
    return (heads_x, b_proj, c_proj, cum_decay, scaled_x, lower_tri)


def ssm_output(
    conv_in,
    select,
    tail_x,
    conv_weight,
    step_bias,
    decay_log,
    skip_gain,
    held_in,
    seg_ids,
    tail_seg,
):
    heads_x, b_proj, c_proj, cum_decay, scaled_x, lower_tri = ssm_parts(
        conv_in, select, tail_x, conv_weight, step_bias, decay_log, seg_ids, tail_seg
    )
    seg_prev = tail_seg[-1]
    same_item = (seg_ids[:, None] == seg_ids[None, :]) & (lower_tri > 0)
    exponent = jnp.where(same_item[None], cum_decay.T[:, :, None] - cum_decay.T[:, None, :], -1e30)
    weights = jnp.exp(exponent) * jnp.dot(c_proj, b_proj.T, precision=highest)[None]
    local_part = jnp.einsum("htr,rhp->thp", weights, scaled_x, precision=highest)
    follow = (seg_ids == seg_prev).astype(jnp.float32)
    carry_weight = jnp.exp(cum_decay) * follow[:, None]
    carried = jnp.einsum("th,hpn,tn->thp", carry_weight, held_in, c_proj, precision=highest)
    outputs = local_part + carried + skip_gain[None, :, None] * heads_x
    return outputs.reshape(conv_in.shape[0], -1)


def ssm_state(conv_in, select, tail_x, conv_weight, step_bias, decay_log, seg_ids, tail_seg):
    heads_x, b_proj, c_proj, cum_decay, scaled_x, lower_tri = ssm_parts(
        conv_in, select, tail_x, conv_weight, step_bias, decay_log, seg_ids, tail_seg
    )
    seg_prev = tail_seg[-1]
    last_same = (seg_ids == seg_ids[-1]).astype(jnp.float32)
    last_weight = jnp.exp(cum_decay[-1][None, :] - cum_decay) * last_same[:, None]
    fresh_state = jnp.einsum("rh,rhp,rn->hpn", last_weight, scaled_x, b_proj, precision=highest)
    through = (seg_ids[-1] == seg_prev).astype(jnp.float32)
    return (fresh_state, jnp.exp(cum_decay[-1]) * through)


def chain_forward(earlier, later):
    return (earlier[0] * later[0], later[0][:, None, None] * earlier[1] + later[1])


def chain_backward(earlier, later):
    return (later[0] * earlier[0], later[1] + later[0][:, None, None] * earlier[1])


def per_device(
    tokens,
    seg_ids,
    meta_index,
    meta_table,
    mixer_gain,
    attn_weight,
    ssm_weight,
    select_weight,
    conv_weight,
    step_bias,
    decay_log,
    skip_gain,
    ssm_down,
    attn_beta,
    ssm_beta,
    ffn_gain,
    gate_up,
    ffn_down,
    cotangent,
):
    row_count = tokens.shape[0]
    model_width = tokens.shape[1]
    kv_width = GROUPS * HEAD
    per_group = HEADS // GROUPS
    qkv_cols = model_width + 2 * kv_width
    score_scale = 1.0 / math.sqrt(HEAD)
    devices = lax.axis_size("seq")
    device_index = lax.axis_index("seq")
    half = devices // 2
    side, place = device_index // half, device_index % half
    groups = [[h * half + q for q in range(half)] for h in range(2)]
    one_hot = (meta_index[:, None] == jnp.arange(META, dtype=jnp.int32)[None, :]).astype(
        jnp.float32
    )
    is_meta = (meta_index < META)[:, None]
    layer_in = jnp.where(
        is_meta,
        jnp.dot(one_hot.astype(jnp.bfloat16), meta_table, preferred_element_type=jnp.float32),
        tokens.astype(jnp.float32),
    )
    normed = scaled_norm(layer_in, mixer_gain).astype(jnp.bfloat16)
    query_weight = attn_weight[:, :model_width]
    kv_weight = attn_weight[:, model_width:qkv_cols]
    flip = [(d, (d + half) % devices) for d in range(devices)]
    kv = jnp.dot(normed, kv_weight, preferred_element_type=jnp.float32).astype(jnp.bfloat16)
    kv_all = gather_half([lax.ppermute(kv, "seq", flip), kv], half, 0)
    queries = lax.dot_general(
        query_weight, normed, (((0,), (1,)), ((), ())), preferred_element_type=jnp.float32
    )
    queries = (queries.astype(jnp.bfloat16) * score_scale).reshape(
        GROUPS, per_group, HEAD, row_count
    )
    seg_all = lax.all_gather(seg_ids, "seq", tiled=True)
    first = jnp.sum((seg_all[:, None] < seg_ids[None, :]).astype(jnp.int32), axis=0)
    steps = jnp.stack([device_index, device_index - first[0] // row_count])
    attn_full, log_sum = attend(steps, queries, kv_all, first[None, :], half)
    attended = attn_full.reshape(model_width, row_count).astype(jnp.bfloat16).T
    out_weight = attn_weight[:, qkv_cols:]
    attn_proj = jnp.dot(attended, out_weight.T, preferred_element_type=jnp.float32)
    ssm_proj = jnp.dot(normed, ssm_weight, preferred_element_type=jnp.float32)
    conv_in = ssm_proj[:, :INNER]
    z_gate = ssm_proj[:, INNER:]
    select = jnp.dot(normed, select_weight, preferred_element_type=jnp.float32)
    tail_x, tail_seg = (
        from_behind(conv_in[row_count - CONV + 1 :].astype(jnp.bfloat16), "seq", 1).astype(
            jnp.float32
        ),
        from_behind(seg_ids[row_count - CONV + 1 :], "seq", 1),
    )
    (fresh_state, decay_all), state_pull = jax.vjp(
        partial(ssm_state, seg_ids=seg_ids, tail_seg=tail_seg),
        conv_in,
        select,
        tail_x,
        conv_weight,
        step_bias,
        decay_log,
    )
    carry_identity = (jnp.ones_like(decay_all), jnp.zeros_like(fresh_state))
    held_in = carried_in_2((decay_all, fresh_state), "seq", chain_forward, carry_identity, False)[1]
    scanned, output_pull = jax.vjp(
        partial(ssm_output, seg_ids=seg_ids, tail_seg=tail_seg),
        conv_in,
        select,
        tail_x,
        conv_weight,
        step_bias,
        decay_log,
        skip_gain,
        held_in,
    )
    gated = (scanned * jax.nn.silu(z_gate)).astype(jnp.bfloat16)
    ssm_proj_out = jnp.dot(gated, ssm_down, preferred_element_type=jnp.float32)
    mixed_terms, mix_pull = jax.vjp(branch_mix, attn_proj, ssm_proj_out, attn_beta, ssm_beta)
    hidden1 = layer_in + mixed_terms
    ffn_in_f, ffn_norm_pull = jax.vjp(scaled_norm, hidden1, ffn_gain)
    ffn_in = ffn_in_f.astype(jnp.bfloat16)
    ffn_rows = gather_half([ffn_in], half, 2).reshape(half * row_count, model_width)
    cot_rows = gathered(cotangent, groups)
    units = FF // half
    gate_w = lax.dynamic_slice_in_dim(gate_up, place * units, units, 1)
    up_w = lax.dynamic_slice_in_dim(gate_up, FF + place * units, units, 1)
    down_w = lax.dynamic_slice_in_dim(ffn_down, place * units, units, 0)
    gate_part = jnp.dot(ffn_rows, gate_w, preferred_element_type=jnp.float32)
    up_part = jnp.dot(ffn_rows, up_w, preferred_element_type=jnp.float32)
    hidden = (jax.nn.silu(gate_part) * up_part).astype(jnp.bfloat16)
    out_terms = jnp.dot(hidden, down_w, preferred_element_type=jnp.float32).astype(jnp.bfloat16)
    layer_out = (hidden1 + summed_rows(out_terms, groups).astype(jnp.float32)).astype(jnp.bfloat16)
    grad_hidden = (
        jnp.dot(cot_rows, down_w.T, preferred_element_type=jnp.float32)
        .astype(jnp.bfloat16)
        .astype(jnp.float32)
    )
    down_terms = jnp.dot(hidden.T, cot_rows, preferred_element_type=jnp.float32)
    grad_gate = (grad_hidden * up_part * silu_slope(gate_part)).astype(jnp.bfloat16)
    grad_up = (grad_hidden * jax.nn.silu(gate_part)).astype(jnp.bfloat16)
    gate_terms = jnp.dot(ffn_rows.T, grad_gate, preferred_element_type=jnp.float32)
    up_terms = jnp.dot(ffn_rows.T, grad_up, preferred_element_type=jnp.float32)
    grad_gate_up = halves_summed(gate_terms, up_terms, side, half)
    own_down = halves_summed(down_terms[: units // 2], down_terms[units // 2 :], side, half)
    grad_ffn_down = lax.ppermute(
        own_down.astype(jnp.bfloat16),
        "seq",
        [(h * half + q, 2 * q + h) for h in range(2) for q in range(half)],
    ).astype(jnp.float32)
    in_terms = jnp.dot(grad_gate, gate_w.T, preferred_element_type=jnp.float32) + jnp.dot(
        grad_up, up_w.T, preferred_element_type=jnp.float32
    )
    in_terms = in_terms.astype(jnp.bfloat16).reshape(half, row_count, model_width)
    grad_ffn_in = sum_half(in_terms, 1, half, 3)[0].astype(jnp.float32)
    grad_from_ffn, grad_ffn_gain = ffn_norm_pull(grad_ffn_in)
    grad_hidden1 = cotangent.astype(jnp.float32) + grad_from_ffn
    grad_attn_proj, grad_ssm_proj_out, grad_attn_beta, grad_ssm_beta = mix_pull(grad_hidden1)
    attn_grad_low = grad_attn_proj.astype(jnp.bfloat16)
    ssm_grad_low = grad_ssm_proj_out.astype(jnp.bfloat16)
    out_grad = (
        lax.dot_general(
            out_weight, attn_grad_low, (((0,), (1,)), ((), ())), preferred_element_type=jnp.float32
        )
        .astype(jnp.bfloat16)
        .reshape(GROUPS, per_group, HEAD, row_count)
    )
    grad_queries, kv_terms = attend_back(
        steps, queries, kv_all, first[None, :], attn_full, log_sum, out_grad, half
    )
    grad_kv_other, grad_kv = sum_half(kv_terms, 2, half, 1)
    grad_kv = grad_kv.astype(jnp.float32) + lax.ppermute(grad_kv_other, "seq", flip).astype(
        jnp.float32
    )
    grad_gated = (
        jnp.dot(ssm_grad_low, ssm_down.T, preferred_element_type=jnp.float32)
        .astype(jnp.bfloat16)
        .astype(jnp.float32)
    )
    grad_scanned = grad_gated * jax.nn.silu(z_gate)
    grad_z_gate = grad_gated * scanned * silu_slope(z_gate)
    output_grads = output_pull(grad_scanned)
    later_grad = carried_in_2(
        (decay_all, output_grads[7]), "seq", chain_backward, carry_identity, True
    )[1]
    grad_decay_all = jnp.sum(later_grad * held_in, axis=(1, 2))
    state_grads = state_pull((later_grad, grad_decay_all))
    grad_tail = output_grads[2] + state_grads[2]
    tail_back = from_behind(as_sent(grad_tail), "seq", -1).astype(grad_tail.dtype)
    grad_conv_in = output_grads[0] + state_grads[0]
    grad_conv_in = jnp.concatenate(
        [grad_conv_in[: row_count - CONV + 1], grad_conv_in[row_count - CONV + 1 :] + tail_back], 0
    )
    grad_select_in = (output_grads[1] + state_grads[1]).astype(jnp.bfloat16)
    grad_conv = output_grads[3] + state_grads[3]
    grad_step_bias = output_grads[4] + state_grads[4]
    grad_decay = output_grads[5] + state_grads[5]
    grad_skip = output_grads[6]
    proj_grad = jnp.concatenate([grad_conv_in, grad_z_gate], 1).astype(jnp.bfloat16)
    qkv_grad = jnp.concatenate(
        [grad_queries.reshape(model_width, row_count).T, grad_kv.astype(jnp.bfloat16)], 1
    )
    grad_normed = jnp.dot(qkv_grad, attn_weight[:, :qkv_cols].T, preferred_element_type=jnp.float32)
    grad_normed = grad_normed + jnp.dot(proj_grad, ssm_weight.T, preferred_element_type=jnp.float32)
    grad_normed = grad_normed + jnp.dot(
        grad_select_in, select_weight.T, preferred_element_type=jnp.float32
    )
    columns = swapped(
        [jnp.concatenate([qkv_grad, attended], 1), proj_grad, gated], half, groups
    )
    normed_rows = gathered(normed, groups)
    attn_grad_rows = gathered(attn_grad_low, groups)
    ssm_grad_rows = gathered(ssm_grad_low, groups)
    grad_attn, grad_ssm = [], []
    for k in range(2):
        block = columns[0][k]
        width = block.shape[1]
        column = (k * half + place) * width + jnp.arange(width, dtype=jnp.int32)
        grad_attn.append(
            jnp.where(
                (column < qkv_cols)[None, :],
                jnp.dot(normed_rows.T, block, preferred_element_type=jnp.float32),
                jnp.dot(attn_grad_rows.T, block, preferred_element_type=jnp.float32),
            )
        )
        grad_ssm.append(jnp.dot(normed_rows.T, columns[1][k], preferred_element_type=jnp.float32))
    grad_attn = halves_summed(grad_attn[0], grad_attn[1], side, half)
    grad_ssm = halves_summed(grad_ssm[0], grad_ssm[1], side, half)
    grad_ssm_down = halves_summed(
        jnp.dot(columns[2][0].T, ssm_grad_rows, preferred_element_type=jnp.float32),
        jnp.dot(columns[2][1].T, ssm_grad_rows, preferred_element_type=jnp.float32),
        side,
        half,
    )
    grad_select = jnp.dot(normed.T, grad_select_in, preferred_element_type=jnp.float32)
    mixer_norm_pull = jax.vjp(scaled_norm, layer_in, mixer_gain)[1]
    grad_from_mixer, grad_mixer_gain = mixer_norm_pull(grad_normed)
    grad_layer_in = grad_hidden1 + grad_from_mixer
    grad_tokens = jnp.where(is_meta, 0.0, grad_layer_in).astype(jnp.bfloat16)
    grad_meta = jnp.dot(one_hot.T, jnp.where(is_meta, grad_layer_in, 0.0), precision=highest)
    small = lax.psum(
        (
            grad_meta,
            grad_mixer_gain,
            grad_select,
            grad_conv,
            grad_step_bias,
            grad_decay,
            grad_skip,
            grad_attn_beta,
            grad_ssm_beta,
            grad_ffn_gain,
        ),
        "seq",
    )
    shares = (grad_attn, grad_ssm, grad_ssm_down, grad_gate_up, grad_ffn_down)
    return (
        layer_out,
        grad_tokens,
        small[0],
        small[1],
        shares[0],
        shares[1],
        small[2],
        small[3],
        small[4],
        small[5],
        small[6],
        shares[2],
        small[7],
        small[8],
        small[9],
        shares[3],
        shares[4],
    )


def solution(mesh):
    placed = (
        P("seq", None),
        P("seq"),
        P("seq"),
        P(),
        P(),
        P(),
        P(),
        P(),
        P(),
        P(),
        P(),
        P(),
        P(),
        P(),
        P(),
        P(),
        P(),
        P(),
        P("seq", None),
    )
    return jax.shard_map(
        per_device,
        mesh=mesh,
        in_specs=placed,
        out_specs=(
            P("seq", None),
            P("seq", None),
            P(),
            P(),
            P(None, "seq"),
            P(None, "seq"),
            P(),
            P(),
            P(),
            P(),
            P(),
            P("seq", None),
            P(),
            P(),
            P(),
            P(None, "seq"),
            P("seq", None),
        ),
        check_vma=False,
    )
```

```python
from functools import partial
import math

import jax
import jax.numpy as jnp
from jax import lax
from jax.experimental import pallas as pl
from jax.experimental.pallas import tpu as pltpu
from jax.sharding import PartitionSpec as P

HEADS = 25
GROUPS = 5
HEAD = 64
INNER = 3200
STATE = 16
CONV = 4
FF = 5504
META = 128
SHEAD = 64


eps = 1e-05
highest = lax.Precision.HIGHEST


MESH = pl.DeviceIdType.MESH
MIB = 2**20


def cost(microseconds):
    return pl.CostEstimate(
        flops=0, transcendentals=0, bytes_accessed=int(microseconds * 3_000_000)
    )


def flipped(v, k):
    bit = 1 << k
    return jnp.where(lax.rem(v // bit, 2) == 0, v + bit, v - bit)


def flips_of(v, bits):
    out = [v]
    for k in bits:
        out = out + [flipped(o, k) for o in out]
    return out


def thirds(rows):
    most = (rows // 3 + 15) // 16 * 16
    return [(0, most), (most, most), (2 * most, rows - 2 * most)]


def parts_of(rows):
    return [part for part in thirds(rows) if part[1] > 0] if rows >= 48 else [(0, rows)]


def greet(partners):
    barrier = pltpu.get_barrier_semaphore()
    for partner in partners:
        pl.semaphore_signal(barrier, inc=1, device_id=(partner,), device_id_type=MESH)
    pl.semaphore_wait(barrier, len(partners))


def remote(src, dst, send, recv, device):
    return pltpu.make_async_remote_copy(
        src_ref=src,
        dst_ref=dst,
        send_sem=send,
        recv_sem=recv,
        device_id=(device,),
        device_id_type=MESH,
    )


def gather_kernel(arrays, half, *refs):
    ins, out = refs[:arrays], refs[arrays]
    send, recv, core_send, core_recv, local_sem = refs[arrays + 1 :]
    me = lax.axis_index("seq")
    place = lax.rem(me, half)
    bits = half.bit_length() - 1
    greet([flipped(me, k) for k in range(bits)])
    parts = thirds(ins[0].shape[0])
    links = bits - 1
    orders = [[1 + (c + s) % links for s in range(links)] for c in range(3)]
    local = [
        pltpu.make_async_copy(ins[a], out.at[a * half + place], local_sem.at[a])
        for a in range(arrays)
    ]
    for copy in local:
        copy.start()
    sent, handed = [], []
    for step in range(links + 1):
        arriving = []
        for c, (first, count) in enumerate(parts):
            rows = pl.ds(first, count)
            held = flips_of(place, orders[c][:step])
            for a in range(arrays):
                if step < links:
                    for i, b in enumerate(held):
                        place_at = out.at[a * half + b, rows]
                        at = (1 << step) - 1 + i
                        copy = remote(
                            ins[a].at[rows] if i == 0 else place_at,
                            place_at,
                            send.at[a, c, at],
                            recv.at[a, c, at],
                            flipped(me, orders[c][step]),
                        )
                        copy.start()
                        arriving.append(copy)
                new = held if step == 0 else held[len(held) // 2 :]
                for i, b in enumerate(new):
                    place_at = out.at[a * half + b, rows]
                    at = 0 if step == 0 else (1 << (step - 1)) + i
                    copy = remote(
                        ins[a].at[rows] if step == 0 else place_at,
                        place_at,
                        core_send.at[a, c, at],
                        core_recv.at[a, c, at],
                        flipped(me, 0),
                    )
                    copy.start()
                    handed.append(copy)
        for copy in arriving:
            copy.wait_recv()
        sent += arriving
    for copy in sent:
        copy.wait_send()
    for copy in handed:
        copy.wait()
    for copy in local:
        copy.wait()


def gather_half(arrays, half, collective_id):
    count = len(arrays)
    shape = arrays[0].shape
    semaphores = pltpu.SemaphoreType.DMA((count, 3, half // 2))
    return pl.pallas_call(
        partial(gather_kernel, count, half),
        out_shape=jax.ShapeDtypeStruct((count * half,) + shape, arrays[0].dtype),
        in_specs=[pl.BlockSpec(memory_space=pl.ANY)] * count,
        out_specs=pl.BlockSpec(memory_space=pl.ANY),
        scratch_shapes=[semaphores] * 4 + [pltpu.SemaphoreType.DMA((count,))],
        compiler_params=pltpu.CompilerParams(collective_id=collective_id, has_side_effects=True),
        cost_estimate=cost(40),
        name="gather_half",
    )(*arrays)


def gather_both_kernel(arrays, half, *refs):
    ins, outs = refs[:arrays], refs[arrays : 2 * arrays]
    send, recv, core_send, core_recv, flip_send, flip_recv, local_sem = refs[2 * arrays :]
    me = lax.axis_index("seq")
    place = lax.rem(me, half)
    twin = jnp.where(me < half, me + half, me - half)
    bits = half.bit_length() - 1
    greet([flipped(me, k) for k in range(bits)] + [twin])
    links = bits - 1
    orders = [[1 + (c + s) % links for s in range(links)] for c in range(3)]
    parts = [parts_of(ref.shape[0]) for ref in ins]
    local, sent, handed, twins = [], [], [], []
    for a in range(arrays):
        copy = remote(ins[a], outs[a].at[place], flip_send.at[a], flip_recv.at[a], twin)
        copy.start()
        twins.append(copy)
        copy = pltpu.make_async_copy(ins[a], outs[a].at[half + place], local_sem.at[a])
        copy.start()
        local.append(copy)
    for time in range(links + 2):
        arriving = []
        for own in (1, 0):
            step = time - (1 - own)
            if step < 0 or step > links:
                continue
            for a in range(arrays):
                for c, (first, count) in enumerate(parts[a]):
                    rows = pl.ds(first, count)
                    slot = own * arrays + a
                    held = flips_of(place, orders[c][:step])
                    if step < links:
                        for i, b in enumerate(held):
                            place_at = outs[a].at[own * half + b, rows]
                            at = (1 << step) - 1 + i
                            copy = remote(
                                ins[a].at[rows] if i == 0 and own else place_at,
                                place_at,
                                send.at[slot, c, at],
                                recv.at[slot, c, at],
                                flipped(me, orders[c][step]),
                            )
                            copy.start()
                            arriving.append(copy)
                    new = held if step == 0 else held[len(held) // 2 :]
                    for i, b in enumerate(new):
                        place_at = outs[a].at[own * half + b, rows]
                        at = 0 if step == 0 else (1 << (step - 1)) + i
                        copy = remote(
                            ins[a].at[rows] if step == 0 and own else place_at,
                            place_at,
                            core_send.at[slot, c, at],
                            core_recv.at[slot, c, at],
                            flipped(me, 0),
                        )
                        copy.start()
                        handed.append(copy)
        if time == 0:
            for copy in twins:
                copy.wait_recv()
        for copy in arriving:
            copy.wait_recv()
        sent += arriving
    for copy in sent + twins:
        copy.wait_send()
    for copy in handed:
        copy.wait()
    for copy in local:
        copy.wait()


def gather_both(arrays, half, collective_id):
    count = len(arrays)
    semaphores = pltpu.SemaphoreType.DMA((2 * count, 3, half // 2))
    single = pltpu.SemaphoreType.DMA((count,))
    return pl.pallas_call(
        partial(gather_both_kernel, count, half),
        out_shape=[jax.ShapeDtypeStruct((2 * half,) + a.shape, a.dtype) for a in arrays],
        in_specs=[pl.BlockSpec(memory_space=pl.ANY)] * count,
        out_specs=[pl.BlockSpec(memory_space=pl.ANY)] * count,
        scratch_shapes=[semaphores] * 4 + [single] * 3,
        compiler_params=pltpu.CompilerParams(collective_id=collective_id, has_side_effects=True),
        cost_estimate=cost(50),
        name="gather_both",
    )(*arrays)


def total_kernel(devices, terms, out, mine, core_in, link_in, send, recv, send_back, recv_back):
    me = lax.axis_index("seq")
    bits = devices.bit_length() - 1
    greet([flipped(me, k) for k in range(bits)])
    pairs = devices // 2
    columns = terms.shape[2]
    third = columns // 3 // 128 * 128
    parts = [(0, third), (third, third), (2 * third, columns - 2 * third)]
    turned = min(3, bits - 1)
    orders = [
        [1 + (c + s) % turned for s in range(turned)] + list(range(1 + turned, bits))
        for c in range(3)
    ]
    everything = pl.ds(0, columns)
    copies = []
    first = []
    for i in range(pairs):
        block = 2 * i + 1 - lax.rem(me, 2)
        copy = remote(
            terms.at[block], core_in.at[i], send.at[0, i], recv.at[0, i], flipped(me, 0)
        )
        copy.start()
        first.append(copy)
    copies += first
    for i in range(pairs):
        first[i].wait_recv()
        mine[i] = terms[2 * i + lax.rem(me, 2)] + core_in[i]
    for step in range(bits - 1):
        arriving = []
        for c, (start, count) in enumerate(parts):
            lanes = pl.ds(start, count)
            for i, b in enumerate(flips_of(me, orders[c][step + 1 :])):
                away = flipped(b, orders[c][step])
                at = pairs - (pairs >> step) + i
                copy = remote(
                    mine.at[away // 2, :, lanes],
                    link_in.at[at, :, lanes],
                    send.at[1 + c, at],
                    recv.at[1 + c, at],
                    flipped(me, orders[c][step]),
                )
                copy.start()
                arriving.append((copy, b, at, lanes))
        for copy, b, at, lanes in arriving:
            copy.wait_recv()
            mine[b // 2, :, lanes] = mine[b // 2, :, lanes] + link_in[at, :, lanes]
            copies.append(copy)
    out[me] = mine[me // 2]
    for step in range(bits - 1):
        arriving = []
        for c, (start, count) in enumerate(parts):
            lanes = pl.ds(start, count)
            order = orders[c][::-1]
            for i, b in enumerate(flips_of(me, order[:step])):
                at = (1 << step) - 1 + i
                copy = remote(
                    out.at[b, :, lanes],
                    out.at[b, :, lanes],
                    send_back.at[1 + c, at],
                    recv_back.at[1 + c, at],
                    flipped(me, order[step]),
                )
                copy.start()
                arriving.append(copy)
        for copy in arriving:
            copy.wait_recv()
        copies += arriving
    last = []
    for i, b in enumerate(flips_of(me, range(1, bits))):
        copy = remote(
            out.at[b], out.at[b], send_back.at[0, i], recv_back.at[0, i], flipped(me, 0)
        )
        copy.start()
        last.append(copy)
    for copy in last:
        copy.wait()
    for copy in copies:
        copy.wait_send()


def total_of(terms, devices, collective_id):
    pairs = devices // 2
    half_shape = (pairs,) + terms.shape[1:]
    semaphores = pltpu.SemaphoreType.DMA((4, pairs))
    return pl.pallas_call(
        partial(total_kernel, devices),
        out_shape=jax.ShapeDtypeStruct(terms.shape, terms.dtype),
        in_specs=[pl.BlockSpec(memory_space=pltpu.VMEM)],
        out_specs=pl.BlockSpec(memory_space=pltpu.VMEM),
        scratch_shapes=[pltpu.VMEM(half_shape, terms.dtype)] * 3 + [semaphores] * 4,
        compiler_params=pltpu.CompilerParams(
            collective_id=collective_id, has_side_effects=True, vmem_limit_bytes=48 * MIB
        ),
        cost_estimate=cost(40),
        name="total_of",
    )(terms)


def sum_kernel(arrays, half, *refs):
    terms, outs = refs[0], refs[1 : 1 + arrays]
    mine, core_in, link_in, load_sem, send, recv, core_send, core_recv = refs[1 + arrays :]
    me = lax.axis_index("seq")
    place = lax.rem(me, half)
    bits = half.bit_length() - 1
    greet([flipped(me, k) for k in range(bits)])
    parts = thirds(terms.shape[1])
    links = bits - 1
    orders = [[1 + (c + s) % links for s in range(links)] for c in range(3)]
    loads = []
    pairs = half // 2
    for a in range(arrays):
        for i in range(pairs):
            block = 2 * i + lax.rem(place, 2)
            copy = pltpu.make_async_copy(
                terms.at[a * half + block], mine.at[a, i], load_sem.at[a, i]
            )
            copy.start()
            loads.append(copy)
    handed = {}
    for wanted in range(2):
        for c, (first, count) in enumerate(parts):
            rows = pl.ds(first, count)
            kept = flips_of(place, orders[c][1:])
            blocks = kept if wanted else [flipped(b, orders[c][0]) for b in kept]
            for a in range(arrays):
                for i, b in enumerate(blocks):
                    at = wanted * (pairs // 2) + i
                    copy = remote(
                        terms.at[a * half + flipped(b, 0), rows],
                        core_in.at[a, at, rows],
                        core_send.at[a, c, at],
                        core_recv.at[a, c, at],
                        flipped(me, 0),
                    )
                    copy.start()
                    handed[a, c, at] = copy
    for copy in loads:
        copy.wait()
    sent = []
    arriving = {}

    def add(ref, slot, rows, other):
        ref[slot, rows] = (
            ref[slot, rows].astype(jnp.float32) + other[...].astype(jnp.float32)
        ).astype(ref.dtype)

    for step in range(links):
        for c, (first, count) in enumerate(parts):
            rows = pl.ds(first, count)
            kept = flips_of(place, orders[c][step + 1 :])
            for a in range(arrays):
                for i, b in enumerate(kept):
                    out_block = flipped(b, orders[c][step])
                    if step == 0:
                        handed[a, c, i].wait_recv()
                        add(mine.at[a], out_block // 2, rows, core_in.at[a, i, rows])
                    at = pairs - (pairs >> step) + i
                    copy = remote(
                        mine.at[a, out_block // 2, rows],
                        link_in.at[a, at, rows],
                        send.at[a, c, at],
                        recv.at[a, c, at],
                        flipped(me, orders[c][step]),
                    )
                    copy.start()
                    arriving[a, c, at] = copy
                    sent.append(copy)
        if step == 0:
            for c, (first, count) in enumerate(parts):
                rows = pl.ds(first, count)
                for a in range(arrays):
                    for i, b in enumerate(flips_of(place, orders[c][1:])):
                        at = pairs // 2 + i
                        handed[a, c, at].wait_recv()
                        add(mine.at[a], b // 2, rows, core_in.at[a, at, rows])
        for c, (first, count) in enumerate(parts):
            rows = pl.ds(first, count)
            kept = flips_of(place, orders[c][step + 1 :])
            for a in range(arrays):
                for i, b in enumerate(kept):
                    at = pairs - (pairs >> step) + i
                    arriving[a, c, at].wait_recv()
                    add(mine.at[a], b // 2, rows, link_in.at[a, at, rows])
    for a in range(arrays):
        outs[a][...] = mine[a, place // 2]
    for copy in sent:
        copy.wait_send()
    for copy in handed.values():
        copy.wait_send()


def sum_half(terms, arrays, half, collective_id):
    rows, columns = terms.shape[1:]
    pairs = half // 2
    block = (rows, columns)
    semaphores = pltpu.SemaphoreType.DMA((arrays, 3, pairs))
    return pl.pallas_call(
        partial(sum_kernel, arrays, half),
        out_shape=[jax.ShapeDtypeStruct(block, terms.dtype)] * arrays,
        in_specs=[pl.BlockSpec(memory_space=pl.ANY)],
        out_specs=[pl.BlockSpec(memory_space=pltpu.VMEM)] * arrays,
        scratch_shapes=[
            pltpu.VMEM((arrays, pairs) + block, terms.dtype),
            pltpu.VMEM((arrays, pairs) + block, terms.dtype),
            pltpu.VMEM((arrays, pairs) + block, terms.dtype),
            pltpu.SemaphoreType.DMA((arrays, pairs)),
        ]
        + [semaphores] * 4,
        compiler_params=pltpu.CompilerParams(
            collective_id=collective_id, has_side_effects=True, vmem_limit_bytes=60 * MIB
        ),
        cost_estimate=cost(50),
        name="sum_half",
    )(terms)


def ffn_kernel(x_ref, cot_ref, in_ref, down_ref, out_ref, grad_in_ref, grad_w_ref, grad_d_ref):
    wide = down_ref.shape[0]
    x, cot = x_ref[...], cot_ref[...]
    low = jnp.bfloat16

    def dot(a, b, contract):
        return lax.dot_general(a, b, (contract, ((), ())), preferred_element_type=jnp.float32)

    vals = dot(x, in_ref[...], ((1,), (0,)))
    gate, up = vals[:, :wide], vals[:, wide:]
    sigma = jax.nn.sigmoid(gate)
    act = gate * sigma
    hidden = (act * up).astype(low)
    out_ref[...] = dot(hidden, down_ref[...], ((1,), (0,))).astype(low)
    grad_hidden = dot(cot, down_ref[...], ((1,), (1,))).astype(low).astype(jnp.float32)
    slope = sigma * (1.0 + gate * (1.0 - sigma))
    grads = jnp.concatenate([grad_hidden * up * slope, grad_hidden * act], 1).astype(low)
    grad_in_ref[...] = dot(grads, in_ref[...], ((1,), (1,))).astype(low)

    @pl.when(pl.program_id(0) == 0)
    def _():
        grad_w_ref[...] = jnp.zeros_like(grad_w_ref)
        grad_d_ref[...] = jnp.zeros_like(grad_d_ref)

    grad_w_ref[...] += dot(grads, x, ((0,), (0,)))
    grad_d_ref[...] += dot(hidden, cot, ((0,), (0,)))


def ffn(x, cot, in_weight, down_weight):
    rows, model = x.shape
    block = min(256, rows)
    wide = down_weight.shape[0]
    moving = pl.BlockSpec((block, model), lambda i: (i, 0))
    fixed = lambda shape: pl.BlockSpec(shape, lambda i: (0, 0))
    return pl.pallas_call(
        ffn_kernel,
        grid=(rows // block,),
        out_shape=[
            jax.ShapeDtypeStruct(x.shape, jnp.bfloat16),
            jax.ShapeDtypeStruct(x.shape, jnp.bfloat16),
            jax.ShapeDtypeStruct((2 * wide, model), jnp.float32),
            jax.ShapeDtypeStruct((wide, model), jnp.float32),
        ],
        in_specs=[moving, moving, fixed(in_weight.shape), fixed(down_weight.shape)],
        out_specs=[moving, moving, fixed((2 * wide, model)), fixed((wide, model))],
        compiler_params=pltpu.CompilerParams(vmem_limit_bytes=56 * MIB),
        cost_estimate=cost(35),
        name="ffn",
    )(x, cot, in_weight, down_weight)


def masked_block(at, first_ref, device_index, rows):
    key = lax.broadcasted_iota(jnp.int32, (rows, rows), 0) + at * rows
    query = lax.broadcasted_iota(jnp.int32, (rows, rows), 1) + device_index * rows
    seen = ((key >= first_ref[...]) & (key <= query)).astype(jnp.float32)
    return jnp.concatenate([seen] * (HEADS // GROUPS), 1) > 0.0


def side_by_side(ref, g):
    return jnp.concatenate([ref[g, j] for j in range(HEADS // GROUPS)], 1)


def over_shards(steps_ref, body):
    body(0)

    @pl.loop(1, steps_ref[1] + 1)
    def _(hop):
        body(hop)


def attend_kernel(half, steps_ref, q_ref, kv_ref, first_ref, out_ref, log_ref, top, total, acc):
    device_index, newest = steps_ref[0], half + lax.rem(steps_ref[0], half)
    rows = kv_ref.shape[1]
    top[...] = jnp.full_like(top, -1e30)
    total[...] = jnp.zeros_like(total)
    acc[...] = jnp.zeros_like(acc)

    def body(hop):
        block = kv_ref[newest - hop]
        seen = masked_block(device_index - hop, first_ref, device_index, rows)
        for g in range(GROUPS):
            keys = block[:, g * HEAD : (g + 1) * HEAD]
            values = block[:, (GROUPS + g) * HEAD : (GROUPS + g + 1) * HEAD]
            scores = jnp.dot(keys, side_by_side(q_ref, g), preferred_element_type=jnp.float32)
            scores = jnp.where(seen, scores, -1e30)
            now = jnp.maximum(top[g], jnp.max(scores, axis=0, keepdims=True))
            probs = jnp.exp(scores - now)
            fade = jnp.exp(top[g] - now)
            top[g] = now
            total[g] = total[g] * fade + jnp.sum(probs, axis=0, keepdims=True)
            acc[g] = acc[g] * fade + lax.dot_general(
                values,
                probs.astype(jnp.bfloat16),
                (((0,), (0,)), ((), ())),
                preferred_element_type=jnp.float32,
            )

    over_shards(steps_ref, body)
    for g in range(GROUPS):
        done = acc[g] / total[g]
        for j in range(HEADS // GROUPS):
            out_ref[g, j] = done[:, j * rows : (j + 1) * rows]
        log_ref[g] = top[g] + jnp.log(total[g])


def attend(steps, queries, kv, first, half):
    rows = kv.shape[1]
    per_group = HEADS // GROUPS
    wide = per_group * rows
    return pl.pallas_call(
        partial(attend_kernel, half),
        out_shape=[
            jax.ShapeDtypeStruct((GROUPS, per_group, HEAD, rows), jnp.float32),
            jax.ShapeDtypeStruct((GROUPS, 1, wide), jnp.float32),
        ],
        in_specs=[pl.BlockSpec(memory_space=pltpu.SMEM)]
        + [pl.BlockSpec(memory_space=pltpu.VMEM)] * 3,
        out_specs=[pl.BlockSpec(memory_space=pltpu.VMEM)] * 2,
        scratch_shapes=[
            pltpu.VMEM((GROUPS, 1, wide), jnp.float32),
            pltpu.VMEM((GROUPS, 1, wide), jnp.float32),
            pltpu.VMEM((GROUPS, HEAD, wide), jnp.float32),
        ],
        compiler_params=pltpu.CompilerParams(vmem_limit_bytes=56 * MIB),
        cost_estimate=cost(15),
        name="attend",
    )(steps, queries, kv, first)


def attend_back_kernel(
    half,
    steps_ref,
    q_ref,
    kv_ref,
    first_ref,
    out_ref,
    log_ref,
    grad_ref,
    grad_q_ref,
    grad_kv_ref,
    dots,
    acc,
):
    device_index, newest = steps_ref[0], half + lax.rem(steps_ref[0], half)
    rows = kv_ref.shape[1]
    contract = lambda a, b, i: lax.dot_general(
        a, b, (((i,), (i,)), ((), ())), preferred_element_type=jnp.float32
    )
    for g in range(GROUPS):
        product = side_by_side(out_ref, g) * side_by_side(grad_ref, g).astype(jnp.float32)
        dots[g] = jnp.sum(product, axis=0, keepdims=True)
    acc[...] = jnp.zeros_like(acc)

    @pl.loop(0, 2 * half)
    def _(i):
        grad_kv_ref[i] = jnp.zeros(grad_kv_ref.shape[1:], grad_kv_ref.dtype)

    def body(hop):
        block = kv_ref[newest - hop]
        seen = masked_block(device_index - hop, first_ref, device_index, rows)
        grad_keys, grad_values = [], []
        for g in range(GROUPS):
            keys = block[:, g * HEAD : (g + 1) * HEAD]
            values = block[:, (GROUPS + g) * HEAD : (GROUPS + g + 1) * HEAD]
            queries, grads = side_by_side(q_ref, g), side_by_side(grad_ref, g)
            scores = jnp.dot(keys, queries, preferred_element_type=jnp.float32)
            probs = jnp.where(seen, jnp.exp(scores - log_ref[g]), 0.0)
            grad_probs = jnp.dot(values, grads, preferred_element_type=jnp.float32)
            grad_values.append(contract(probs.astype(jnp.bfloat16), grads, 1))
            grad_scores = (probs * (grad_probs - dots[g])).astype(jnp.bfloat16)
            grad_keys.append(contract(grad_scores, queries, 1))
            acc[g] += contract(keys, grad_scores, 0)
        grad_kv_ref[newest - hop] = jnp.concatenate(grad_keys + grad_values, 1).astype(
            grad_kv_ref.dtype
        )

    over_shards(steps_ref, body)
    for g in range(GROUPS):
        for j in range(HEADS // GROUPS):
            grad_q_ref[g, j] = (acc[g, :, j * rows : (j + 1) * rows] * (HEAD**-0.5)).astype(
                grad_q_ref.dtype
            )


def attend_back(steps, queries, kv, first, out, log_sum, grads, half):
    rows = kv.shape[1]
    wide = HEADS // GROUPS * rows
    return pl.pallas_call(
        partial(attend_back_kernel, half),
        out_shape=[
            jax.ShapeDtypeStruct(queries.shape, jnp.bfloat16),
            jax.ShapeDtypeStruct(kv.shape, jnp.bfloat16),
        ],
        in_specs=[pl.BlockSpec(memory_space=pltpu.SMEM)]
        + [pl.BlockSpec(memory_space=pltpu.VMEM)] * 6,
        out_specs=[pl.BlockSpec(memory_space=pltpu.VMEM)] * 2,
        scratch_shapes=[
            pltpu.VMEM((GROUPS, 1, wide), jnp.float32),
            pltpu.VMEM((GROUPS, HEAD, wide), jnp.float32),
        ],
        compiler_params=pltpu.CompilerParams(vmem_limit_bytes=60 * MIB),
        cost_estimate=cost(20),
        name="attend_back",
    )(steps, queries, kv, first, out, log_sum, grads)


def from_behind(x, axis, by):
    count = lax.axis_size(axis)
    pairs = [(i, i + by) for i in range(count) if 0 <= i + by < count]
    return lax.ppermute(x, axis, pairs)


def as_sent(x):
    return jax.tree.map(lambda a: a.astype(jnp.bfloat16) if a.dtype == jnp.float32 else a, x)


def gathered(x, groups):
    return lax.all_gather(x, "seq", axis_index_groups=groups, tiled=True)


def summed_rows(x, groups):
    return lax.psum_scatter(x, "seq", scatter_dimension=0, axis_index_groups=groups, tiled=True)


def exchanged(first, second, side, half):
    send = jnp.where(side == 0, second, first).astype(jnp.bfloat16)
    keep = jnp.where(side == 0, first, second)
    pairs = [(d, (d + half) % (2 * half)) for d in range(2 * half)]
    return keep, lax.ppermute(send, "seq", pairs), send


def after(x, late):
    return lax.optimization_barrier((x, late))[0]


def swapped(arrays, half, groups):
    widths = [a.shape[1] // (2 * half) for a in arrays]
    rows = arrays[0].shape[0]
    packed = jnp.concatenate([a.reshape(rows, 2, half, -1) for a in arrays], 3)
    packed = jnp.transpose(packed, (2, 0, 1, 3))
    packed = lax.all_to_all(packed, "seq", 0, 0, axis_index_groups=groups, tiled=True)
    packed = packed.reshape(half * rows, 2, -1)
    out, at = [], 0
    for width in widths:
        out.append([packed[:, k, at : at + width] for k in range(2)])
        at += width
    return out


def rms_scale(entries):
    return entries * lax.rsqrt(jnp.mean(entries * entries, axis=-1, keepdims=True) + eps)


def scaled_norm(entries, gain):
    return rms_scale(entries) * gain


def branch_mix(attn_proj, ssm_proj_out, attn_beta, ssm_beta):
    return attn_beta * rms_scale(attn_proj) + ssm_beta * rms_scale(ssm_proj_out)


def silu_slope(entries):
    sigma = jax.nn.sigmoid(entries)
    return sigma * (1.0 + entries * (1.0 - sigma))


def conv_local(conv_in, tail_x, conv_weight, place_in_item):
    row_count = conv_in.shape[0]
    tap_count = conv_weight.shape[0]
    extended = jnp.concatenate([tail_x, conv_in], 0)
    summed = conv_weight[0] * conv_in
    for tap_lag in range(1, tap_count):
        first_row = tap_count - 1 - tap_lag
        lagged = extended[first_row : first_row + row_count]
        same_item = (place_in_item >= tap_lag)[:, None]
        summed = summed + conv_weight[tap_lag] * jnp.where(same_item, lagged, 0.0)
    return jax.nn.silu(summed)


def ssm_parts(conv_in, select, tail_x, conv_weight, step_bias, decay_log, place_in_item):
    row_count = conv_in.shape[0]
    conv_out = conv_local(conv_in, tail_x, conv_weight, place_in_item)
    heads_x = conv_out.reshape(row_count, -1, SHEAD)
    b_proj = select[:, :STATE]
    c_proj = select[:, STATE : 2 * STATE]
    step_size = jax.nn.softplus(select[:, 2 * STATE :] + step_bias)
    log_decay = -step_size * jnp.exp(decay_log)
    lower_tri = (jnp.arange(row_count)[:, None] >= jnp.arange(row_count)[None, :]).astype(
        jnp.float32
    )
    cum_decay = jnp.dot(lower_tri, log_decay, precision=highest)
    scaled_x = heads_x * step_size[:, :, None]
    return (heads_x, b_proj, c_proj, cum_decay, scaled_x, lower_tri)


def ssm_output(
    conv_in,
    select,
    tail_x,
    conv_weight,
    step_bias,
    decay_log,
    skip_gain,
    held_in,
    place_in_item,
    items,
):
    heads_x, b_proj, c_proj, cum_decay, scaled_x, lower_tri = ssm_parts(
        conv_in, select, tail_x, conv_weight, step_bias, decay_log, place_in_item
    )
    same_item = (items[:, None] == items[None, :]) & (lower_tri > 0)
    exponent = jnp.where(same_item[None], cum_decay.T[:, :, None] - cum_decay.T[:, None, :], -1e30)
    weights = jnp.exp(exponent) * jnp.dot(c_proj, b_proj.T, precision=highest)[None]
    local_part = jnp.einsum("htr,rhp->thp", weights, scaled_x, precision=highest)
    follow = (items == 0).astype(jnp.float32)
    carry_weight = jnp.exp(cum_decay) * follow[:, None]
    carried = jnp.einsum("th,hpn,tn->thp", carry_weight, held_in, c_proj, precision=highest)
    outputs = local_part + carried + skip_gain[None, :, None] * heads_x
    return outputs.reshape(conv_in.shape[0], -1)


def ssm_state(conv_in, select, tail_x, conv_weight, step_bias, decay_log, place_in_item, items):
    heads_x, b_proj, c_proj, cum_decay, scaled_x, lower_tri = ssm_parts(
        conv_in, select, tail_x, conv_weight, step_bias, decay_log, place_in_item
    )
    last_same = (items == items[-1]).astype(jnp.float32)
    last_weight = jnp.exp(cum_decay[-1][None, :] - cum_decay) * last_same[:, None]
    fresh_state = jnp.einsum("rh,rhp,rn->hpn", last_weight, scaled_x, b_proj, precision=highest)
    through = (items[-1] == 0).astype(jnp.float32)
    return (fresh_state, jnp.exp(cum_decay[-1]) * through)


def per_device(
    tokens,
    seg_ids,
    meta_index,
    meta_table,
    mixer_gain,
    attn_weight,
    ssm_weight,
    select_weight,
    conv_weight,
    step_bias,
    decay_log,
    skip_gain,
    ssm_down,
    attn_beta,
    ssm_beta,
    ffn_gain,
    gate_up,
    ffn_down,
    cotangent,
):
    row_count = tokens.shape[0]
    model_width = tokens.shape[1]
    kv_width = GROUPS * HEAD
    per_group = HEADS // GROUPS
    qkv_cols = model_width + 2 * kv_width
    score_scale = 1.0 / math.sqrt(HEAD)
    devices = lax.axis_size("seq")
    device_index = lax.axis_index("seq")
    half = devices // 2
    side, place = device_index // half, device_index % half
    groups = [[h * half + q for q in range(half)] for h in range(2)]
    one_hot = (meta_index[:, None] == jnp.arange(META, dtype=jnp.int32)[None, :]).astype(
        jnp.float32
    )
    is_meta = (meta_index < META)[:, None]
    layer_in = jnp.where(
        is_meta,
        jnp.dot(one_hot.astype(jnp.bfloat16), meta_table, preferred_element_type=jnp.float32),
        tokens.astype(jnp.float32),
    )
    normed = scaled_norm(layer_in, mixer_gain).astype(jnp.bfloat16)
    query_weight = attn_weight[:, :model_width]
    kv_weight = attn_weight[:, model_width:qkv_cols]
    flip = [(d, (d + half) % devices) for d in range(devices)]
    kv = jnp.dot(normed, kv_weight, preferred_element_type=jnp.float32).astype(jnp.bfloat16)
    queries = lax.dot_general(
        query_weight, normed, (((0,), (1,)), ((), ())), preferred_element_type=jnp.float32
    )
    queries = (queries.astype(jnp.bfloat16) * score_scale).reshape(
        GROUPS, per_group, HEAD, row_count
    )
    ssm_proj = jnp.dot(normed, ssm_weight, preferred_element_type=jnp.float32)
    conv_in = ssm_proj[:, :INNER]
    z_gate = ssm_proj[:, INNER:]
    select = jnp.dot(normed, select_weight, preferred_element_type=jnp.float32)
    tail_x = from_behind(conv_in[row_count - CONV + 1 :].astype(jnp.bfloat16), "seq", 1).astype(
        jnp.float32
    )
    row = jnp.arange(row_count, dtype=jnp.int32)
    starts = jnp.where((meta_index == 0)[None, :] & (row[None, :] <= row[:, None]), 1, 0)
    items = jnp.sum(starts, axis=1)
    own_start = jnp.max(starts * (row[None, :] + 1), axis=1) - 1 + device_index * row_count
    (fresh_state, decay_all), state_pull = jax.vjp(
        partial(ssm_state, place_in_item=meta_index, items=items),
        conv_in,
        select,
        tail_x,
        conv_weight,
        step_bias,
        decay_log,
    )
    sheads = INNER // SHEAD
    padded = (sheads + 15) // 16 * 16
    state_sent = jnp.pad(
        fresh_state.reshape(sheads, SHEAD * STATE).astype(jnp.bfloat16),
        ((0, padded - sheads), (0, 0)),
    )
    last_start = jnp.where(items[-1] > 0, own_start[-1], -1).astype(jnp.float32)
    facts = jnp.concatenate(
        [decay_all, jnp.full((128 - sheads,), 1.0) * last_start]
    )
    facts = jnp.broadcast_to(facts[None, :], (8, 128))
    kv_all, states, facts = gather_both([kv, state_sent, facts], half, 0)
    ordered = facts[:, 0].reshape(2, half, 128)
    ordered = jnp.where(side == 0, ordered[::-1], ordered).reshape(devices, 128)
    shard = jnp.arange(devices, dtype=jnp.int32)
    earlier_start = jnp.max(jnp.where(shard < device_index, ordered[:, sheads], -1.0)).astype(
        jnp.int32
    )
    first = jnp.where(items > 0, own_start, earlier_start)
    steps = jnp.stack([device_index, device_index - first[0] // row_count])
    attn_full, log_sum = attend(steps, queries, kv_all, first[None, :], half)
    attended = attn_full.reshape(model_width, row_count).astype(jnp.bfloat16).T
    out_weight = attn_weight[:, qkv_cols:]
    attn_proj = jnp.dot(attended, out_weight.T, preferred_element_type=jnp.float32)
    decays = ordered[:, :sheads]
    between_before = (shard[None, :] > shard[:, None]) & (shard[None, :] < device_index)
    weight_before = jnp.where(
        (shard < device_index)[:, None],
        jnp.prod(jnp.where(between_before[:, :, None], decays[None], 1.0), axis=1),
        0.0,
    )
    between_after = (shard[None, :] < shard[:, None]) & (shard[None, :] > device_index)
    weight_after = jnp.where(
        (shard > device_index)[:, None],
        jnp.prod(jnp.where(between_after[:, :, None], decays[None], 1.0), axis=1),
        0.0,
    )
    by_slot = weight_before.reshape(2, half, sheads)
    by_slot = jnp.where(side == 0, by_slot[::-1], by_slot).reshape(devices, sheads)
    by_slot = jnp.pad(by_slot, ((0, 0), (0, padded - sheads)))
    held_in = jnp.sum(by_slot[:, :, None] * states.astype(jnp.float32), axis=0)[:sheads]
    held_in = held_in.reshape(sheads, SHEAD, STATE)
    scanned, output_pull = jax.vjp(
        partial(ssm_output, place_in_item=meta_index, items=items),
        conv_in,
        select,
        tail_x,
        conv_weight,
        step_bias,
        decay_log,
        skip_gain,
        held_in,
    )
    gated = (scanned * jax.nn.silu(z_gate)).astype(jnp.bfloat16)
    ssm_proj_out = jnp.dot(gated, ssm_down, preferred_element_type=jnp.float32)
    mixed_terms, mix_pull = jax.vjp(branch_mix, attn_proj, ssm_proj_out, attn_beta, ssm_beta)
    hidden1 = layer_in + mixed_terms
    ffn_in_f, ffn_norm_pull = jax.vjp(scaled_norm, hidden1, ffn_gain)
    ffn_in = ffn_in_f.astype(jnp.bfloat16)
    ffn_rows = gather_half([ffn_in], half, 2).reshape(half * row_count, model_width)
    cot_rows = gathered(cotangent, groups)
    units = FF // half
    wide = (units + 127) // 128 * 128
    in_weight = jnp.concatenate(
        [
            jnp.pad(
                lax.dynamic_slice_in_dim(gate_up, first_unit + place * units, units, 1),
                ((0, 0), (0, wide - units)),
            )
            for first_unit in (0, FF)
        ],
        1,
    )
    down_weight = jnp.pad(
        lax.dynamic_slice_in_dim(ffn_down, place * units, units, 0), ((0, wide - units), (0, 0))
    )
    out_terms, in_terms, in_weight_terms, down_terms = ffn(
        ffn_rows, cot_rows, in_weight, down_weight
    )
    in_terms = in_terms.reshape(half, row_count, model_width)
    grad_ffn_in = sum_half(in_terms, 1, half, 3)[0].astype(jnp.float32)
    out_sum = summed_rows(out_terms, groups)
    gate_keep, gate_sent, _ = exchanged(
        in_weight_terms[:units], in_weight_terms[wide : wide + units], side, half
    )
    down_keep, down_sent, _ = exchanged(
        down_terms[: units // 2], down_terms[units // 2 : units], side, half
    )
    grad_from_ffn, grad_ffn_gain = ffn_norm_pull(grad_ffn_in)
    grad_hidden1 = cotangent.astype(jnp.float32) + grad_from_ffn
    grad_attn_proj, grad_ssm_proj_out, grad_attn_beta, grad_ssm_beta = mix_pull(grad_hidden1)
    attn_grad_low = grad_attn_proj.astype(jnp.bfloat16)
    ssm_grad_low = grad_ssm_proj_out.astype(jnp.bfloat16)
    out_grad = (
        lax.dot_general(
            out_weight, attn_grad_low, (((0,), (1,)), ((), ())), preferred_element_type=jnp.float32
        )
        .astype(jnp.bfloat16)
        .reshape(GROUPS, per_group, HEAD, row_count)
    )
    grad_queries, kv_terms = attend_back(
        steps, queries, kv_all, first[None, :], attn_full, log_sum, out_grad, half
    )
    down_own = down_keep + after(down_sent, grad_queries).astype(jnp.float32)
    down_moved = lax.ppermute(
        down_own.astype(jnp.bfloat16),
        "seq",
        [(h * half + q, 2 * q + h) for h in range(2) for q in range(half)],
    )
    grad_kv_other, grad_kv = sum_half(kv_terms, 2, half, 1)
    grad_kv = grad_kv.astype(jnp.float32) + lax.ppermute(grad_kv_other, "seq", flip).astype(
        jnp.float32
    )
    qkv_grad = jnp.concatenate(
        [grad_queries.reshape(model_width, row_count).T, grad_kv.astype(jnp.bfloat16)], 1
    )
    gated_columns = swapped([gated], half, groups)[0]
    attn_columns = swapped([jnp.concatenate([qkv_grad, attended], 1)], half, groups)[0]
    normed_rows = gathered(normed, groups)
    attn_grad_rows = gathered(attn_grad_low, groups)
    ssm_grad_rows = gathered(ssm_grad_low, groups)
    attn_terms = []
    for k in range(2):
        block = attn_columns[k]
        width = block.shape[1]
        column = (k * half + place) * width + jnp.arange(width, dtype=jnp.int32)
        attn_terms.append(
            jnp.where(
                (column < qkv_cols)[:, None],
                jnp.dot(block.T, normed_rows, preferred_element_type=jnp.float32),
                jnp.dot(block.T, attn_grad_rows, preferred_element_type=jnp.float32),
            )
        )
    attn_keep, attn_sent, attn_send = exchanged(attn_terms[0], attn_terms[1], side, half)
    ssm_down_keep, ssm_down_sent, ssm_down_send = exchanged(
        jnp.dot(gated_columns[0].T, ssm_grad_rows, preferred_element_type=jnp.float32),
        jnp.dot(gated_columns[1].T, ssm_grad_rows, preferred_element_type=jnp.float32),
        side,
        half,
    )
    grad_gated = (
        jnp.dot(ssm_grad_low, ssm_down.T, preferred_element_type=jnp.float32)
        .astype(jnp.bfloat16)
        .astype(jnp.float32)
    )
    grad_scanned = grad_gated * jax.nn.silu(z_gate)
    grad_z_gate = grad_gated * scanned * silu_slope(z_gate)
    output_grads = output_pull(grad_scanned)
    held_grads = lax.all_gather(
        output_grads[7].reshape(sheads, SHEAD * STATE).astype(jnp.bfloat16), "seq"
    )
    later_grad = jnp.sum(weight_after[:, :, None] * held_grads.astype(jnp.float32), axis=0)
    later_grad = later_grad.reshape(sheads, SHEAD, STATE)
    grad_decay_all = jnp.sum(later_grad * held_in, axis=(1, 2))
    state_grads = state_pull((later_grad, grad_decay_all))
    grad_tail = output_grads[2] + state_grads[2]
    tail_back = from_behind(as_sent(grad_tail), "seq", -1).astype(grad_tail.dtype)
    grad_conv_in = output_grads[0] + state_grads[0]
    grad_conv_in = jnp.concatenate(
        [grad_conv_in[: row_count - CONV + 1], grad_conv_in[row_count - CONV + 1 :] + tail_back], 0
    )
    grad_select_in = (output_grads[1] + state_grads[1]).astype(jnp.bfloat16)
    grad_conv = output_grads[3] + state_grads[3]
    grad_step_bias = output_grads[4] + state_grads[4]
    grad_decay = output_grads[5] + state_grads[5]
    grad_skip = output_grads[6]
    proj_grad = jnp.concatenate([grad_conv_in, grad_z_gate], 1).astype(jnp.bfloat16)
    ssm_columns = swapped([proj_grad], half, groups)[0]
    grad_normed = jnp.dot(qkv_grad, attn_weight[:, :qkv_cols].T, preferred_element_type=jnp.float32)
    grad_normed = grad_normed + jnp.dot(proj_grad, ssm_weight.T, preferred_element_type=jnp.float32)
    grad_normed = grad_normed + jnp.dot(
        grad_select_in, select_weight.T, preferred_element_type=jnp.float32
    )
    ssm_keep, ssm_sent, ssm_send = exchanged(
        jnp.dot(ssm_columns[0].T, normed_rows, preferred_element_type=jnp.float32),
        jnp.dot(ssm_columns[1].T, normed_rows, preferred_element_type=jnp.float32),
        side,
        half,
    )
    grad_select = jnp.dot(grad_select_in.T, normed, preferred_element_type=jnp.float32)
    mixer_norm_pull = jax.vjp(scaled_norm, layer_in, mixer_gain)[1]
    grad_from_mixer, grad_mixer_gain = mixer_norm_pull(grad_normed)
    grad_layer_in = grad_hidden1 + grad_from_mixer
    grad_tokens = jnp.where(is_meta, 0.0, grad_layer_in).astype(jnp.bfloat16)
    grad_meta = jnp.dot(one_hot.T, jnp.where(is_meta, grad_layer_in, 0.0), precision=highest)
    pieces = [
        grad_meta,
        grad_select,
        grad_conv.reshape(-1, model_width),
        jnp.stack([grad_mixer_gain, grad_attn_beta, grad_ssm_beta, grad_ffn_gain]),
        jnp.pad(
            jnp.concatenate([grad_step_bias, grad_decay, grad_skip])[None, :],
            ((0, 0), (0, model_width - 3 * sheads)),
        ),
    ]
    counts = [piece.shape[0] for piece in pieces]
    share = -(-sum(counts) // (8 * devices)) * 8
    packed = jnp.concatenate(
        pieces + [jnp.zeros((share * devices - sum(counts), model_width), jnp.float32)], 0
    )
    packed = after(packed, (attn_send, ssm_down_send, ssm_send))
    packed = total_of(packed.reshape(devices, share, model_width), devices, 4)
    packed = packed.reshape(devices * share, model_width)
    at = [sum(counts[:i]) for i in range(len(counts))]
    gains = packed[at[3] : at[4]]
    little = packed[at[4]]
    small = (
        packed[: counts[0]],
        gains[0],
        packed[at[1] : at[2]].T,
        packed[at[2] : at[3]].reshape(grad_conv.shape),
        little[:sheads],
        little[sheads : 2 * sheads],
        little[2 * sheads : 3 * sheads],
        gains[1],
        gains[2],
        gains[3],
    )
    late = little

    def complete(keep, sent):
        return keep + after(sent, late).astype(jnp.float32)

    layer_out = (hidden1 + after(out_sum, late).astype(jnp.float32)).astype(jnp.bfloat16)
    shares = (
        complete(attn_keep, attn_sent).T,
        complete(ssm_keep, ssm_sent).T,
        complete(ssm_down_keep, ssm_down_sent),
        complete(gate_keep, gate_sent).T,
        after(down_moved, late).astype(jnp.float32),
    )
    return (
        layer_out,
        grad_tokens,
        small[0],
        small[1],
        shares[0],
        shares[1],
        small[2],
        small[3],
        small[4],
        small[5],
        small[6],
        shares[2],
        small[7],
        small[8],
        small[9],
        shares[3],
        shares[4],
    )


def solution(mesh):
    placed = (
        P("seq", None),
        P("seq"),
        P("seq"),
        P(),
        P(),
        P(),
        P(),
        P(),
        P(),
        P(),
        P(),
        P(),
        P(),
        P(),
        P(),
        P(),
        P(),
        P(),
        P("seq", None),
    )
    return jax.shard_map(
        per_device,
        mesh=mesh,
        in_specs=placed,
        out_specs=(
            P("seq", None),
            P("seq", None),
            P(),
            P(),
            P(None, "seq"),
            P(None, "seq"),
            P(),
            P(),
            P(),
            P(),
            P(),
            P("seq", None),
            P(),
            P(),
            P(),
            P(None, "seq"),
            P("seq", None),
        ),
        check_vma=False,
    )
```

```python
from functools import partial
import math

import jax
import jax.numpy as jnp
from jax import lax
from jax.experimental import pallas as pl
from jax.experimental.pallas import tpu as pltpu
from jax.sharding import PartitionSpec as P

HEADS = 25
GROUPS = 5
HEAD = 64
INNER = 3200
STATE = 16
CONV = 4
FF = 5504
META = 128
SHEAD = 64


eps = 1e-05
highest = lax.Precision.HIGHEST


MESH = pl.DeviceIdType.MESH
MIB = 2**20


def cost(microseconds):
    return pl.CostEstimate(
        flops=0, transcendentals=0, bytes_accessed=int(microseconds * 3_000_000)
    )


def flipped(v, k):
    bit = 1 << k
    return jnp.where(lax.rem(v // bit, 2) == 0, v + bit, v - bit)


def flips_of(v, bits):
    out = [v]
    for k in bits:
        out = out + [flipped(o, k) for o in out]
    return out


def thirds(rows):
    most = (rows // 3 + 15) // 16 * 16
    return [(0, most), (most, most), (2 * most, rows - 2 * most)]


def parts_of(rows):
    return [part for part in thirds(rows) if part[1] > 0] if rows >= 48 else [(0, rows)]


def greet(partners):
    barrier = pltpu.get_barrier_semaphore()
    for partner in partners:
        pl.semaphore_signal(barrier, inc=1, device_id=(partner,), device_id_type=MESH)
    pl.semaphore_wait(barrier, len(partners))


def remote(src, dst, send, recv, device):
    return pltpu.make_async_remote_copy(
        src_ref=src,
        dst_ref=dst,
        send_sem=send,
        recv_sem=recv,
        device_id=(device,),
        device_id_type=MESH,
    )


def gather_kernel(arrays, half, *refs):
    ins, out = refs[:arrays], refs[arrays]
    send, recv, core_send, core_recv, local_sem = refs[arrays + 1 :]
    me = lax.axis_index("seq")
    place = lax.rem(me, half)
    bits = half.bit_length() - 1
    greet([flipped(me, k) for k in range(bits)])
    parts = thirds(ins[0].shape[0])
    links = bits - 1
    orders = [[1 + (c + s) % links for s in range(links)] for c in range(3)]
    local = [
        pltpu.make_async_copy(ins[a], out.at[a * half + place], local_sem.at[a])
        for a in range(arrays)
    ]
    for copy in local:
        copy.start()
    sent, handed = [], []
    for step in range(links + 1):
        arriving = []
        for c, (first, count) in enumerate(parts):
            rows = pl.ds(first, count)
            held = flips_of(place, orders[c][:step])
            for a in range(arrays):
                if step < links:
                    for i, b in enumerate(held):
                        place_at = out.at[a * half + b, rows]
                        at = (1 << step) - 1 + i
                        copy = remote(
                            ins[a].at[rows] if i == 0 else place_at,
                            place_at,
                            send.at[a, c, at],
                            recv.at[a, c, at],
                            flipped(me, orders[c][step]),
                        )
                        copy.start()
                        arriving.append(copy)
                new = held if step == 0 else held[len(held) // 2 :]
                for i, b in enumerate(new):
                    place_at = out.at[a * half + b, rows]
                    at = 0 if step == 0 else (1 << (step - 1)) + i
                    copy = remote(
                        ins[a].at[rows] if step == 0 else place_at,
                        place_at,
                        core_send.at[a, c, at],
                        core_recv.at[a, c, at],
                        flipped(me, 0),
                    )
                    copy.start()
                    handed.append(copy)
        for copy in arriving:
            copy.wait_recv()
        sent += arriving
    for copy in sent:
        copy.wait_send()
    for copy in handed:
        copy.wait()
    for copy in local:
        copy.wait()


def gather_half(arrays, half, collective_id):
    count = len(arrays)
    shape = arrays[0].shape
    semaphores = pltpu.SemaphoreType.DMA((count, 3, half // 2))
    return pl.pallas_call(
        partial(gather_kernel, count, half),
        out_shape=jax.ShapeDtypeStruct((count * half,) + shape, arrays[0].dtype),
        in_specs=[pl.BlockSpec(memory_space=pl.ANY)] * count,
        out_specs=pl.BlockSpec(memory_space=pl.ANY),
        scratch_shapes=[semaphores] * 4 + [pltpu.SemaphoreType.DMA((count,))],
        compiler_params=pltpu.CompilerParams(collective_id=collective_id, has_side_effects=True),
        cost_estimate=cost(40),
        name="gather_half",
    )(*arrays)


def gather_both_kernel(arrays, half, *refs):
    ins, outs = refs[:arrays], refs[arrays : 2 * arrays]
    send, recv, core_send, core_recv, flip_send, flip_recv, local_sem = refs[2 * arrays :]
    me = lax.axis_index("seq")
    place = lax.rem(me, half)
    twin = jnp.where(me < half, me + half, me - half)
    bits = half.bit_length() - 1
    greet([flipped(me, k) for k in range(bits)] + [twin])
    links = bits - 1
    orders = [[1 + (c + s) % links for s in range(links)] for c in range(3)]
    parts = [parts_of(ref.shape[0]) for ref in ins]
    local, sent, handed, twins = [], [], [], []
    for a in range(arrays):
        copy = remote(ins[a], outs[a].at[place], flip_send.at[a], flip_recv.at[a], twin)
        copy.start()
        twins.append(copy)
        copy = pltpu.make_async_copy(ins[a], outs[a].at[half + place], local_sem.at[a])
        copy.start()
        local.append(copy)
    for time in range(links + 2):
        arriving = []
        for own in (1, 0):
            step = time - (1 - own)
            if step < 0 or step > links:
                continue
            for a in range(arrays):
                for c, (first, count) in enumerate(parts[a]):
                    rows = pl.ds(first, count)
                    slot = own * arrays + a
                    held = flips_of(place, orders[c][:step])
                    if step < links:
                        for i, b in enumerate(held):
                            place_at = outs[a].at[own * half + b, rows]
                            at = (1 << step) - 1 + i
                            copy = remote(
                                ins[a].at[rows] if i == 0 and own else place_at,
                                place_at,
                                send.at[slot, c, at],
                                recv.at[slot, c, at],
                                flipped(me, orders[c][step]),
                            )
                            copy.start()
                            arriving.append(copy)
                    new = held if step == 0 else held[len(held) // 2 :]
                    for i, b in enumerate(new):
                        place_at = outs[a].at[own * half + b, rows]
                        at = 0 if step == 0 else (1 << (step - 1)) + i
                        copy = remote(
                            ins[a].at[rows] if step == 0 and own else place_at,
                            place_at,
                            core_send.at[slot, c, at],
                            core_recv.at[slot, c, at],
                            flipped(me, 0),
                        )
                        copy.start()
                        handed.append(copy)
        if time == 0:
            for copy in twins:
                copy.wait_recv()
        for copy in arriving:
            copy.wait_recv()
        sent += arriving
    for copy in sent + twins:
        copy.wait_send()
    for copy in handed:
        copy.wait()
    for copy in local:
        copy.wait()


def gather_both(arrays, half, collective_id):
    count = len(arrays)
    semaphores = pltpu.SemaphoreType.DMA((2 * count, 3, half // 2))
    single = pltpu.SemaphoreType.DMA((count,))
    return pl.pallas_call(
        partial(gather_both_kernel, count, half),
        out_shape=[jax.ShapeDtypeStruct((2 * half,) + a.shape, a.dtype) for a in arrays],
        in_specs=[pl.BlockSpec(memory_space=pl.ANY)] * count,
        out_specs=[pl.BlockSpec(memory_space=pl.ANY)] * count,
        scratch_shapes=[semaphores] * 4 + [single] * 3,
        compiler_params=pltpu.CompilerParams(collective_id=collective_id, has_side_effects=True),
        cost_estimate=cost(50),
        name="gather_both",
    )(*arrays)


def total_kernel(devices, terms, out, mine, core_in, link_in, send, recv, send_back, recv_back):
    me = lax.axis_index("seq")
    bits = devices.bit_length() - 1
    greet([flipped(me, k) for k in range(bits)])
    pairs = devices // 2
    columns = terms.shape[2]
    third = columns // 3 // 128 * 128
    parts = [(0, third), (third, third), (2 * third, columns - 2 * third)]
    turned = min(3, bits - 1)
    orders = [
        [1 + (c + s) % turned for s in range(turned)] + list(range(1 + turned, bits))
        for c in range(3)
    ]
    everything = pl.ds(0, columns)
    copies = []
    first = []
    for i in range(pairs):
        block = 2 * i + 1 - lax.rem(me, 2)
        copy = remote(
            terms.at[block], core_in.at[i], send.at[0, i], recv.at[0, i], flipped(me, 0)
        )
        copy.start()
        first.append(copy)
    copies += first
    for i in range(pairs):
        first[i].wait_recv()
        mine[i] = terms[2 * i + lax.rem(me, 2)] + core_in[i]
    for step in range(bits - 1):
        arriving = []
        for c, (start, count) in enumerate(parts):
            lanes = pl.ds(start, count)
            for i, b in enumerate(flips_of(me, orders[c][step + 1 :])):
                away = flipped(b, orders[c][step])
                at = pairs - (pairs >> step) + i
                copy = remote(
                    mine.at[away // 2, :, lanes],
                    link_in.at[at, :, lanes],
                    send.at[1 + c, at],
                    recv.at[1 + c, at],
                    flipped(me, orders[c][step]),
                )
                copy.start()
                arriving.append((copy, b, at, lanes))
        for copy, b, at, lanes in arriving:
            copy.wait_recv()
            mine[b // 2, :, lanes] = mine[b // 2, :, lanes] + link_in[at, :, lanes]
            copies.append(copy)
    out[me] = mine[me // 2]
    for step in range(bits - 1):
        arriving = []
        for c, (start, count) in enumerate(parts):
            lanes = pl.ds(start, count)
            order = orders[c][::-1]
            for i, b in enumerate(flips_of(me, order[:step])):
                at = (1 << step) - 1 + i
                copy = remote(
                    out.at[b, :, lanes],
                    out.at[b, :, lanes],
                    send_back.at[1 + c, at],
                    recv_back.at[1 + c, at],
                    flipped(me, order[step]),
                )
                copy.start()
                arriving.append(copy)
        for copy in arriving:
            copy.wait_recv()
        copies += arriving
    last = []
    for i, b in enumerate(flips_of(me, range(1, bits))):
        copy = remote(
            out.at[b], out.at[b], send_back.at[0, i], recv_back.at[0, i], flipped(me, 0)
        )
        copy.start()
        last.append(copy)
    for copy in last:
        copy.wait()
    for copy in copies:
        copy.wait_send()


def total_of(terms, devices, collective_id):
    pairs = devices // 2
    half_shape = (pairs,) + terms.shape[1:]
    semaphores = pltpu.SemaphoreType.DMA((4, pairs))
    return pl.pallas_call(
        partial(total_kernel, devices),
        out_shape=jax.ShapeDtypeStruct(terms.shape, terms.dtype),
        in_specs=[pl.BlockSpec(memory_space=pltpu.VMEM)],
        out_specs=pl.BlockSpec(memory_space=pltpu.VMEM),
        scratch_shapes=[pltpu.VMEM(half_shape, terms.dtype)] * 3 + [semaphores] * 4,
        compiler_params=pltpu.CompilerParams(
            collective_id=collective_id, has_side_effects=True, vmem_limit_bytes=48 * MIB
        ),
        cost_estimate=cost(40),
        name="total_of",
    )(terms)


def sum_kernel(arrays, half, *refs):
    terms, out = refs[:2]
    mine, core_in, link_in, load_sem, send, recv, core_send, core_recv, flip_in, flip_sem = refs[2:]
    me = lax.axis_index("seq")
    place = lax.rem(me, half)
    bits = half.bit_length() - 1
    twin = jnp.where(me < half, me + half, me - half)
    greet([flipped(me, k) for k in range(bits)] + ([twin] if arrays == 2 else []))
    parts = thirds(terms.shape[1])
    links = bits - 1
    orders = [[1 + (c + s) % links for s in range(links)] for c in range(3)]
    loads = []
    pairs = half // 2
    for a in range(arrays):
        for i in range(pairs):
            block = 2 * i + lax.rem(place, 2)
            copy = pltpu.make_async_copy(
                terms.at[a * half + block], mine.at[a, i], load_sem.at[a, i]
            )
            copy.start()
            loads.append(copy)
    handed = {}
    for wanted in range(2):
        for c, (first, count) in enumerate(parts):
            rows = pl.ds(first, count)
            kept = flips_of(place, orders[c][1:])
            blocks = kept if wanted else [flipped(b, orders[c][0]) for b in kept]
            for a in range(arrays):
                for i, b in enumerate(blocks):
                    at = wanted * (pairs // 2) + i
                    copy = remote(
                        terms.at[a * half + flipped(b, 0), rows],
                        core_in.at[a, at, rows],
                        core_send.at[a, c, at],
                        core_recv.at[a, c, at],
                        flipped(me, 0),
                    )
                    copy.start()
                    handed[a, c, at] = copy
    for copy in loads:
        copy.wait()
    sent = []
    arriving = {}

    def add(ref, slot, rows, other):
        ref[slot, rows] = (
            ref[slot, rows].astype(jnp.float32) + other[...].astype(jnp.float32)
        ).astype(ref.dtype)

    for step in range(links):
        for c, (first, count) in enumerate(parts):
            rows = pl.ds(first, count)
            kept = flips_of(place, orders[c][step + 1 :])
            for a in range(arrays):
                for i, b in enumerate(kept):
                    out_block = flipped(b, orders[c][step])
                    if step == 0:
                        handed[a, c, i].wait_recv()
                        add(mine.at[a], out_block // 2, rows, core_in.at[a, i, rows])
                    at = pairs - (pairs >> step) + i
                    copy = remote(
                        mine.at[a, out_block // 2, rows],
                        link_in.at[a, at, rows],
                        send.at[a, c, at],
                        recv.at[a, c, at],
                        flipped(me, orders[c][step]),
                    )
                    copy.start()
                    arriving[a, c, at] = copy
                    sent.append(copy)
        if step == 0:
            for c, (first, count) in enumerate(parts):
                rows = pl.ds(first, count)
                for a in range(arrays):
                    for i, b in enumerate(flips_of(place, orders[c][1:])):
                        at = pairs // 2 + i
                        handed[a, c, at].wait_recv()
                        add(mine.at[a], b // 2, rows, core_in.at[a, at, rows])
        for c, (first, count) in enumerate(parts):
            rows = pl.ds(first, count)
            kept = flips_of(place, orders[c][step + 1 :])
            for a in range(arrays):
                for i, b in enumerate(kept):
                    at = pairs - (pairs >> step) + i
                    arriving[a, c, at].wait_recv()
                    add(mine.at[a], b // 2, rows, link_in.at[a, at, rows])
    if arrays == 2:
        flip = remote(mine.at[0, place // 2], flip_in, flip_sem.at[0], flip_sem.at[1], twin)
        flip.start()
        flip.wait_recv()
        out[...] = mine[1, place // 2].astype(jnp.float32) + flip_in[...].astype(jnp.float32)
        sent.append(flip)
    else:
        out[...] = mine[0, place // 2].astype(jnp.float32)
    for copy in sent:
        copy.wait_send()
    for copy in handed.values():
        copy.wait_send()


def sum_half(terms, arrays, half, collective_id):
    rows, columns = terms.shape[1:]
    pairs = half // 2
    block = (rows, columns)
    semaphores = pltpu.SemaphoreType.DMA((arrays, 3, pairs))
    return pl.pallas_call(
        partial(sum_kernel, arrays, half),
        out_shape=jax.ShapeDtypeStruct(block, jnp.float32),
        in_specs=[pl.BlockSpec(memory_space=pl.ANY)],
        out_specs=pl.BlockSpec(memory_space=pltpu.VMEM),
        scratch_shapes=[
            pltpu.VMEM((arrays, pairs) + block, terms.dtype),
            pltpu.VMEM((arrays, pairs) + block, terms.dtype),
            pltpu.VMEM((arrays, pairs) + block, terms.dtype),
            pltpu.SemaphoreType.DMA((arrays, pairs)),
        ]
        + [semaphores] * 4
        + [
            pltpu.VMEM(block if arrays == 2 else (16, 128), terms.dtype),
            pltpu.SemaphoreType.DMA((2,)),
        ],
        compiler_params=pltpu.CompilerParams(
            collective_id=collective_id, has_side_effects=True, vmem_limit_bytes=60 * MIB
        ),
        cost_estimate=cost(50),
        name="sum_half",
    )(terms)


def ffn_kernel(x_ref, cot_ref, in_ref, down_ref, out_ref, grad_in_ref, grad_w_ref, grad_d_ref):
    wide = down_ref.shape[0]
    x, cot = x_ref[...], cot_ref[...]
    low = jnp.bfloat16

    def dot(a, b, contract):
        return lax.dot_general(a, b, (contract, ((), ())), preferred_element_type=jnp.float32)

    vals = dot(x, in_ref[...], ((1,), (0,)))
    gate, up = vals[:, :wide], vals[:, wide:]
    sigma = jax.nn.sigmoid(gate)
    act = gate * sigma
    hidden = (act * up).astype(low)
    out_ref[...] = dot(hidden, down_ref[...], ((1,), (0,))).astype(low)
    grad_hidden = dot(cot, down_ref[...], ((1,), (1,))).astype(low).astype(jnp.float32)
    slope = sigma * (1.0 + gate * (1.0 - sigma))
    grads = jnp.concatenate([grad_hidden * up * slope, grad_hidden * act], 1).astype(low)
    grad_in_ref[...] = dot(grads, in_ref[...], ((1,), (1,))).astype(low)

    @pl.when(pl.program_id(0) == 0)
    def _():
        grad_w_ref[...] = jnp.zeros_like(grad_w_ref)
        grad_d_ref[...] = jnp.zeros_like(grad_d_ref)

    grad_w_ref[...] += dot(grads, x, ((0,), (0,)))
    grad_d_ref[...] += dot(hidden, cot, ((0,), (0,)))


def ffn(x, cot, in_weight, down_weight):
    rows, model = x.shape
    block = min(256, rows)
    wide = down_weight.shape[0]
    moving = pl.BlockSpec((block, model), lambda i: (i, 0))
    fixed = lambda shape: pl.BlockSpec(shape, lambda i: (0, 0))
    return pl.pallas_call(
        ffn_kernel,
        grid=(rows // block,),
        out_shape=[
            jax.ShapeDtypeStruct(x.shape, jnp.bfloat16),
            jax.ShapeDtypeStruct(x.shape, jnp.bfloat16),
            jax.ShapeDtypeStruct((2 * wide, model), jnp.float32),
            jax.ShapeDtypeStruct((wide, model), jnp.float32),
        ],
        in_specs=[moving, moving, fixed(in_weight.shape), fixed(down_weight.shape)],
        out_specs=[moving, moving, fixed((2 * wide, model)), fixed((wide, model))],
        compiler_params=pltpu.CompilerParams(vmem_limit_bytes=56 * MIB),
        cost_estimate=cost(35),
        name="ffn",
    )(x, cot, in_weight, down_weight)


def masked_block(at, first_ref, device_index, rows):
    key = lax.broadcasted_iota(jnp.int32, (rows, rows), 0) + at * rows
    query = lax.broadcasted_iota(jnp.int32, (rows, rows), 1) + device_index * rows
    seen = ((key >= first_ref[...]) & (key <= query)).astype(jnp.float32)
    return jnp.concatenate([seen] * (HEADS // GROUPS), 1) > 0.0


def side_by_side(ref, g):
    return jnp.concatenate([ref[g, j] for j in range(HEADS // GROUPS)], 1)


def over_shards(steps_ref, body):
    body(0)

    @pl.loop(1, steps_ref[1] + 1)
    def _(hop):
        body(hop)


def attend_kernel(half, steps_ref, q_ref, kv_ref, first_ref, out_ref, log_ref, top, total, acc):
    device_index, newest = steps_ref[0], half + lax.rem(steps_ref[0], half)
    rows = kv_ref.shape[1]
    top[...] = jnp.full_like(top, -1e30)
    total[...] = jnp.zeros_like(total)
    acc[...] = jnp.zeros_like(acc)

    def body(hop):
        block = kv_ref[newest - hop]
        seen = masked_block(device_index - hop, first_ref, device_index, rows)
        for g in range(GROUPS):
            keys = block[:, g * HEAD : (g + 1) * HEAD]
            values = block[:, (GROUPS + g) * HEAD : (GROUPS + g + 1) * HEAD]
            scores = jnp.dot(keys, side_by_side(q_ref, g), preferred_element_type=jnp.float32)
            scores = jnp.where(seen, scores, -1e30)
            now = jnp.maximum(top[g], jnp.max(scores, axis=0, keepdims=True))
            probs = jnp.exp(scores - now)
            fade = jnp.exp(top[g] - now)
            top[g] = now
            total[g] = total[g] * fade + jnp.sum(probs, axis=0, keepdims=True)
            acc[g] = acc[g] * fade + lax.dot_general(
                values,
                probs.astype(jnp.bfloat16),
                (((0,), (0,)), ((), ())),
                preferred_element_type=jnp.float32,
            )

    over_shards(steps_ref, body)
    for g in range(GROUPS):
        done = acc[g] / total[g]
        for j in range(HEADS // GROUPS):
            out_ref[g, j] = done[:, j * rows : (j + 1) * rows]
        log_ref[g] = top[g] + jnp.log(total[g])


def attend(steps, queries, kv, first, half):
    rows = kv.shape[1]
    per_group = HEADS // GROUPS
    wide = per_group * rows
    return pl.pallas_call(
        partial(attend_kernel, half),
        out_shape=[
            jax.ShapeDtypeStruct((GROUPS, per_group, HEAD, rows), jnp.float32),
            jax.ShapeDtypeStruct((GROUPS, 1, wide), jnp.float32),
        ],
        in_specs=[pl.BlockSpec(memory_space=pltpu.SMEM)]
        + [pl.BlockSpec(memory_space=pltpu.VMEM)] * 3,
        out_specs=[pl.BlockSpec(memory_space=pltpu.VMEM)] * 2,
        scratch_shapes=[
            pltpu.VMEM((GROUPS, 1, wide), jnp.float32),
            pltpu.VMEM((GROUPS, 1, wide), jnp.float32),
            pltpu.VMEM((GROUPS, HEAD, wide), jnp.float32),
        ],
        compiler_params=pltpu.CompilerParams(vmem_limit_bytes=56 * MIB),
        cost_estimate=cost(15),
        name="attend",
    )(steps, queries, kv, first)


def attend_back_kernel(
    half,
    steps_ref,
    q_ref,
    kv_ref,
    first_ref,
    out_ref,
    log_ref,
    grad_ref,
    grad_q_ref,
    grad_kv_ref,
    dots,
    acc,
):
    device_index, newest = steps_ref[0], half + lax.rem(steps_ref[0], half)
    rows = kv_ref.shape[1]
    contract = lambda a, b, i: lax.dot_general(
        a, b, (((i,), (i,)), ((), ())), preferred_element_type=jnp.float32
    )
    for g in range(GROUPS):
        product = side_by_side(out_ref, g) * side_by_side(grad_ref, g).astype(jnp.float32)
        dots[g] = jnp.sum(product, axis=0, keepdims=True)
    acc[...] = jnp.zeros_like(acc)

    @pl.loop(0, 2 * half)
    def _(i):
        grad_kv_ref[i] = jnp.zeros(grad_kv_ref.shape[1:], grad_kv_ref.dtype)

    def body(hop):
        block = kv_ref[newest - hop]
        seen = masked_block(device_index - hop, first_ref, device_index, rows)
        grad_keys, grad_values = [], []
        for g in range(GROUPS):
            keys = block[:, g * HEAD : (g + 1) * HEAD]
            values = block[:, (GROUPS + g) * HEAD : (GROUPS + g + 1) * HEAD]
            queries, grads = side_by_side(q_ref, g), side_by_side(grad_ref, g)
            scores = jnp.dot(keys, queries, preferred_element_type=jnp.float32)
            probs = jnp.where(seen, jnp.exp(scores - log_ref[g]), 0.0)
            grad_probs = jnp.dot(values, grads, preferred_element_type=jnp.float32)
            grad_values.append(contract(probs.astype(jnp.bfloat16), grads, 1))
            grad_scores = (probs * (grad_probs - dots[g])).astype(jnp.bfloat16)
            grad_keys.append(contract(grad_scores, queries, 1))
            acc[g] += contract(keys, grad_scores, 0)
        grad_kv_ref[newest - hop] = jnp.concatenate(grad_keys + grad_values, 1).astype(
            grad_kv_ref.dtype
        )

    over_shards(steps_ref, body)
    for g in range(GROUPS):
        for j in range(HEADS // GROUPS):
            grad_q_ref[g, j] = (acc[g, :, j * rows : (j + 1) * rows] * (HEAD**-0.5)).astype(
                grad_q_ref.dtype
            )


def attend_back(steps, queries, kv, first, out, log_sum, grads, half):
    rows = kv.shape[1]
    wide = HEADS // GROUPS * rows
    return pl.pallas_call(
        partial(attend_back_kernel, half),
        out_shape=[
            jax.ShapeDtypeStruct(queries.shape, jnp.bfloat16),
            jax.ShapeDtypeStruct(kv.shape, jnp.bfloat16),
        ],
        in_specs=[pl.BlockSpec(memory_space=pltpu.SMEM)]
        + [pl.BlockSpec(memory_space=pltpu.VMEM)] * 6,
        out_specs=[pl.BlockSpec(memory_space=pltpu.VMEM)] * 2,
        scratch_shapes=[
            pltpu.VMEM((GROUPS, 1, wide), jnp.float32),
            pltpu.VMEM((GROUPS, HEAD, wide), jnp.float32),
        ],
        compiler_params=pltpu.CompilerParams(vmem_limit_bytes=60 * MIB),
        cost_estimate=cost(20),
        name="attend_back",
    )(steps, queries, kv, first, out, log_sum, grads)


def spread_heads(ref, tile, rows):
    first_half = lax.broadcasted_iota(jnp.int32, (rows, 128), 1) < SHEAD
    return jnp.where(
        first_half, ref[:, 2 * tile : 2 * tile + 1], ref[:, 2 * tile + 1 : 2 * tile + 2]
    )


def conv_tile(proj_ref, tail_ref, taps_ref, place, extended, at, rows):
    extended[8 : 8 + rows] = proj_ref[:, at]
    extended[0:8] = tail_ref[:, at]
    lagged = []
    summed = jnp.zeros((rows, 128), jnp.float32)
    for lag in range(taps_ref.shape[0]):
        moved = extended[8 - lag : 8 - lag + rows]
        moved = moved if lag == 0 else jnp.where(place >= lag, moved, 0.0)
        lagged.append(moved)
        summed = summed + taps_ref[lag : lag + 1, at] * moved
    return summed, lagged


def ssm_state_kernel(
    proj_ref,
    tail_ref,
    taps_ref,
    place_ref,
    items_ref,
    select_ref,
    bias_ref,
    rate_ref,
    state_ref,
    b_ref,
    c_ref,
    raw_ref,
    step_ref,
    cum_ref,
    cum_t_ref,
    last_ref,
    carry_ref,
    all_ref,
    extended,
):
    rows, inner = proj_ref.shape[0], taps_ref.shape[1]
    heads = step_ref.shape[1]
    low = jnp.bfloat16
    b_ref[...] = select_ref[:, :STATE].astype(low)
    c_ref[...] = select_ref[:, STATE : 2 * STATE].astype(low)
    raw = select_ref[:, 2 * STATE :] + bias_ref[...]
    raw_ref[...] = raw
    step = jnp.maximum(raw, 0.0) + jnp.log1p(jnp.exp(-jnp.abs(raw)))
    step_ref[...] = step
    lower = (
        lax.broadcasted_iota(jnp.int32, (rows, rows), 0)
        >= lax.broadcasted_iota(jnp.int32, (rows, rows), 1)
    ).astype(jnp.float32)
    cum = jnp.dot(
        lower, -step * rate_ref[...], precision=highest, preferred_element_type=jnp.float32
    )
    cum_ref[...] = cum
    wide = jnp.concatenate([cum, jnp.zeros((rows, 128 - heads), jnp.float32)], 1)
    cum_t_ref[...] = wide.T[:heads]
    items = items_ref[...]
    final = items_ref[rows - 1 : rows, :]
    total = cum[rows - 1 : rows, :]
    last_ref[...] = jnp.where(items == final, jnp.exp(total - cum), 0.0)
    carry_ref[...] = jnp.where(items == 0, jnp.exp(cum), 0.0)
    all_ref[...] = jnp.where(final == 0, jnp.exp(total), 0.0)
    place = place_ref[...]
    b = b_ref[...]
    for tile in range(inner // 128):
        at = slice(tile * 128, (tile + 1) * 128)
        summed, _ = conv_tile(proj_ref, tail_ref, taps_ref, place, extended, at, rows)
        x = summed * jax.nn.sigmoid(summed)
        taken = x * spread_heads(step_ref, tile, rows) * spread_heads(last_ref, tile, rows)
        state_ref[:, at] = lax.dot_general(
            b, taken.astype(low), (((0,), (0,)), ((), ())), preferred_element_type=jnp.float32
        ).astype(low)


def whole_call(kernel, operands, outs, scratch, microseconds, name):
    return pl.pallas_call(
        kernel,
        out_shape=[jax.ShapeDtypeStruct(dims, kind) for dims, kind in outs],
        in_specs=[pl.BlockSpec(memory_space=pltpu.VMEM)] * len(operands),
        out_specs=[pl.BlockSpec(memory_space=pltpu.VMEM)] * len(outs),
        scratch_shapes=scratch,
        compiler_params=pltpu.CompilerParams(vmem_limit_bytes=48 * MIB),
        cost_estimate=cost(microseconds),
        name=name,
    )(*operands)


def ssm_state(proj, tail, taps, place, items, select, bias, rate):
    rows, inner, heads = proj.shape[0], taps.shape[1], bias.shape[1]
    low, full = jnp.bfloat16, jnp.float32
    by_head = ((rows, heads), full)
    outs = [((STATE, inner), low), ((rows, STATE), low), ((rows, STATE), low)]
    outs += [by_head, by_head, by_head, ((heads, rows), full), by_head, by_head]
    outs += [((1, heads), full)]
    operands = (proj, tail, taps, place, items, select, bias, rate)
    scratch = [pltpu.VMEM((rows + 8, 128), full)]
    return whole_call(ssm_state_kernel, operands, outs, scratch, 8, "ssm_state")


def ssm_output_kernel(
    proj_ref,
    tail_ref,
    taps_ref,
    place_ref,
    b_ref,
    c_ref,
    cum_ref,
    cum_t_ref,
    step_ref,
    skip_ref,
    carry_ref,
    same_ref,
    held_ref,
    scanned_ref,
    gated_ref,
    extended,
):
    rows, inner = proj_ref.shape[0], taps_ref.shape[1]
    low = jnp.bfloat16
    place, c = place_ref[...], c_ref[...]
    both = lax.dot_general(
        c, b_ref[...], (((1,), (1,)), ((), ())), preferred_element_type=jnp.float32
    )
    same = same_ref[...] > 0.0
    first_half = lax.broadcasted_iota(jnp.int32, (rows, 128), 1) < SHEAD
    for tile in range(inner // 128):
        at = slice(tile * 128, (tile + 1) * 128)
        summed, _ = conv_tile(proj_ref, tail_ref, taps_ref, place, extended, at, rows)
        x = summed * jax.nn.sigmoid(summed)
        scaled = (x * spread_heads(step_ref, tile, rows)).astype(low)
        halves = []
        for k in range(2):
            head = 2 * tile + k
            exponent = jnp.where(
                same, cum_ref[:, head : head + 1] - cum_t_ref[head : head + 1, :], -1e30
            )
            weights = (jnp.exp(exponent) * both).astype(low)
            halves.append(jnp.dot(weights, scaled, preferred_element_type=jnp.float32))
        carried = jnp.dot(c, held_ref[:, at].astype(low), preferred_element_type=jnp.float32)
        out = (
            jnp.where(first_half, halves[0], halves[1])
            + carried * spread_heads(carry_ref, tile, rows)
            + spread_heads(skip_ref, tile, rows) * x
        )
        scanned_ref[:, at] = out
        z = proj_ref[:, inner + tile * 128 : inner + (tile + 1) * 128]
        gated_ref[:, at] = (out * z * jax.nn.sigmoid(z)).astype(low)


def ssm_output(*operands):
    rows, inner = operands[0].shape[0], operands[2].shape[1]
    outs = [((rows, inner), jnp.float32), ((rows, inner), jnp.bfloat16)]
    scratch = [pltpu.VMEM((rows + 8, 128), jnp.float32)]
    return whole_call(ssm_output_kernel, operands, outs, scratch, 8, "ssm_output")


def held_grad_kernel(proj_ref, grad_ref, carry_ref, c_ref, out_ref):
    rows, inner = grad_ref.shape
    for tile in range(inner // 128):
        at = slice(tile * 128, (tile + 1) * 128)
        z = proj_ref[:, inner + tile * 128 : inner + (tile + 1) * 128]
        grad = grad_ref[:, at].astype(jnp.float32) * z * jax.nn.sigmoid(z)
        grad = (grad * spread_heads(carry_ref, tile, rows)).astype(jnp.bfloat16)
        out_ref[:, at] = lax.dot_general(
            c_ref[...], grad, (((0,), (0,)), ((), ())), preferred_element_type=jnp.float32
        ).astype(jnp.bfloat16)


def held_grad(proj, grad, carry, c):
    outs = [((STATE, grad.shape[1]), jnp.bfloat16)]
    return whole_call(held_grad_kernel, (proj, grad, carry, c), outs, [], 4, "held_grad")[0]


def ssm_back_kernel(
    proj_ref,
    tail_ref,
    taps_ref,
    place_ref,
    grad_ref,
    scanned_ref,
    b_ref,
    c_ref,
    cum_ref,
    cum_t_ref,
    step_ref,
    raw_ref,
    rate_ref,
    skip_ref,
    last_ref,
    carry_ref,
    same_ref,
    held_ref,
    later_ref,
    grad_all_ref,
    grad_conv_ref,
    grad_z_ref,
    end_ref,
    grad_tail_ref,
    grad_b_ref,
    grad_c_ref,
    grad_raw_ref,
    grad_taps_ref,
    grad_heads_ref,
    extended,
    sums,
    columns,
):
    rows = b_ref.shape[0]
    inner = taps_ref.shape[1]
    tap_count = taps_ref.shape[0]
    heads = step_ref.shape[1]
    low = jnp.bfloat16

    def dot(a, b, left=1, right=0):
        return lax.dot_general(
            a, b, (((left,), (right,)), ((), ())), preferred_element_type=jnp.float32
        )

    lane = lax.broadcasted_iota(jnp.int32, (rows, 128), 1)
    first_half = lane < SHEAD
    place = place_ref[...]
    b, c = b_ref[...], c_ref[...]
    both = dot(c, b, 1, 1)
    same = same_ref[...] > 0.0
    sums[...] = jnp.zeros_like(sums)
    columns[...] = jnp.zeros_like(columns)
    grad_b = jnp.zeros((rows, STATE), jnp.float32)
    grad_c = jnp.zeros((rows, STATE), jnp.float32)
    grad_both = jnp.zeros((rows, rows), jnp.float32)
    grad_skip = jnp.zeros((1, 128), jnp.float32)
    picker_row = lax.broadcasted_iota(jnp.int32, (128, 128), 0)
    picker_lane = lax.broadcasted_iota(jnp.int32, (128, 128), 1)

    def head_sums(values, tile):
        pick = (picker_lane == 2 * tile + picker_row // SHEAD).astype(low)
        high = values.astype(low)
        rest = (values - high.astype(jnp.float32)).astype(low)
        return dot(high, pick) + dot(rest, pick)

    def spread(ref, tile):
        return jnp.where(
            first_half,
            ref[:, 2 * tile : 2 * tile + 1],
            ref[:, 2 * tile + 1 : 2 * tile + 2],
        )

    for tile in range(inner // 128):
        at = slice(tile * 128, (tile + 1) * 128)
        z_at = slice(inner + tile * 128, inner + (tile + 1) * 128)
        extended[8 : 8 + rows] = proj_ref[:, at]
        extended[0:8] = tail_ref[:, at]
        lagged = []
        summed = jnp.zeros((rows, 128), jnp.float32)
        for lag in range(tap_count):
            moved = extended[8 - lag : 8 - lag + rows]
            moved = moved if lag == 0 else jnp.where(place >= lag, moved, 0.0)
            lagged.append(moved)
            summed = summed + taps_ref[lag : lag + 1, at] * moved
        sigma = jax.nn.sigmoid(summed)
        x = summed * sigma
        step = spread(step_ref, tile)
        scaled = x * step
        z = proj_ref[:, z_at]
        z_sigma = jax.nn.sigmoid(z)
        grad_gated = grad_ref[:, at].astype(jnp.float32)
        grad_y = grad_gated * z * z_sigma
        grad_z_ref[:, at] = (
            grad_gated * scanned_ref[:, at] * (z_sigma * (1.0 + z * (1.0 - z_sigma)))
        ).astype(low)
        held, later = held_ref[:, at].astype(low), later_ref[:, at].astype(low)
        last, carry = spread(last_ref, tile), spread(carry_ref, tile)
        from_later = dot(b, later)
        from_held = dot(c, held)
        grad_b = grad_b + dot((scaled * last).astype(low), later, 1, 1)
        carried_grad = grad_y * carry
        grad_c = grad_c + dot(carried_grad.astype(low), held, 1, 1)
        cum_grad = head_sums(carried_grad * from_held - scaled * last * from_later, tile)
        last_total = head_sums(
            jnp.sum(scaled * last * from_later, axis=0, keepdims=True), tile
        )
        grad_scaled = last * from_later
        grad_skip = grad_skip + head_sums(jnp.sum(grad_y * x, axis=0, keepdims=True), tile)
        grad_low, scaled_low = grad_y.astype(low), scaled.astype(low)
        halves = []
        for k in range(2):
            head = 2 * tile + k
            mine = first_half if k == 0 else ~first_half
            exponent = jnp.where(
                same, cum_ref[:, head : head + 1] - cum_t_ref[head : head + 1, :], -1e30
            )
            fade = jnp.exp(exponent)
            weights = fade * both
            halves.append(dot(weights.astype(low), grad_low, 0, 0))
            grad_weights = dot(jnp.where(mine, grad_y, 0.0).astype(low), scaled_low, 1, 1)
            grad_both = grad_both + grad_weights * fade
            grad_exponent = grad_weights * weights
            columns[head : head + 1, :] = jnp.sum(grad_exponent, axis=0, keepdims=True)
            pick = (picker_lane == head).astype(low)
            high = grad_exponent.astype(low)
            rest = (grad_exponent - high.astype(jnp.float32)).astype(low)
            cum_grad = cum_grad + dot(high, pick) + dot(rest, pick)
        grad_scaled = grad_scaled + jnp.where(first_half, halves[0], halves[1])
        sums[0] += cum_grad
        sums[1] += head_sums(grad_scaled * x, tile)
        sums[2] += last_total
        grad_x = grad_scaled * step + spread(skip_ref, tile) * grad_y
        grad_summed = grad_x * (sigma * (1.0 + summed * (1.0 - sigma)))
        for lag in range(tap_count):
            grad_taps_ref[lag : lag + 1, at] = jnp.sum(
                grad_summed * lagged[lag], axis=0, keepdims=True
            )
        extended[...] = jnp.zeros_like(extended)
        for lag in range(tap_count):
            moved = taps_ref[lag : lag + 1, at] * grad_summed
            moved = moved if lag == 0 else jnp.where(place >= lag, moved, 0.0)
            extended[8 - lag : 8 - lag + rows] += moved
        grad_conv_ref[:, at] = extended[8 : 8 + rows].astype(low)
        end_ref[:, at] = extended[rows : 8 + rows]
        grad_tail_ref[:, at] = extended[0:8]

    grad_c_ref[...] = grad_c + dot(grad_both.astype(low), b)
    grad_b_ref[...] = grad_b + dot(grad_both.astype(low), c, 0, 0)
    row_at = lax.broadcasted_iota(jnp.int32, (rows, 128), 0)
    cum_grad = sums[0] - columns[...].T
    cum_grad = cum_grad + jnp.where(row_at == rows - 1, sums[2] + grad_all_ref[...], 0.0)
    upper = (
        lax.broadcasted_iota(jnp.int32, (rows, rows), 0)
        <= lax.broadcasted_iota(jnp.int32, (rows, rows), 1)
    ).astype(jnp.float32)
    log_grad = jnp.dot(upper, cum_grad, precision=highest, preferred_element_type=jnp.float32)
    log_grad = log_grad[:, :heads]
    rate = rate_ref[...]
    step = step_ref[...]
    raw_grad = (sums[1][:, :heads] - rate * log_grad) * jax.nn.sigmoid(raw_ref[...])
    grad_raw_ref[...] = raw_grad
    grad_heads_ref[0:1, :] = jnp.sum(raw_grad, axis=0, keepdims=True)
    grad_heads_ref[1:2, :] = jnp.sum(-rate * step * log_grad, axis=0, keepdims=True)
    grad_heads_ref[2:3, :] = grad_skip[:, :heads]
    grad_heads_ref[3:8, :] = jnp.zeros((5, heads), jnp.float32)


def ssm_back(*operands):
    proj, taps, b, step = operands[0], operands[2], operands[6], operands[10]
    rows, inner = proj.shape[0], taps.shape[1]
    heads = step.shape[1]
    shape = lambda dims, kind: jax.ShapeDtypeStruct(dims, kind)
    outs = [
        shape((rows, inner), jnp.bfloat16),
        shape((rows, inner), jnp.bfloat16),
        shape((8, inner), jnp.float32),
        shape((8, inner), jnp.float32),
        shape((rows, STATE), jnp.float32),
        shape((rows, STATE), jnp.float32),
        shape((rows, heads), jnp.float32),
        shape(taps.shape, jnp.float32),
        shape((8, heads), jnp.float32),
    ]
    return pl.pallas_call(
        ssm_back_kernel,
        out_shape=outs,
        in_specs=[pl.BlockSpec(memory_space=pltpu.VMEM)] * len(operands),
        out_specs=[pl.BlockSpec(memory_space=pltpu.VMEM)] * len(outs),
        scratch_shapes=[
            pltpu.VMEM((rows + 8, 128), jnp.float32),
            pltpu.VMEM((3, rows, 128), jnp.float32),
            pltpu.VMEM((128, rows), jnp.float32),
        ],
        compiler_params=pltpu.CompilerParams(vmem_limit_bytes=48 * MIB),
        cost_estimate=cost(20),
        name="ssm_back",
    )(*operands)


def from_behind(x, axis, by):
    count = lax.axis_size(axis)
    pairs = [(i, i + by) for i in range(count) if 0 <= i + by < count]
    return lax.ppermute(x, axis, pairs)


def as_sent(x):
    return jax.tree.map(lambda a: a.astype(jnp.bfloat16) if a.dtype == jnp.float32 else a, x)


def gathered(x, groups):
    return lax.all_gather(x, "seq", axis_index_groups=groups, tiled=True)


def summed_rows(x, groups):
    return lax.psum_scatter(x, "seq", scatter_dimension=0, axis_index_groups=groups, tiled=True)


def after(x, late):
    return lax.optimization_barrier((x, late))[0]


def exchanged(first, second, side, half, late=None):
    send = jnp.where(side == 0, second, first).astype(jnp.bfloat16)
    keep = jnp.where(side == 0, first, second)
    if late is not None:
        send = after(send, late)
    pairs = [(d, (d + half) % (2 * half)) for d in range(2 * half)]
    return keep, lax.ppermute(send, "seq", pairs), send


def swapped(arrays, half, groups, late=None):
    widths = [a.shape[1] // (2 * half) for a in arrays]
    rows = arrays[0].shape[0]
    packed = jnp.concatenate([a.reshape(rows, 2, half, -1) for a in arrays], 3)
    packed = jnp.transpose(packed, (2, 0, 1, 3))
    packed = lax.all_to_all(packed, "seq", 0, 0, axis_index_groups=groups, tiled=True)
    if late is not None:
        packed = after(packed, late)
    packed = packed.reshape(half * rows, 2, -1)
    out, at = [], 0
    for width in widths:
        out.append([packed[:, k, at : at + width] for k in range(2)])
        at += width
    return out


def rms_scale(entries):
    return entries * lax.rsqrt(jnp.mean(entries * entries, axis=-1, keepdims=True) + eps)


def scaled_norm(entries, gain):
    return rms_scale(entries) * gain


def branch_mix(attn_proj, ssm_proj_out, attn_beta, ssm_beta):
    return attn_beta * rms_scale(attn_proj) + ssm_beta * rms_scale(ssm_proj_out)


def per_device(
    tokens,
    seg_ids,
    meta_index,
    meta_table,
    mixer_gain,
    attn_weight,
    ssm_weight,
    select_weight,
    conv_weight,
    step_bias,
    decay_log,
    skip_gain,
    ssm_down,
    attn_beta,
    ssm_beta,
    ffn_gain,
    gate_up,
    ffn_down,
    cotangent,
):
    row_count = tokens.shape[0]
    model_width = tokens.shape[1]
    kv_width = GROUPS * HEAD
    per_group = HEADS // GROUPS
    qkv_cols = model_width + 2 * kv_width
    score_scale = 1.0 / math.sqrt(HEAD)
    devices = lax.axis_size("seq")
    device_index = lax.axis_index("seq")
    half = devices // 2
    side, place = device_index // half, device_index % half
    groups = [[h * half + q for q in range(half)] for h in range(2)]
    one_hot = (meta_index[:, None] == jnp.arange(META, dtype=jnp.int32)[None, :]).astype(
        jnp.float32
    )
    is_meta = (meta_index < META)[:, None]
    layer_in = jnp.where(
        is_meta,
        jnp.dot(one_hot.astype(jnp.bfloat16), meta_table, preferred_element_type=jnp.float32),
        tokens.astype(jnp.float32),
    )
    normed = scaled_norm(layer_in, mixer_gain).astype(jnp.bfloat16)
    query_weight = attn_weight[:, :model_width]
    kv_weight = attn_weight[:, model_width:qkv_cols]
    kv = jnp.dot(normed, kv_weight, preferred_element_type=jnp.float32).astype(jnp.bfloat16)
    queries = lax.dot_general(
        query_weight, normed, (((0,), (1,)), ((), ())), preferred_element_type=jnp.float32
    )
    queries = (queries.astype(jnp.bfloat16) * score_scale).reshape(
        GROUPS, per_group, HEAD, row_count
    )
    ssm_proj = jnp.dot(normed, ssm_weight, preferred_element_type=jnp.float32)
    select = jnp.dot(normed, select_weight, preferred_element_type=jnp.float32)
    last_rows = ssm_proj[row_count - CONV + 1 :, :INNER].astype(jnp.bfloat16)
    tail_x = jnp.pad(
        from_behind(last_rows, "seq", 1).astype(jnp.float32), ((8 - CONV + 1, 0), (0, 0))
    )
    row = jnp.arange(row_count, dtype=jnp.int32)
    starts = jnp.where((meta_index == 0)[None, :] & (row[None, :] <= row[:, None]), 1, 0)
    items = jnp.sum(starts, axis=1)
    own_start = jnp.max(starts * (row[None, :] + 1), axis=1) - 1 + device_index * row_count
    same_item = ((items[:, None] == items[None, :]) & (row[None, :] <= row[:, None])).astype(
        jnp.float32
    )
    sheads = INNER // SHEAD
    place_in_item = meta_index[:, None]
    rate = jnp.exp(decay_log)[None, :]
    state, b_proj, c_proj, raw, step_size, cum, cum_t, last_weight, carry_weight, decay_all = (
        ssm_state(
            ssm_proj,
            tail_x,
            conv_weight,
            place_in_item,
            items[:, None],
            select,
            step_bias[None, :],
            rate,
        )
    )
    states = lax.all_gather(state, "seq")
    last_start = jnp.where(items[-1] > 0, own_start[-1], -1).astype(jnp.float32)
    facts = jnp.concatenate(
        [decay_all[0], jnp.full((128 - sheads,), 1.0) * last_start]
    )
    facts = jnp.broadcast_to(facts[None, :], (8, 128))
    kv_all, facts = gather_both([kv, facts], half, 0)
    ordered = facts[:, 0].reshape(2, half, 128)
    ordered = jnp.where(side == 0, ordered[::-1], ordered).reshape(devices, 128)
    shard = jnp.arange(devices, dtype=jnp.int32)
    earlier_start = jnp.max(jnp.where(shard < device_index, ordered[:, sheads], -1.0)).astype(
        jnp.int32
    )
    first = jnp.where(items > 0, own_start, earlier_start)
    steps = jnp.stack([device_index, device_index - first[0] // row_count])
    attn_full, log_sum = attend(steps, queries, kv_all, first[None, :], half)
    attended = attn_full.reshape(model_width, row_count).astype(jnp.bfloat16).T
    out_weight = attn_weight[:, qkv_cols:]
    attn_proj = jnp.dot(attended, out_weight.T, preferred_element_type=jnp.float32)
    decays = ordered[:, :sheads]
    between_before = (shard[None, :] > shard[:, None]) & (shard[None, :] < device_index)
    weight_before = jnp.where(
        (shard < device_index)[:, None],
        jnp.prod(jnp.where(between_before[:, :, None], decays[None], 1.0), axis=1),
        0.0,
    )
    between_after = (shard[None, :] < shard[:, None]) & (shard[None, :] > device_index)
    weight_after = jnp.where(
        (shard > device_index)[:, None],
        jnp.prod(jnp.where(between_after[:, :, None], decays[None], 1.0), axis=1),
        0.0,
    )
    per_channel = lambda weight: jnp.repeat(weight, SHEAD, axis=1)[:, None, :]
    held_in = jnp.sum(per_channel(weight_before) * states.astype(jnp.float32), axis=0)
    scanned, gated = ssm_output(
        ssm_proj,
        tail_x,
        conv_weight,
        place_in_item,
        b_proj,
        c_proj,
        cum,
        cum_t,
        step_size,
        skip_gain[None, :],
        carry_weight,
        same_item,
        held_in,
    )
    ssm_proj_out = jnp.dot(gated, ssm_down, preferred_element_type=jnp.float32)
    mixed_terms, mix_pull = jax.vjp(branch_mix, attn_proj, ssm_proj_out, attn_beta, ssm_beta)
    hidden1 = layer_in + mixed_terms
    ffn_in_f, ffn_norm_pull = jax.vjp(scaled_norm, hidden1, ffn_gain)
    ffn_in = ffn_in_f.astype(jnp.bfloat16)
    ffn_rows = gather_half([ffn_in], half, 2).reshape(half * row_count, model_width)
    cot_rows = gathered(cotangent, groups)
    units = FF // half
    wide = (units + 127) // 128 * 128
    in_weight = jnp.concatenate(
        [
            jnp.pad(
                lax.dynamic_slice_in_dim(gate_up, first_unit + place * units, units, 1),
                ((0, 0), (0, wide - units)),
            )
            for first_unit in (0, FF)
        ],
        1,
    )
    down_weight = jnp.pad(
        lax.dynamic_slice_in_dim(ffn_down, place * units, units, 0), ((0, wide - units), (0, 0))
    )
    out_terms, in_terms, in_weight_terms, down_terms = ffn(
        ffn_rows, cot_rows, in_weight, down_weight
    )
    in_terms = in_terms.reshape(half, row_count, model_width)
    grad_ffn_in = sum_half(in_terms, 1, half, 3)
    gate_keep, gate_sent, _ = exchanged(
        in_weight_terms[:units], in_weight_terms[wide : wide + units], side, half
    )
    down_low = down_terms[:units].astype(jnp.bfloat16).reshape(2, units // 2, model_width)
    down_low = jnp.where(side == 0, down_low, down_low[::-1])
    down_sent = [
        lax.ppermute(
            down_low[k],
            "seq",
            [(h * half + q, 2 * q + (h + k) % 2) for h in range(2) for q in range(half)],
        )
        for k in range(2)
    ]
    grad_from_ffn, grad_ffn_gain = ffn_norm_pull(grad_ffn_in)
    grad_hidden1 = cotangent.astype(jnp.float32) + grad_from_ffn
    grad_attn_proj, grad_ssm_proj_out, grad_attn_beta, grad_ssm_beta = mix_pull(grad_hidden1)
    attn_grad_low = grad_attn_proj.astype(jnp.bfloat16)
    ssm_grad_low = grad_ssm_proj_out.astype(jnp.bfloat16)
    grad_gated = jnp.dot(ssm_grad_low, ssm_down.T, preferred_element_type=jnp.float32).astype(
        jnp.bfloat16
    )
    out_grad = (
        lax.dot_general(
            out_weight, attn_grad_low, (((0,), (1,)), ((), ())), preferred_element_type=jnp.float32
        )
        .astype(jnp.bfloat16)
        .reshape(GROUPS, per_group, HEAD, row_count)
    )
    grad_queries, kv_terms = attend_back(
        steps, queries, kv_all, first[None, :], attn_full, log_sum, out_grad, half
    )
    def complete(keep, sent, late):
        return keep + after(sent, late).astype(jnp.float32)

    grad_kv = sum_half(kv_terms, 2, half, 1)
    grad_gate_up = complete(gate_keep, gate_sent, grad_queries)
    grad_ffn_down = sum(after(sent, grad_queries).astype(jnp.float32) for sent in down_sent)
    grad_kv = after(grad_kv, (grad_gate_up, grad_ffn_down))
    qkv_grad = jnp.concatenate(
        [grad_queries.reshape(model_width, row_count).T, grad_kv.astype(jnp.bfloat16)], 1
    )
    gated_columns = swapped([gated], half, groups, grad_kv)[0]
    attn_columns = swapped([jnp.concatenate([qkv_grad, attended], 1)], half, groups)[0]
    normed_rows = gathered(normed, groups)
    attn_grad_rows = gathered(attn_grad_low, groups)
    ssm_grad_rows = gathered(ssm_grad_low, groups)
    attn_terms = []
    for k in range(2):
        block = attn_columns[k]
        width = block.shape[1]
        column = (k * half + place) * width + jnp.arange(width, dtype=jnp.int32)
        attn_terms.append(
            jnp.where(
                (column < qkv_cols)[:, None],
                jnp.dot(block.T, normed_rows, preferred_element_type=jnp.float32),
                jnp.dot(block.T, attn_grad_rows, preferred_element_type=jnp.float32),
            )
        )
    held_grads = lax.all_gather(held_grad(ssm_proj, grad_gated, carry_weight, c_proj), "seq")
    later_grad = jnp.sum(per_channel(weight_after) * held_grads.astype(jnp.float32), axis=0)
    grad_decay_all = jnp.sum((later_grad * held_in).reshape(STATE, sheads, SHEAD), axis=(0, 2))
    grad_all = jnp.pad((grad_decay_all * decay_all[0])[None, :], ((0, 0), (0, 128 - sheads)))
    conv_grad, z_grad, end_rows, grad_tail, grad_b, grad_c, grad_raw, grad_conv, grad_heads = (
        ssm_back(
            ssm_proj,
            tail_x,
            conv_weight,
            place_in_item,
            grad_gated,
            scanned,
            b_proj,
            c_proj,
            cum,
            cum_t,
            step_size,
            raw,
            rate,
            skip_gain[None, :],
            last_weight,
            carry_weight,
            same_item,
            held_in,
            later_grad,
            grad_all,
        )
    )
    grad_step_bias, grad_decay, grad_skip = grad_heads[0], grad_heads[1], grad_heads[2]
    out_sum = summed_rows(after(out_terms, grad_raw), groups)
    tail_back = from_behind(grad_tail[8 - CONV + 1 :].astype(jnp.bfloat16), "seq", -1)
    end_rows = end_rows[8 - CONV + 1 :] + tail_back.astype(jnp.float32)
    grad_select_in = jnp.concatenate([grad_b, grad_c, grad_raw], 1).astype(jnp.bfloat16)
    attn_keep, attn_sent, attn_send = exchanged(
        attn_terms[0], attn_terms[1], side, half, tail_back
    )
    ssm_down_keep, ssm_down_sent, ssm_down_send = exchanged(
        jnp.dot(gated_columns[0].T, ssm_grad_rows, preferred_element_type=jnp.float32),
        jnp.dot(gated_columns[1].T, ssm_grad_rows, preferred_element_type=jnp.float32),
        side,
        half,
        tail_back,
    )
    conv_grad = jnp.concatenate(
        [conv_grad[: row_count - CONV + 1], end_rows.astype(jnp.bfloat16)], 0
    )
    proj_grad = jnp.concatenate([conv_grad, z_grad], 1)
    proj_grad = after(proj_grad, attn_send)
    ssm_columns = swapped([proj_grad], half, groups)[0]
    grad_normed = jnp.dot(qkv_grad, attn_weight[:, :qkv_cols].T, preferred_element_type=jnp.float32)
    grad_normed = grad_normed + jnp.dot(proj_grad, ssm_weight.T, preferred_element_type=jnp.float32)
    grad_normed = grad_normed + jnp.dot(
        grad_select_in, select_weight.T, preferred_element_type=jnp.float32
    )
    ssm_keep, ssm_sent, ssm_send = exchanged(
        jnp.dot(ssm_columns[0].T, normed_rows, preferred_element_type=jnp.float32),
        jnp.dot(ssm_columns[1].T, normed_rows, preferred_element_type=jnp.float32),
        side,
        half,
    )
    grad_select = jnp.dot(grad_select_in.T, normed, preferred_element_type=jnp.float32)
    mixer_norm_pull = jax.vjp(scaled_norm, layer_in, mixer_gain)[1]
    grad_from_mixer, grad_mixer_gain = mixer_norm_pull(grad_normed)
    grad_layer_in = grad_hidden1 + grad_from_mixer
    grad_tokens = jnp.where(is_meta, 0.0, grad_layer_in).astype(jnp.bfloat16)
    grad_meta = jnp.dot(one_hot.T, jnp.where(is_meta, grad_layer_in, 0.0), precision=highest)
    pieces = [
        grad_meta,
        grad_select,
        grad_conv.reshape(-1, model_width),
        jnp.stack([grad_mixer_gain, grad_attn_beta, grad_ssm_beta, grad_ffn_gain]),
        jnp.pad(
            jnp.concatenate([grad_step_bias, grad_decay, grad_skip])[None, :],
            ((0, 0), (0, model_width - 3 * sheads)),
        ),
    ]
    counts = [piece.shape[0] for piece in pieces]
    share = -(-sum(counts) // (8 * devices)) * 8
    packed = jnp.concatenate(
        pieces + [jnp.zeros((share * devices - sum(counts), model_width), jnp.float32)], 0
    )
    packed = after(
        packed, (attn_send, ssm_down_send, ssm_send)
    )
    packed = total_of(packed.reshape(devices, share, model_width), devices, 4)
    packed = packed.reshape(devices * share, model_width)
    at = [sum(counts[:i]) for i in range(len(counts))]
    gains = packed[at[3] : at[4]]
    little = packed[at[4]]
    small = (
        packed[: counts[0]],
        gains[0],
        packed[at[1] : at[2]].T,
        packed[at[2] : at[3]].reshape(grad_conv.shape),
        little[:sheads],
        little[sheads : 2 * sheads],
        little[2 * sheads : 3 * sheads],
        gains[1],
        gains[2],
        gains[3],
    )
    grad_ssm = complete(ssm_keep, ssm_sent, little)
    late = grad_ssm[0]
    layer_out = (hidden1 + after(out_sum, late).astype(jnp.float32)).astype(jnp.bfloat16)
    shares = (
        complete(attn_keep, attn_sent, late).T,
        grad_ssm.T,
        complete(ssm_down_keep, ssm_down_sent, late),
        grad_gate_up.T,
        grad_ffn_down,
    )
    return (
        layer_out,
        grad_tokens,
        small[0],
        small[1],
        shares[0],
        shares[1],
        small[2],
        small[3],
        small[4],
        small[5],
        small[6],
        shares[2],
        small[7],
        small[8],
        small[9],
        shares[3],
        shares[4],
    )


def solution(mesh):
    placed = (
        P("seq", None),
        P("seq"),
        P("seq"),
        P(),
        P(),
        P(),
        P(),
        P(),
        P(),
        P(),
        P(),
        P(),
        P(),
        P(),
        P(),
        P(),
        P(),
        P(),
        P("seq", None),
    )
    return jax.shard_map(
        per_device,
        mesh=mesh,
        in_specs=placed,
        out_specs=(
            P("seq", None),
            P("seq", None),
            P(),
            P(),
            P(None, "seq"),
            P(None, "seq"),
            P(),
            P(),
            P(),
            P(),
            P(),
            P("seq", None),
            P(),
            P(),
            P(),
            P(None, "seq"),
            P("seq", None),
        ),
        check_vma=False,
    )
```

```python
from functools import partial
import math

import jax
import jax.numpy as jnp
from jax import lax
from jax.experimental import pallas as pl
from jax.experimental.pallas import tpu as pltpu
from jax.sharding import PartitionSpec as P

HEADS = 25
GROUPS = 5
HEAD = 64
INNER = 3200
STATE = 16
CONV = 4
FF = 5504
META = 128
SHEAD = 64


eps = 1e-05
highest = lax.Precision.HIGHEST


MESH = pl.DeviceIdType.MESH
MIB = 2**20


def cost(microseconds):
    return pl.CostEstimate(
        flops=0, transcendentals=0, bytes_accessed=int(microseconds * 3_000_000)
    )


def flipped(v, k):
    bit = 1 << k
    return jnp.where(lax.rem(v // bit, 2) == 0, v + bit, v - bit)


def flips_of(v, bits):
    out = [v]
    for k in bits:
        out = out + [flipped(o, k) for o in out]
    return out


def thirds(rows):
    most = (rows // 3 + 15) // 16 * 16
    return [(0, most), (most, most), (2 * most, rows - 2 * most)]


def parts_of(rows):
    return [part for part in thirds(rows) if part[1] > 0] if rows >= 48 else [(0, rows)]


def greet(partners):
    barrier = pltpu.get_barrier_semaphore()
    for partner in partners:
        pl.semaphore_signal(barrier, inc=1, device_id=(partner,), device_id_type=MESH)
    pl.semaphore_wait(barrier, len(partners))


def remote(src, dst, send, recv, device):
    return pltpu.make_async_remote_copy(
        src_ref=src,
        dst_ref=dst,
        send_sem=send,
        recv_sem=recv,
        device_id=(device,),
        device_id_type=MESH,
    )


def gather_kernel(arrays, half, *refs):
    ins, out = refs[:arrays], refs[arrays]
    send, recv, core_send, core_recv, local_sem = refs[arrays + 1 :]
    me = lax.axis_index("seq")
    place = lax.rem(me, half)
    bits = half.bit_length() - 1
    greet([flipped(me, k) for k in range(bits)])
    parts = thirds(ins[0].shape[0])
    links = bits - 1
    orders = [[1 + (c + s) % links for s in range(links)] for c in range(3)]
    local = [
        pltpu.make_async_copy(ins[a], out.at[a * half + place], local_sem.at[a])
        for a in range(arrays)
    ]
    for copy in local:
        copy.start()
    sent, handed = [], []
    for step in range(links + 1):
        arriving = []
        for c, (first, count) in enumerate(parts):
            rows = pl.ds(first, count)
            held = flips_of(place, orders[c][:step])
            for a in range(arrays):
                if step < links:
                    for i, b in enumerate(held):
                        place_at = out.at[a * half + b, rows]
                        at = (1 << step) - 1 + i
                        copy = remote(
                            ins[a].at[rows] if i == 0 else place_at,
                            place_at,
                            send.at[a, c, at],
                            recv.at[a, c, at],
                            flipped(me, orders[c][step]),
                        )
                        copy.start()
                        arriving.append(copy)
                new = held if step == 0 else held[len(held) // 2 :]
                for i, b in enumerate(new):
                    place_at = out.at[a * half + b, rows]
                    at = 0 if step == 0 else (1 << (step - 1)) + i
                    copy = remote(
                        ins[a].at[rows] if step == 0 else place_at,
                        place_at,
                        core_send.at[a, c, at],
                        core_recv.at[a, c, at],
                        flipped(me, 0),
                    )
                    copy.start()
                    handed.append(copy)
        for copy in arriving:
            copy.wait_recv()
        sent += arriving
    for copy in sent:
        copy.wait_send()
    for copy in handed:
        copy.wait()
    for copy in local:
        copy.wait()


def gather_half(arrays, half, collective_id):
    count = len(arrays)
    shape = arrays[0].shape
    semaphores = pltpu.SemaphoreType.DMA((count, 3, half // 2))
    return pl.pallas_call(
        partial(gather_kernel, count, half),
        out_shape=jax.ShapeDtypeStruct((count * half,) + shape, arrays[0].dtype),
        in_specs=[pl.BlockSpec(memory_space=pl.ANY)] * count,
        out_specs=pl.BlockSpec(memory_space=pl.ANY),
        scratch_shapes=[semaphores] * 4 + [pltpu.SemaphoreType.DMA((count,))],
        compiler_params=pltpu.CompilerParams(collective_id=collective_id, has_side_effects=True),
        cost_estimate=cost(40),
        name="gather_half",
    )(*arrays)


def gather_both_kernel(arrays, half, *refs):
    ins, outs = refs[:arrays], refs[arrays : 2 * arrays]
    send, recv, core_send, core_recv, flip_send, flip_recv, local_sem = refs[2 * arrays :]
    me = lax.axis_index("seq")
    place = lax.rem(me, half)
    twin = jnp.where(me < half, me + half, me - half)
    bits = half.bit_length() - 1
    greet([flipped(me, k) for k in range(bits)] + [twin])
    links = bits - 1
    orders = [[1 + (c + s) % links for s in range(links)] for c in range(3)]
    parts = [parts_of(ref.shape[0]) for ref in ins]
    local, sent, handed, twins = [], [], [], []
    for a in range(arrays):
        copy = remote(ins[a], outs[a].at[place], flip_send.at[a], flip_recv.at[a], twin)
        copy.start()
        twins.append(copy)
        copy = pltpu.make_async_copy(ins[a], outs[a].at[half + place], local_sem.at[a])
        copy.start()
        local.append(copy)
    for time in range(links + 2):
        arriving = []
        for own in (1, 0):
            step = time - (1 - own)
            if step < 0 or step > links:
                continue
            for a in range(arrays):
                for c, (first, count) in enumerate(parts[a]):
                    rows = pl.ds(first, count)
                    slot = own * arrays + a
                    held = flips_of(place, orders[c][:step])
                    if step < links:
                        for i, b in enumerate(held):
                            place_at = outs[a].at[own * half + b, rows]
                            at = (1 << step) - 1 + i
                            copy = remote(
                                ins[a].at[rows] if i == 0 and own else place_at,
                                place_at,
                                send.at[slot, c, at],
                                recv.at[slot, c, at],
                                flipped(me, orders[c][step]),
                            )
                            copy.start()
                            arriving.append(copy)
                    new = held if step == 0 else held[len(held) // 2 :]
                    for i, b in enumerate(new):
                        place_at = outs[a].at[own * half + b, rows]
                        at = 0 if step == 0 else (1 << (step - 1)) + i
                        copy = remote(
                            ins[a].at[rows] if step == 0 and own else place_at,
                            place_at,
                            core_send.at[slot, c, at],
                            core_recv.at[slot, c, at],
                            flipped(me, 0),
                        )
                        copy.start()
                        handed.append(copy)
        if time == 0:
            for copy in twins:
                copy.wait_recv()
        for copy in arriving:
            copy.wait_recv()
        sent += arriving
    for copy in sent + twins:
        copy.wait_send()
    for copy in handed:
        copy.wait()
    for copy in local:
        copy.wait()


def gather_both(arrays, half, collective_id):
    count = len(arrays)
    semaphores = pltpu.SemaphoreType.DMA((2 * count, 3, half // 2))
    single = pltpu.SemaphoreType.DMA((count,))
    return pl.pallas_call(
        partial(gather_both_kernel, count, half),
        out_shape=[jax.ShapeDtypeStruct((2 * half,) + a.shape, a.dtype) for a in arrays],
        in_specs=[pl.BlockSpec(memory_space=pl.ANY)] * count,
        out_specs=[pl.BlockSpec(memory_space=pl.ANY)] * count,
        scratch_shapes=[semaphores] * 4 + [single] * 3,
        compiler_params=pltpu.CompilerParams(collective_id=collective_id, has_side_effects=True),
        cost_estimate=cost(50),
        name="gather_both",
    )(*arrays)


def total_kernel(devices, terms, out, mine, core_in, link_in, send, recv, send_back, recv_back):
    me = lax.axis_index("seq")
    bits = devices.bit_length() - 1
    greet([flipped(me, k) for k in range(bits)])
    pairs = devices // 2
    columns = terms.shape[2]
    third = columns // 3 // 128 * 128
    parts = [(0, third), (third, third), (2 * third, columns - 2 * third)]
    turned = min(3, bits - 1)
    orders = [
        [1 + (c + s) % turned for s in range(turned)] + list(range(1 + turned, bits))
        for c in range(3)
    ]
    everything = pl.ds(0, columns)
    copies = []
    first = []
    for i in range(pairs):
        block = 2 * i + 1 - lax.rem(me, 2)
        copy = remote(
            terms.at[block], core_in.at[i], send.at[0, i], recv.at[0, i], flipped(me, 0)
        )
        copy.start()
        first.append(copy)
    copies += first
    for i in range(pairs):
        first[i].wait_recv()
        mine[i] = terms[2 * i + lax.rem(me, 2)] + core_in[i]
    for step in range(bits - 1):
        arriving = []
        for c, (start, count) in enumerate(parts):
            lanes = pl.ds(start, count)
            for i, b in enumerate(flips_of(me, orders[c][step + 1 :])):
                away = flipped(b, orders[c][step])
                at = pairs - (pairs >> step) + i
                copy = remote(
                    mine.at[away // 2, :, lanes],
                    link_in.at[at, :, lanes],
                    send.at[1 + c, at],
                    recv.at[1 + c, at],
                    flipped(me, orders[c][step]),
                )
                copy.start()
                arriving.append((copy, b, at, lanes))
        for copy, b, at, lanes in arriving:
            copy.wait_recv()
            mine[b // 2, :, lanes] = mine[b // 2, :, lanes] + link_in[at, :, lanes]
            copies.append(copy)
    out[me] = mine[me // 2]
    for step in range(bits - 1):
        arriving = []
        for c, (start, count) in enumerate(parts):
            lanes = pl.ds(start, count)
            order = orders[c][::-1]
            for i, b in enumerate(flips_of(me, order[:step])):
                at = (1 << step) - 1 + i
                copy = remote(
                    out.at[b, :, lanes],
                    out.at[b, :, lanes],
                    send_back.at[1 + c, at],
                    recv_back.at[1 + c, at],
                    flipped(me, order[step]),
                )
                copy.start()
                arriving.append(copy)
        for copy in arriving:
            copy.wait_recv()
        copies += arriving
    last = []
    for i, b in enumerate(flips_of(me, range(1, bits))):
        copy = remote(
            out.at[b], out.at[b], send_back.at[0, i], recv_back.at[0, i], flipped(me, 0)
        )
        copy.start()
        last.append(copy)
    for copy in last:
        copy.wait()
    for copy in copies:
        copy.wait_send()


def total_of(terms, devices, collective_id):
    pairs = devices // 2
    half_shape = (pairs,) + terms.shape[1:]
    semaphores = pltpu.SemaphoreType.DMA((4, pairs))
    return pl.pallas_call(
        partial(total_kernel, devices),
        out_shape=jax.ShapeDtypeStruct(terms.shape, terms.dtype),
        in_specs=[pl.BlockSpec(memory_space=pltpu.VMEM)],
        out_specs=pl.BlockSpec(memory_space=pltpu.VMEM),
        scratch_shapes=[pltpu.VMEM(half_shape, terms.dtype)] * 3 + [semaphores] * 4,
        compiler_params=pltpu.CompilerParams(
            collective_id=collective_id, has_side_effects=True, vmem_limit_bytes=48 * MIB
        ),
        cost_estimate=cost(40),
        name="total_of",
    )(terms)


def sum_kernel(arrays, half, *refs):
    terms, out = refs[:2]
    mine, core_in, link_in, load_sem, send, recv, core_send, core_recv, flip_in, flip_sem = refs[2:]
    me = lax.axis_index("seq")
    place = lax.rem(me, half)
    bits = half.bit_length() - 1
    twin = jnp.where(me < half, me + half, me - half)
    greet([flipped(me, k) for k in range(bits)] + ([twin] if arrays == 2 else []))
    parts = thirds(terms.shape[1])
    links = bits - 1
    orders = [[1 + (c + s) % links for s in range(links)] for c in range(3)]
    loads = []
    pairs = half // 2
    for a in range(arrays):
        for i in range(pairs):
            block = 2 * i + lax.rem(place, 2)
            copy = pltpu.make_async_copy(
                terms.at[a * half + block], mine.at[a, i], load_sem.at[a, i]
            )
            copy.start()
            loads.append(copy)
    handed = {}
    for wanted in range(2):
        for c, (first, count) in enumerate(parts):
            rows = pl.ds(first, count)
            kept = flips_of(place, orders[c][1:])
            blocks = kept if wanted else [flipped(b, orders[c][0]) for b in kept]
            for a in range(arrays):
                for i, b in enumerate(blocks):
                    at = wanted * (pairs // 2) + i
                    copy = remote(
                        terms.at[a * half + flipped(b, 0), rows],
                        core_in.at[a, at, rows],
                        core_send.at[a, c, at],
                        core_recv.at[a, c, at],
                        flipped(me, 0),
                    )
                    copy.start()
                    handed[a, c, at] = copy
    for copy in loads:
        copy.wait()
    sent = []
    arriving = {}

    def add(ref, slot, rows, other):
        ref[slot, rows] = (
            ref[slot, rows].astype(jnp.float32) + other[...].astype(jnp.float32)
        ).astype(ref.dtype)

    for step in range(links):
        for c, (first, count) in enumerate(parts):
            rows = pl.ds(first, count)
            kept = flips_of(place, orders[c][step + 1 :])
            for a in range(arrays):
                for i, b in enumerate(kept):
                    out_block = flipped(b, orders[c][step])
                    if step == 0:
                        handed[a, c, i].wait_recv()
                        add(mine.at[a], out_block // 2, rows, core_in.at[a, i, rows])
                    at = pairs - (pairs >> step) + i
                    copy = remote(
                        mine.at[a, out_block // 2, rows],
                        link_in.at[a, at, rows],
                        send.at[a, c, at],
                        recv.at[a, c, at],
                        flipped(me, orders[c][step]),
                    )
                    copy.start()
                    arriving[a, c, at] = copy
                    sent.append(copy)
        if step == 0:
            for c, (first, count) in enumerate(parts):
                rows = pl.ds(first, count)
                for a in range(arrays):
                    for i, b in enumerate(flips_of(place, orders[c][1:])):
                        at = pairs // 2 + i
                        handed[a, c, at].wait_recv()
                        add(mine.at[a], b // 2, rows, core_in.at[a, at, rows])
        for c, (first, count) in enumerate(parts):
            rows = pl.ds(first, count)
            kept = flips_of(place, orders[c][step + 1 :])
            for a in range(arrays):
                for i, b in enumerate(kept):
                    at = pairs - (pairs >> step) + i
                    arriving[a, c, at].wait_recv()
                    add(mine.at[a], b // 2, rows, link_in.at[a, at, rows])
    if arrays == 2:
        flip = remote(mine.at[0, place // 2], flip_in, flip_sem.at[0], flip_sem.at[1], twin)
        flip.start()
        flip.wait_recv()
        out[...] = mine[1, place // 2].astype(jnp.float32) + flip_in[...].astype(jnp.float32)
        sent.append(flip)
    else:
        out[...] = mine[0, place // 2].astype(jnp.float32)
    for copy in sent:
        copy.wait_send()
    for copy in handed.values():
        copy.wait_send()


def sum_half(terms, arrays, half, collective_id):
    rows, columns = terms.shape[1:]
    pairs = half // 2
    block = (rows, columns)
    semaphores = pltpu.SemaphoreType.DMA((arrays, 3, pairs))
    return pl.pallas_call(
        partial(sum_kernel, arrays, half),
        out_shape=jax.ShapeDtypeStruct(block, jnp.float32),
        in_specs=[pl.BlockSpec(memory_space=pl.ANY)],
        out_specs=pl.BlockSpec(memory_space=pltpu.VMEM),
        scratch_shapes=[
            pltpu.VMEM((arrays, pairs) + block, terms.dtype),
            pltpu.VMEM((arrays, pairs) + block, terms.dtype),
            pltpu.VMEM((arrays, pairs) + block, terms.dtype),
            pltpu.SemaphoreType.DMA((arrays, pairs)),
        ]
        + [semaphores] * 4
        + [
            pltpu.VMEM(block if arrays == 2 else (16, 128), terms.dtype),
            pltpu.SemaphoreType.DMA((2,)),
        ],
        compiler_params=pltpu.CompilerParams(
            collective_id=collective_id, has_side_effects=True, vmem_limit_bytes=60 * MIB
        ),
        cost_estimate=cost(50),
        name="sum_half",
    )(terms)


def ffn_kernel(x_ref, cot_ref, in_ref, down_ref, out_ref, grad_in_ref, grad_w_ref, grad_d_ref):
    wide = down_ref.shape[0]
    x, cot = x_ref[...], cot_ref[...]
    low = jnp.bfloat16

    def dot(a, b, contract):
        return lax.dot_general(a, b, (contract, ((), ())), preferred_element_type=jnp.float32)

    vals = dot(x, in_ref[...], ((1,), (0,)))
    gate, up = vals[:, :wide], vals[:, wide:]
    sigma = jax.nn.sigmoid(gate)
    act = gate * sigma
    hidden = (act * up).astype(low)
    out_ref[...] = dot(hidden, down_ref[...], ((1,), (0,))).astype(low)
    grad_hidden = dot(cot, down_ref[...], ((1,), (1,))).astype(low).astype(jnp.float32)
    slope = sigma * (1.0 + gate * (1.0 - sigma))
    grads = jnp.concatenate([grad_hidden * up * slope, grad_hidden * act], 1).astype(low)
    grad_in_ref[...] = dot(grads, in_ref[...], ((1,), (1,))).astype(low)

    @pl.when(pl.program_id(0) == 0)
    def _():
        grad_w_ref[...] = jnp.zeros_like(grad_w_ref)
        grad_d_ref[...] = jnp.zeros_like(grad_d_ref)

    grad_w_ref[...] += dot(grads, x, ((0,), (0,)))
    grad_d_ref[...] += dot(hidden, cot, ((0,), (0,)))


def ffn(x, cot, in_weight, down_weight):
    rows, model = x.shape
    block = min(256, rows)
    wide = down_weight.shape[0]
    moving = pl.BlockSpec((block, model), lambda i: (i, 0))
    fixed = lambda shape: pl.BlockSpec(shape, lambda i: (0, 0))
    return pl.pallas_call(
        ffn_kernel,
        grid=(rows // block,),
        out_shape=[
            jax.ShapeDtypeStruct(x.shape, jnp.bfloat16),
            jax.ShapeDtypeStruct(x.shape, jnp.bfloat16),
            jax.ShapeDtypeStruct((2 * wide, model), jnp.float32),
            jax.ShapeDtypeStruct((wide, model), jnp.float32),
        ],
        in_specs=[moving, moving, fixed(in_weight.shape), fixed(down_weight.shape)],
        out_specs=[moving, moving, fixed((2 * wide, model)), fixed((wide, model))],
        compiler_params=pltpu.CompilerParams(vmem_limit_bytes=56 * MIB),
        cost_estimate=cost(35),
        name="ffn",
    )(x, cot, in_weight, down_weight)


def masked_block(at, first_ref, device_index, rows):
    key = lax.broadcasted_iota(jnp.int32, (rows, rows), 0) + at * rows
    query = lax.broadcasted_iota(jnp.int32, (rows, rows), 1) + device_index * rows
    seen = ((key >= first_ref[...]) & (key <= query)).astype(jnp.float32)
    return jnp.concatenate([seen] * (HEADS // GROUPS), 1) > 0.0


def side_by_side(ref, g):
    return jnp.concatenate([ref[g, j] for j in range(HEADS // GROUPS)], 1)


def over_shards(steps_ref, body):
    body(0)

    @pl.loop(1, steps_ref[1] + 1)
    def _(hop):
        body(hop)


def attend_kernel(half, steps_ref, q_ref, kv_ref, first_ref, out_ref, log_ref, top, total, acc):
    device_index, newest = steps_ref[0], half + lax.rem(steps_ref[0], half)
    rows = kv_ref.shape[1]
    top[...] = jnp.full_like(top, -1e30)
    total[...] = jnp.zeros_like(total)
    acc[...] = jnp.zeros_like(acc)

    def body(hop):
        block = kv_ref[newest - hop]
        seen = masked_block(device_index - hop, first_ref, device_index, rows)
        for g in range(GROUPS):
            keys = block[:, g * HEAD : (g + 1) * HEAD]
            values = block[:, (GROUPS + g) * HEAD : (GROUPS + g + 1) * HEAD]
            scores = jnp.dot(keys, side_by_side(q_ref, g), preferred_element_type=jnp.float32)
            scores = jnp.where(seen, scores, -1e30)
            now = jnp.maximum(top[g], jnp.max(scores, axis=0, keepdims=True))
            probs = jnp.exp(scores - now)
            fade = jnp.exp(top[g] - now)
            top[g] = now
            total[g] = total[g] * fade + jnp.sum(probs, axis=0, keepdims=True)
            acc[g] = acc[g] * fade + lax.dot_general(
                values,
                probs.astype(jnp.bfloat16),
                (((0,), (0,)), ((), ())),
                preferred_element_type=jnp.float32,
            )

    over_shards(steps_ref, body)
    for g in range(GROUPS):
        done = acc[g] / total[g]
        for j in range(HEADS // GROUPS):
            out_ref[g, j] = done[:, j * rows : (j + 1) * rows]
        log_ref[g] = top[g] + jnp.log(total[g])


def attend(steps, queries, kv, first, half):
    rows = kv.shape[1]
    per_group = HEADS // GROUPS
    wide = per_group * rows
    return pl.pallas_call(
        partial(attend_kernel, half),
        out_shape=[
            jax.ShapeDtypeStruct((GROUPS, per_group, HEAD, rows), jnp.float32),
            jax.ShapeDtypeStruct((GROUPS, 1, wide), jnp.float32),
        ],
        in_specs=[pl.BlockSpec(memory_space=pltpu.SMEM)]
        + [pl.BlockSpec(memory_space=pltpu.VMEM)] * 3,
        out_specs=[pl.BlockSpec(memory_space=pltpu.VMEM)] * 2,
        scratch_shapes=[
            pltpu.VMEM((GROUPS, 1, wide), jnp.float32),
            pltpu.VMEM((GROUPS, 1, wide), jnp.float32),
            pltpu.VMEM((GROUPS, HEAD, wide), jnp.float32),
        ],
        compiler_params=pltpu.CompilerParams(vmem_limit_bytes=56 * MIB),
        cost_estimate=cost(15),
        name="attend",
    )(steps, queries, kv, first)


def attend_back_kernel(
    half,
    steps_ref,
    q_ref,
    kv_ref,
    first_ref,
    out_ref,
    log_ref,
    grad_ref,
    grad_q_ref,
    grad_kv_ref,
    dots,
    acc,
):
    device_index, newest = steps_ref[0], half + lax.rem(steps_ref[0], half)
    rows = kv_ref.shape[1]
    contract = lambda a, b, i: lax.dot_general(
        a, b, (((i,), (i,)), ((), ())), preferred_element_type=jnp.float32
    )
    for g in range(GROUPS):
        product = side_by_side(out_ref, g) * side_by_side(grad_ref, g).astype(jnp.float32)
        dots[g] = jnp.sum(product, axis=0, keepdims=True)
    acc[...] = jnp.zeros_like(acc)

    @pl.loop(0, 2 * half)
    def _(i):
        grad_kv_ref[i] = jnp.zeros(grad_kv_ref.shape[1:], grad_kv_ref.dtype)

    def body(hop):
        block = kv_ref[newest - hop]
        seen = masked_block(device_index - hop, first_ref, device_index, rows)
        grad_keys, grad_values = [], []
        for g in range(GROUPS):
            keys = block[:, g * HEAD : (g + 1) * HEAD]
            values = block[:, (GROUPS + g) * HEAD : (GROUPS + g + 1) * HEAD]
            queries, grads = side_by_side(q_ref, g), side_by_side(grad_ref, g)
            scores = jnp.dot(keys, queries, preferred_element_type=jnp.float32)
            probs = jnp.where(seen, jnp.exp(scores - log_ref[g]), 0.0)
            grad_probs = jnp.dot(values, grads, preferred_element_type=jnp.float32)
            grad_values.append(contract(probs.astype(jnp.bfloat16), grads, 1))
            grad_scores = (probs * (grad_probs - dots[g])).astype(jnp.bfloat16)
            grad_keys.append(contract(grad_scores, queries, 1))
            acc[g] += contract(keys, grad_scores, 0)
        grad_kv_ref[newest - hop] = jnp.concatenate(grad_keys + grad_values, 1).astype(
            grad_kv_ref.dtype
        )

    over_shards(steps_ref, body)
    for g in range(GROUPS):
        for j in range(HEADS // GROUPS):
            grad_q_ref[g, j] = (acc[g, :, j * rows : (j + 1) * rows] * (HEAD**-0.5)).astype(
                grad_q_ref.dtype
            )


def attend_back(steps, queries, kv, first, out, log_sum, grads, half):
    rows = kv.shape[1]
    wide = HEADS // GROUPS * rows
    return pl.pallas_call(
        partial(attend_back_kernel, half),
        out_shape=[
            jax.ShapeDtypeStruct(queries.shape, jnp.bfloat16),
            jax.ShapeDtypeStruct(kv.shape, jnp.bfloat16),
        ],
        in_specs=[pl.BlockSpec(memory_space=pltpu.SMEM)]
        + [pl.BlockSpec(memory_space=pltpu.VMEM)] * 6,
        out_specs=[pl.BlockSpec(memory_space=pltpu.VMEM)] * 2,
        scratch_shapes=[
            pltpu.VMEM((GROUPS, 1, wide), jnp.float32),
            pltpu.VMEM((GROUPS, HEAD, wide), jnp.float32),
        ],
        compiler_params=pltpu.CompilerParams(vmem_limit_bytes=60 * MIB),
        cost_estimate=cost(20),
        name="attend_back",
    )(steps, queries, kv, first, out, log_sum, grads)


def spread_heads(ref, tile, rows):
    first_half = lax.broadcasted_iota(jnp.int32, (rows, 128), 1) < SHEAD
    return jnp.where(
        first_half, ref[:, 2 * tile : 2 * tile + 1], ref[:, 2 * tile + 1 : 2 * tile + 2]
    )


def conv_tile(proj_ref, tail_ref, taps_ref, place, extended, at, rows):
    extended[8 : 8 + rows] = proj_ref[:, at]
    extended[0:8] = tail_ref[:, at]
    lagged = []
    summed = jnp.zeros((rows, 128), jnp.float32)
    for lag in range(taps_ref.shape[0]):
        moved = extended[8 - lag : 8 - lag + rows]
        moved = moved if lag == 0 else jnp.where(place >= lag, moved, 0.0)
        lagged.append(moved)
        summed = summed + taps_ref[lag : lag + 1, at] * moved
    return summed, lagged


def ssm_state_kernel(
    proj_ref,
    tail_ref,
    taps_ref,
    place_ref,
    items_ref,
    select_ref,
    bias_ref,
    rate_ref,
    state_ref,
    b_ref,
    c_ref,
    raw_ref,
    step_ref,
    cum_ref,
    cum_t_ref,
    last_ref,
    carry_ref,
    all_ref,
    extended,
):
    rows, inner = proj_ref.shape[0], taps_ref.shape[1]
    heads = step_ref.shape[1]
    low = jnp.bfloat16
    b_ref[...] = select_ref[:, :STATE].astype(low)
    c_ref[...] = select_ref[:, STATE : 2 * STATE].astype(low)
    raw = select_ref[:, 2 * STATE :] + bias_ref[...]
    raw_ref[...] = raw
    step = jnp.maximum(raw, 0.0) + jnp.log1p(jnp.exp(-jnp.abs(raw)))
    step_ref[...] = step
    lower = (
        lax.broadcasted_iota(jnp.int32, (rows, rows), 0)
        >= lax.broadcasted_iota(jnp.int32, (rows, rows), 1)
    ).astype(jnp.float32)
    cum = jnp.dot(
        lower, -step * rate_ref[...], precision=highest, preferred_element_type=jnp.float32
    )
    cum_ref[...] = cum
    wide = jnp.concatenate([cum, jnp.zeros((rows, 128 - heads), jnp.float32)], 1)
    cum_t_ref[...] = wide.T[:heads]
    items = items_ref[...]
    final = items_ref[rows - 1 : rows, :]
    total = cum[rows - 1 : rows, :]
    last_ref[...] = jnp.where(items == final, jnp.exp(total - cum), 0.0)
    carry_ref[...] = jnp.where(items == 0, jnp.exp(cum), 0.0)
    all_ref[...] = jnp.where(final == 0, jnp.exp(total), 0.0)
    place = place_ref[...]
    b = b_ref[...]
    for tile in range(inner // 128):
        at = slice(tile * 128, (tile + 1) * 128)
        summed, _ = conv_tile(proj_ref, tail_ref, taps_ref, place, extended, at, rows)
        x = summed * jax.nn.sigmoid(summed)
        taken = x * spread_heads(step_ref, tile, rows) * spread_heads(last_ref, tile, rows)
        state_ref[:, at] = lax.dot_general(
            b, taken.astype(low), (((0,), (0,)), ((), ())), preferred_element_type=jnp.float32
        ).astype(low)


def whole_call(kernel, operands, outs, scratch, microseconds, name):
    return pl.pallas_call(
        kernel,
        out_shape=[jax.ShapeDtypeStruct(dims, kind) for dims, kind in outs],
        in_specs=[pl.BlockSpec(memory_space=pltpu.VMEM)] * len(operands),
        out_specs=[pl.BlockSpec(memory_space=pltpu.VMEM)] * len(outs),
        scratch_shapes=scratch,
        compiler_params=pltpu.CompilerParams(vmem_limit_bytes=48 * MIB),
        cost_estimate=cost(microseconds),
        name=name,
    )(*operands)


def ssm_state(proj, tail, taps, place, items, select, bias, rate):
    rows, inner, heads = proj.shape[0], taps.shape[1], bias.shape[1]
    low, full = jnp.bfloat16, jnp.float32
    by_head = ((rows, heads), full)
    outs = [((STATE, inner), low), ((rows, STATE), low), ((rows, STATE), low)]
    outs += [by_head, by_head, by_head, ((heads, rows), full), by_head, by_head]
    outs += [((1, heads), full)]
    operands = (proj, tail, taps, place, items, select, bias, rate)
    scratch = [pltpu.VMEM((rows + 8, 128), full)]
    return whole_call(ssm_state_kernel, operands, outs, scratch, 8, "ssm_state")


def ssm_output_kernel(
    proj_ref,
    tail_ref,
    taps_ref,
    place_ref,
    b_ref,
    c_ref,
    cum_ref,
    cum_t_ref,
    step_ref,
    skip_ref,
    carry_ref,
    same_ref,
    held_ref,
    scanned_ref,
    gated_ref,
    extended,
):
    rows, inner = proj_ref.shape[0], taps_ref.shape[1]
    low = jnp.bfloat16
    place, c = place_ref[...], c_ref[...]
    both = lax.dot_general(
        c, b_ref[...], (((1,), (1,)), ((), ())), preferred_element_type=jnp.float32
    )
    same = same_ref[...] > 0.0
    first_half = lax.broadcasted_iota(jnp.int32, (rows, 128), 1) < SHEAD
    for tile in range(inner // 128):
        at = slice(tile * 128, (tile + 1) * 128)
        summed, _ = conv_tile(proj_ref, tail_ref, taps_ref, place, extended, at, rows)
        x = summed * jax.nn.sigmoid(summed)
        scaled = (x * spread_heads(step_ref, tile, rows)).astype(low)
        halves = []
        for k in range(2):
            head = 2 * tile + k
            exponent = jnp.where(
                same, cum_ref[:, head : head + 1] - cum_t_ref[head : head + 1, :], -1e30
            )
            weights = (jnp.exp(exponent) * both).astype(low)
            halves.append(jnp.dot(weights, scaled, preferred_element_type=jnp.float32))
        carried = jnp.dot(c, held_ref[:, at].astype(low), preferred_element_type=jnp.float32)
        out = (
            jnp.where(first_half, halves[0], halves[1])
            + carried * spread_heads(carry_ref, tile, rows)
            + spread_heads(skip_ref, tile, rows) * x
        )
        scanned_ref[:, at] = out
        z = proj_ref[:, inner + tile * 128 : inner + (tile + 1) * 128]
        gated_ref[:, at] = (out * z * jax.nn.sigmoid(z)).astype(low)


def ssm_output(*operands):
    rows, inner = operands[0].shape[0], operands[2].shape[1]
    outs = [((rows, inner), jnp.float32), ((rows, inner), jnp.bfloat16)]
    scratch = [pltpu.VMEM((rows + 8, 128), jnp.float32)]
    return whole_call(ssm_output_kernel, operands, outs, scratch, 8, "ssm_output")


def held_grad_kernel(proj_ref, grad_ref, carry_ref, c_ref, out_ref):
    rows, inner = grad_ref.shape
    for tile in range(inner // 128):
        at = slice(tile * 128, (tile + 1) * 128)
        z = proj_ref[:, inner + tile * 128 : inner + (tile + 1) * 128]
        grad = grad_ref[:, at].astype(jnp.float32) * z * jax.nn.sigmoid(z)
        grad = (grad * spread_heads(carry_ref, tile, rows)).astype(jnp.bfloat16)
        out_ref[:, at] = lax.dot_general(
            c_ref[...], grad, (((0,), (0,)), ((), ())), preferred_element_type=jnp.float32
        ).astype(jnp.bfloat16)


def held_grad(proj, grad, carry, c):
    outs = [((STATE, grad.shape[1]), jnp.bfloat16)]
    return whole_call(held_grad_kernel, (proj, grad, carry, c), outs, [], 4, "held_grad")[0]


def ssm_back_kernel(
    proj_ref,
    tail_ref,
    taps_ref,
    place_ref,
    grad_ref,
    scanned_ref,
    b_ref,
    c_ref,
    cum_ref,
    cum_t_ref,
    step_ref,
    raw_ref,
    rate_ref,
    skip_ref,
    last_ref,
    carry_ref,
    same_ref,
    held_ref,
    later_ref,
    grad_all_ref,
    grad_conv_ref,
    grad_z_ref,
    end_ref,
    grad_tail_ref,
    grad_b_ref,
    grad_c_ref,
    grad_raw_ref,
    grad_taps_ref,
    grad_heads_ref,
    extended,
    sums,
    columns,
):
    rows = b_ref.shape[0]
    inner = taps_ref.shape[1]
    tap_count = taps_ref.shape[0]
    heads = step_ref.shape[1]
    low = jnp.bfloat16

    def dot(a, b, left=1, right=0):
        return lax.dot_general(
            a, b, (((left,), (right,)), ((), ())), preferred_element_type=jnp.float32
        )

    lane = lax.broadcasted_iota(jnp.int32, (rows, 128), 1)
    first_half = lane < SHEAD
    place = place_ref[...]
    b, c = b_ref[...], c_ref[...]
    both = dot(c, b, 1, 1)
    same = same_ref[...] > 0.0
    sums[...] = jnp.zeros_like(sums)
    columns[...] = jnp.zeros_like(columns)
    grad_b = jnp.zeros((rows, STATE), jnp.float32)
    grad_c = jnp.zeros((rows, STATE), jnp.float32)
    grad_both = jnp.zeros((rows, rows), jnp.float32)
    grad_skip = jnp.zeros((1, 128), jnp.float32)
    picker_row = lax.broadcasted_iota(jnp.int32, (128, 128), 0)
    picker_lane = lax.broadcasted_iota(jnp.int32, (128, 128), 1)

    def head_sums(values, tile):
        pick = (picker_lane == 2 * tile + picker_row // SHEAD).astype(low)
        high = values.astype(low)
        rest = (values - high.astype(jnp.float32)).astype(low)
        return dot(high, pick) + dot(rest, pick)

    def spread(ref, tile):
        return jnp.where(
            first_half,
            ref[:, 2 * tile : 2 * tile + 1],
            ref[:, 2 * tile + 1 : 2 * tile + 2],
        )

    for tile in range(inner // 128):
        at = slice(tile * 128, (tile + 1) * 128)
        z_at = slice(inner + tile * 128, inner + (tile + 1) * 128)
        extended[8 : 8 + rows] = proj_ref[:, at]
        extended[0:8] = tail_ref[:, at]
        lagged = []
        summed = jnp.zeros((rows, 128), jnp.float32)
        for lag in range(tap_count):
            moved = extended[8 - lag : 8 - lag + rows]
            moved = moved if lag == 0 else jnp.where(place >= lag, moved, 0.0)
            lagged.append(moved)
            summed = summed + taps_ref[lag : lag + 1, at] * moved
        sigma = jax.nn.sigmoid(summed)
        x = summed * sigma
        step = spread(step_ref, tile)
        scaled = x * step
        z = proj_ref[:, z_at]
        z_sigma = jax.nn.sigmoid(z)
        grad_gated = grad_ref[:, at].astype(jnp.float32)
        grad_y = grad_gated * z * z_sigma
        grad_z_ref[:, at] = (
            grad_gated * scanned_ref[:, at] * (z_sigma * (1.0 + z * (1.0 - z_sigma)))
        ).astype(low)
        held, later = held_ref[:, at].astype(low), later_ref[:, at].astype(low)
        last, carry = spread(last_ref, tile), spread(carry_ref, tile)
        from_later = dot(b, later)
        from_held = dot(c, held)
        grad_b = grad_b + dot((scaled * last).astype(low), later, 1, 1)
        carried_grad = grad_y * carry
        grad_c = grad_c + dot(carried_grad.astype(low), held, 1, 1)
        cum_grad = head_sums(carried_grad * from_held - scaled * last * from_later, tile)
        last_total = head_sums(
            jnp.sum(scaled * last * from_later, axis=0, keepdims=True), tile
        )
        grad_scaled = last * from_later
        grad_skip = grad_skip + head_sums(jnp.sum(grad_y * x, axis=0, keepdims=True), tile)
        grad_low, scaled_low = grad_y.astype(low), scaled.astype(low)
        halves = []
        for k in range(2):
            head = 2 * tile + k
            mine = first_half if k == 0 else ~first_half
            exponent = jnp.where(
                same, cum_ref[:, head : head + 1] - cum_t_ref[head : head + 1, :], -1e30
            )
            fade = jnp.exp(exponent)
            weights = fade * both
            halves.append(dot(weights.astype(low), grad_low, 0, 0))
            grad_weights = dot(jnp.where(mine, grad_y, 0.0).astype(low), scaled_low, 1, 1)
            grad_both = grad_both + grad_weights * fade
            grad_exponent = grad_weights * weights
            columns[head : head + 1, :] = jnp.sum(grad_exponent, axis=0, keepdims=True)
            pick = (picker_lane == head).astype(low)
            high = grad_exponent.astype(low)
            rest = (grad_exponent - high.astype(jnp.float32)).astype(low)
            cum_grad = cum_grad + dot(high, pick) + dot(rest, pick)
        grad_scaled = grad_scaled + jnp.where(first_half, halves[0], halves[1])
        sums[0] += cum_grad
        sums[1] += head_sums(grad_scaled * x, tile)
        sums[2] += last_total
        grad_x = grad_scaled * step + spread(skip_ref, tile) * grad_y
        grad_summed = grad_x * (sigma * (1.0 + summed * (1.0 - sigma)))
        for lag in range(tap_count):
            grad_taps_ref[lag : lag + 1, at] = jnp.sum(
                grad_summed * lagged[lag], axis=0, keepdims=True
            )
        extended[...] = jnp.zeros_like(extended)
        for lag in range(tap_count):
            moved = taps_ref[lag : lag + 1, at] * grad_summed
            moved = moved if lag == 0 else jnp.where(place >= lag, moved, 0.0)
            extended[8 - lag : 8 - lag + rows] += moved
        grad_conv_ref[:, at] = extended[8 : 8 + rows].astype(low)
        end_ref[:, at] = extended[rows : 8 + rows]
        grad_tail_ref[:, at] = extended[0:8]

    grad_c_ref[...] = grad_c + dot(grad_both.astype(low), b)
    grad_b_ref[...] = grad_b + dot(grad_both.astype(low), c, 0, 0)
    row_at = lax.broadcasted_iota(jnp.int32, (rows, 128), 0)
    cum_grad = sums[0] - columns[...].T
    cum_grad = cum_grad + jnp.where(row_at == rows - 1, sums[2] + grad_all_ref[...], 0.0)
    upper = (
        lax.broadcasted_iota(jnp.int32, (rows, rows), 0)
        <= lax.broadcasted_iota(jnp.int32, (rows, rows), 1)
    ).astype(jnp.float32)
    log_grad = jnp.dot(upper, cum_grad, precision=highest, preferred_element_type=jnp.float32)
    log_grad = log_grad[:, :heads]
    rate = rate_ref[...]
    step = step_ref[...]
    raw_grad = (sums[1][:, :heads] - rate * log_grad) * jax.nn.sigmoid(raw_ref[...])
    grad_raw_ref[...] = raw_grad
    grad_heads_ref[0:1, :] = jnp.sum(raw_grad, axis=0, keepdims=True)
    grad_heads_ref[1:2, :] = jnp.sum(-rate * step * log_grad, axis=0, keepdims=True)
    grad_heads_ref[2:3, :] = grad_skip[:, :heads]
    grad_heads_ref[3:8, :] = jnp.zeros((5, heads), jnp.float32)


def ssm_back(*operands):
    proj, taps, b, step = operands[0], operands[2], operands[6], operands[10]
    rows, inner = proj.shape[0], taps.shape[1]
    heads = step.shape[1]
    shape = lambda dims, kind: jax.ShapeDtypeStruct(dims, kind)
    outs = [
        shape((rows, inner), jnp.bfloat16),
        shape((rows, inner), jnp.bfloat16),
        shape((8, inner), jnp.float32),
        shape((8, inner), jnp.float32),
        shape((rows, STATE), jnp.float32),
        shape((rows, STATE), jnp.float32),
        shape((rows, heads), jnp.float32),
        shape(taps.shape, jnp.float32),
        shape((8, heads), jnp.float32),
    ]
    return pl.pallas_call(
        ssm_back_kernel,
        out_shape=outs,
        in_specs=[pl.BlockSpec(memory_space=pltpu.VMEM)] * len(operands),
        out_specs=[pl.BlockSpec(memory_space=pltpu.VMEM)] * len(outs),
        scratch_shapes=[
            pltpu.VMEM((rows + 8, 128), jnp.float32),
            pltpu.VMEM((3, rows, 128), jnp.float32),
            pltpu.VMEM((128, rows), jnp.float32),
        ],
        compiler_params=pltpu.CompilerParams(vmem_limit_bytes=48 * MIB),
        cost_estimate=cost(20),
        name="ssm_back",
    )(*operands)


def from_behind(x, axis, by):
    count = lax.axis_size(axis)
    pairs = [(i, i + by) for i in range(count) if 0 <= i + by < count]
    return lax.ppermute(x, axis, pairs)


def as_sent(x):
    return jax.tree.map(lambda a: a.astype(jnp.bfloat16) if a.dtype == jnp.float32 else a, x)


def gathered(x, groups):
    return lax.all_gather(x, "seq", axis_index_groups=groups, tiled=True)


def summed_rows(x, groups):
    return lax.psum_scatter(x, "seq", scatter_dimension=0, axis_index_groups=groups, tiled=True)


def after(x, late):
    return lax.optimization_barrier((x, late))[0]


def exchanged(first, second, side, half, late=None):
    send = jnp.where(side == 0, second, first).astype(jnp.bfloat16)
    keep = jnp.where(side == 0, first, second)
    if late is not None:
        send = after(send, late)
    pairs = [(d, (d + half) % (2 * half)) for d in range(2 * half)]
    return keep, lax.ppermute(send, "seq", pairs), send


def swapped(arrays, half, groups, late=None):
    widths = [a.shape[1] // (2 * half) for a in arrays]
    rows = arrays[0].shape[0]
    packed = jnp.concatenate([a.reshape(rows, 2, half, -1) for a in arrays], 3)
    packed = jnp.transpose(packed, (2, 0, 1, 3))
    packed = lax.all_to_all(packed, "seq", 0, 0, axis_index_groups=groups, tiled=True)
    if late is not None:
        packed = after(packed, late)
    packed = packed.reshape(half * rows, 2, -1)
    out, at = [], 0
    for width in widths:
        out.append([packed[:, k, at : at + width] for k in range(2)])
        at += width
    return out


def rms_scale(entries):
    return entries * lax.rsqrt(jnp.mean(entries * entries, axis=-1, keepdims=True) + eps)


def scaled_norm(entries, gain):
    return rms_scale(entries) * gain


def branch_mix(attn_proj, ssm_proj_out, attn_beta, ssm_beta):
    return attn_beta * rms_scale(attn_proj) + ssm_beta * rms_scale(ssm_proj_out)


def per_device(
    tokens,
    seg_ids,
    meta_index,
    meta_table,
    mixer_gain,
    attn_weight,
    ssm_weight,
    select_weight,
    conv_weight,
    step_bias,
    decay_log,
    skip_gain,
    ssm_down,
    attn_beta,
    ssm_beta,
    ffn_gain,
    gate_up,
    ffn_down,
    cotangent,
):
    row_count = tokens.shape[0]
    model_width = tokens.shape[1]
    kv_width = GROUPS * HEAD
    per_group = HEADS // GROUPS
    qkv_cols = model_width + 2 * kv_width
    score_scale = 1.0 / math.sqrt(HEAD)
    devices = lax.axis_size("seq")
    device_index = lax.axis_index("seq")
    half = devices // 2
    side, place = device_index // half, device_index % half
    groups = [[h * half + q for q in range(half)] for h in range(2)]
    one_hot = (meta_index[:, None] == jnp.arange(META, dtype=jnp.int32)[None, :]).astype(
        jnp.float32
    )
    is_meta = (meta_index < META)[:, None]
    layer_in = jnp.where(
        is_meta,
        jnp.dot(one_hot.astype(jnp.bfloat16), meta_table, preferred_element_type=jnp.float32),
        tokens.astype(jnp.float32),
    )
    normed = scaled_norm(layer_in, mixer_gain).astype(jnp.bfloat16)
    query_weight = attn_weight[:, :model_width]
    kv_weight = attn_weight[:, model_width:qkv_cols]
    cot_rows = gathered(cotangent, groups)
    kv = jnp.dot(normed, kv_weight, preferred_element_type=jnp.float32).astype(jnp.bfloat16)
    kv = after(kv, cot_rows)
    queries = lax.dot_general(
        query_weight, normed, (((0,), (1,)), ((), ())), preferred_element_type=jnp.float32
    )
    queries = (queries.astype(jnp.bfloat16) * score_scale).reshape(
        GROUPS, per_group, HEAD, row_count
    )
    ssm_proj = jnp.dot(normed, ssm_weight, preferred_element_type=jnp.float32)
    select = jnp.dot(normed, select_weight, preferred_element_type=jnp.float32)
    last_rows = ssm_proj[row_count - CONV + 1 :, :INNER].astype(jnp.bfloat16)
    tail_x = jnp.pad(
        from_behind(last_rows, "seq", 1).astype(jnp.float32), ((8 - CONV + 1, 0), (0, 0))
    )
    row = jnp.arange(row_count, dtype=jnp.int32)
    starts = jnp.where((meta_index == 0)[None, :] & (row[None, :] <= row[:, None]), 1, 0)
    items = jnp.sum(starts, axis=1)
    own_start = jnp.max(starts * (row[None, :] + 1), axis=1) - 1 + device_index * row_count
    same_item = ((items[:, None] == items[None, :]) & (row[None, :] <= row[:, None])).astype(
        jnp.float32
    )
    sheads = INNER // SHEAD
    place_in_item = meta_index[:, None]
    rate = jnp.exp(decay_log)[None, :]
    state, b_proj, c_proj, raw, step_size, cum, cum_t, last_weight, carry_weight, decay_all = (
        ssm_state(
            ssm_proj,
            tail_x,
            conv_weight,
            place_in_item,
            items[:, None],
            select,
            step_bias[None, :],
            rate,
        )
    )
    states = lax.all_gather(state, "seq")
    last_start = jnp.where(items[-1] > 0, own_start[-1], -1).astype(jnp.float32)
    facts = jnp.concatenate(
        [decay_all[0], jnp.full((128 - sheads,), 1.0) * last_start]
    )
    facts = jnp.broadcast_to(facts[None, :], (8, 128))
    kv_all, facts = gather_both([kv, facts], half, 0)
    ordered = facts[:, 0].reshape(2, half, 128)
    ordered = jnp.where(side == 0, ordered[::-1], ordered).reshape(devices, 128)
    shard = jnp.arange(devices, dtype=jnp.int32)
    earlier_start = jnp.max(jnp.where(shard < device_index, ordered[:, sheads], -1.0)).astype(
        jnp.int32
    )
    first = jnp.where(items > 0, own_start, earlier_start)
    steps = jnp.stack([device_index, device_index - first[0] // row_count])
    attn_full, log_sum = attend(steps, queries, kv_all, first[None, :], half)
    attended = attn_full.reshape(model_width, row_count).astype(jnp.bfloat16).T
    out_weight = attn_weight[:, qkv_cols:]
    attn_proj = jnp.dot(attended, out_weight.T, preferred_element_type=jnp.float32)
    decays = ordered[:, :sheads]
    between_before = (shard[None, :] > shard[:, None]) & (shard[None, :] < device_index)
    weight_before = jnp.where(
        (shard < device_index)[:, None],
        jnp.prod(jnp.where(between_before[:, :, None], decays[None], 1.0), axis=1),
        0.0,
    )
    between_after = (shard[None, :] < shard[:, None]) & (shard[None, :] > device_index)
    weight_after = jnp.where(
        (shard > device_index)[:, None],
        jnp.prod(jnp.where(between_after[:, :, None], decays[None], 1.0), axis=1),
        0.0,
    )
    per_channel = lambda weight: jnp.repeat(weight, SHEAD, axis=1)[:, None, :]
    held_in = jnp.sum(per_channel(weight_before) * states.astype(jnp.float32), axis=0)
    scanned, gated = ssm_output(
        ssm_proj,
        tail_x,
        conv_weight,
        place_in_item,
        b_proj,
        c_proj,
        cum,
        cum_t,
        step_size,
        skip_gain[None, :],
        carry_weight,
        same_item,
        held_in,
    )
    ssm_proj_out = jnp.dot(gated, ssm_down, preferred_element_type=jnp.float32)
    mixed_terms, mix_pull = jax.vjp(branch_mix, attn_proj, ssm_proj_out, attn_beta, ssm_beta)
    hidden1 = layer_in + mixed_terms
    ffn_in_f, ffn_norm_pull = jax.vjp(scaled_norm, hidden1, ffn_gain)
    normed_rows = gathered(after(normed, state), groups)
    ffn_in = after(ffn_in_f.astype(jnp.bfloat16), normed_rows)
    ffn_rows = gather_half([ffn_in], half, 2).reshape(half * row_count, model_width)
    units = FF // half
    wide = (units + 127) // 128 * 128
    in_weight = jnp.concatenate(
        [
            jnp.pad(
                lax.dynamic_slice_in_dim(gate_up, first_unit + place * units, units, 1),
                ((0, 0), (0, wide - units)),
            )
            for first_unit in (0, FF)
        ],
        1,
    )
    down_weight = jnp.pad(
        lax.dynamic_slice_in_dim(ffn_down, place * units, units, 0), ((0, wide - units), (0, 0))
    )
    out_terms, in_terms, in_weight_terms, down_terms = ffn(
        ffn_rows, cot_rows, in_weight, down_weight
    )
    in_terms = in_terms.reshape(half, row_count, model_width)
    grad_ffn_in = sum_half(in_terms, 1, half, 3)
    gate_keep, gate_sent, _ = exchanged(
        in_weight_terms[:units], in_weight_terms[wide : wide + units], side, half
    )
    down_low = down_terms[:units].astype(jnp.bfloat16).reshape(2, units // 2, model_width)
    down_low = jnp.where(side == 0, down_low, down_low[::-1])
    grad_from_ffn, grad_ffn_gain = ffn_norm_pull(grad_ffn_in)
    grad_hidden1 = cotangent.astype(jnp.float32) + grad_from_ffn
    grad_attn_proj, grad_ssm_proj_out, grad_attn_beta, grad_ssm_beta = mix_pull(grad_hidden1)
    attn_grad_low = grad_attn_proj.astype(jnp.bfloat16)
    ssm_grad_low = grad_ssm_proj_out.astype(jnp.bfloat16)
    grad_gated = jnp.dot(ssm_grad_low, ssm_down.T, preferred_element_type=jnp.float32).astype(
        jnp.bfloat16
    )
    out_grad = (
        lax.dot_general(
            out_weight, attn_grad_low, (((0,), (1,)), ((), ())), preferred_element_type=jnp.float32
        )
        .astype(jnp.bfloat16)
        .reshape(GROUPS, per_group, HEAD, row_count)
    )
    grad_queries, kv_terms = attend_back(
        steps, queries, kv_all, first[None, :], attn_full, log_sum, out_grad, half
    )
    def complete(keep, sent, late):
        return keep + after(sent, late).astype(jnp.float32)

    grad_kv = sum_half(kv_terms, 2, half, 1)
    grad_gate_up = complete(gate_keep, gate_sent, grad_queries)
    down_sent = [
        lax.ppermute(
            after(down_low[k], grad_kv),
            "seq",
            [(h * half + q, 2 * q + (h + k) % 2) for h in range(2) for q in range(half)],
        )
        for k in range(2)
    ]
    grad_kv = after(grad_kv, grad_gate_up)
    qkv_grad = jnp.concatenate(
        [grad_queries.reshape(model_width, row_count).T, grad_kv.astype(jnp.bfloat16)], 1
    )
    gated_columns = swapped([gated], half, groups, grad_kv)[0]
    attn_columns = swapped([jnp.concatenate([qkv_grad, attended], 1)], half, groups)[0]
    attn_grad_rows = gathered(attn_grad_low, groups)
    ssm_grad_rows = gathered(ssm_grad_low, groups)
    attn_terms = []
    for k in range(2):
        block = attn_columns[k]
        width = block.shape[1]
        column = (k * half + place) * width + jnp.arange(width, dtype=jnp.int32)
        attn_terms.append(
            jnp.where(
                (column < qkv_cols)[:, None],
                jnp.dot(block.T, normed_rows, preferred_element_type=jnp.float32),
                jnp.dot(block.T, attn_grad_rows, preferred_element_type=jnp.float32),
            )
        )
    held_grads = lax.all_gather(held_grad(ssm_proj, grad_gated, carry_weight, c_proj), "seq")
    later_grad = jnp.sum(per_channel(weight_after) * held_grads.astype(jnp.float32), axis=0)
    grad_decay_all = jnp.sum((later_grad * held_in).reshape(STATE, sheads, SHEAD), axis=(0, 2))
    grad_all = jnp.pad((grad_decay_all * decay_all[0])[None, :], ((0, 0), (0, 128 - sheads)))
    conv_grad, z_grad, end_rows, grad_tail, grad_b, grad_c, grad_raw, grad_conv, grad_heads = (
        ssm_back(
            ssm_proj,
            tail_x,
            conv_weight,
            place_in_item,
            grad_gated,
            scanned,
            b_proj,
            c_proj,
            cum,
            cum_t,
            step_size,
            raw,
            rate,
            skip_gain[None, :],
            last_weight,
            carry_weight,
            same_item,
            held_in,
            later_grad,
            grad_all,
        )
    )
    grad_step_bias, grad_decay, grad_skip = grad_heads[0], grad_heads[1], grad_heads[2]
    out_sum = summed_rows(after(out_terms, grad_raw), groups)
    grad_ffn_down = sum(after(sent, grad_raw).astype(jnp.float32) for sent in down_sent)
    tail_back = from_behind(grad_tail[8 - CONV + 1 :].astype(jnp.bfloat16), "seq", -1)
    end_rows = end_rows[8 - CONV + 1 :] + tail_back.astype(jnp.float32)
    grad_select_in = jnp.concatenate([grad_b, grad_c, grad_raw], 1).astype(jnp.bfloat16)
    attn_keep, attn_sent, attn_send = exchanged(
        attn_terms[0], attn_terms[1], side, half, tail_back
    )
    ssm_down_keep, ssm_down_sent, ssm_down_send = exchanged(
        jnp.dot(gated_columns[0].T, ssm_grad_rows, preferred_element_type=jnp.float32),
        jnp.dot(gated_columns[1].T, ssm_grad_rows, preferred_element_type=jnp.float32),
        side,
        half,
        tail_back,
    )
    conv_grad = jnp.concatenate(
        [conv_grad[: row_count - CONV + 1], end_rows.astype(jnp.bfloat16)], 0
    )
    proj_grad = jnp.concatenate([conv_grad, z_grad], 1)
    proj_grad = after(proj_grad, attn_send)
    ssm_columns = swapped([proj_grad], half, groups)[0]
    grad_normed = jnp.dot(qkv_grad, attn_weight[:, :qkv_cols].T, preferred_element_type=jnp.float32)
    grad_normed = grad_normed + jnp.dot(proj_grad, ssm_weight.T, preferred_element_type=jnp.float32)
    grad_normed = grad_normed + jnp.dot(
        grad_select_in, select_weight.T, preferred_element_type=jnp.float32
    )
    ssm_keep, ssm_sent, ssm_send = exchanged(
        jnp.dot(ssm_columns[0].T, normed_rows, preferred_element_type=jnp.float32),
        jnp.dot(ssm_columns[1].T, normed_rows, preferred_element_type=jnp.float32),
        side,
        half,
    )
    grad_select = jnp.dot(grad_select_in.T, normed, preferred_element_type=jnp.float32)
    mixer_norm_pull = jax.vjp(scaled_norm, layer_in, mixer_gain)[1]
    grad_from_mixer, grad_mixer_gain = mixer_norm_pull(grad_normed)
    grad_layer_in = grad_hidden1 + grad_from_mixer
    grad_tokens = jnp.where(is_meta, 0.0, grad_layer_in).astype(jnp.bfloat16)
    grad_meta = jnp.dot(one_hot.T, jnp.where(is_meta, grad_layer_in, 0.0), precision=highest)
    pieces = [
        grad_meta,
        grad_select,
        grad_conv.reshape(-1, model_width),
        jnp.stack([grad_mixer_gain, grad_attn_beta, grad_ssm_beta, grad_ffn_gain]),
        jnp.pad(
            jnp.concatenate([grad_step_bias, grad_decay, grad_skip])[None, :],
            ((0, 0), (0, model_width - 3 * sheads)),
        ),
    ]
    counts = [piece.shape[0] for piece in pieces]
    share = -(-sum(counts) // (8 * devices)) * 8
    packed = jnp.concatenate(
        pieces + [jnp.zeros((share * devices - sum(counts), model_width), jnp.float32)], 0
    )
    packed = after(
        packed, (attn_send, ssm_down_send, ssm_send, grad_ffn_down)
    )
    packed = total_of(packed.reshape(devices, share, model_width), devices, 4)
    packed = packed.reshape(devices * share, model_width)
    at = [sum(counts[:i]) for i in range(len(counts))]
    gains = packed[at[3] : at[4]]
    little = packed[at[4]]
    small = (
        packed[: counts[0]],
        gains[0],
        packed[at[1] : at[2]].T,
        packed[at[2] : at[3]].reshape(grad_conv.shape),
        little[:sheads],
        little[sheads : 2 * sheads],
        little[2 * sheads : 3 * sheads],
        gains[1],
        gains[2],
        gains[3],
    )
    grad_ssm = complete(ssm_keep, ssm_sent, little)
    late = grad_ssm[0]
    layer_out = (hidden1 + after(out_sum, late).astype(jnp.float32)).astype(jnp.bfloat16)
    shares = (
        complete(attn_keep, attn_sent, late).T,
        grad_ssm.T,
        complete(ssm_down_keep, ssm_down_sent, late),
        grad_gate_up.T,
        grad_ffn_down,
    )
    return (
        layer_out,
        grad_tokens,
        small[0],
        small[1],
        shares[0],
        shares[1],
        small[2],
        small[3],
        small[4],
        small[5],
        small[6],
        shares[2],
        small[7],
        small[8],
        small[9],
        shares[3],
        shares[4],
    )


def solution(mesh):
    placed = (
        P("seq", None),
        P("seq"),
        P("seq"),
        P(),
        P(),
        P(),
        P(),
        P(),
        P(),
        P(),
        P(),
        P(),
        P(),
        P(),
        P(),
        P(),
        P(),
        P(),
        P("seq", None),
    )
    return jax.shard_map(
        per_device,
        mesh=mesh,
        in_specs=placed,
        out_specs=(
            P("seq", None),
            P("seq", None),
            P(),
            P(),
            P(None, "seq"),
            P(None, "seq"),
            P(),
            P(),
            P(),
            P(),
            P(),
            P("seq", None),
            P(),
            P(),
            P(),
            P(None, "seq"),
            P("seq", None),
        ),
        check_vma=False,
    )
```

```python
from functools import partial
import math

import jax
import jax.numpy as jnp
from jax import lax
from jax.experimental import pallas as pl
from jax.experimental.pallas import tpu as pltpu
from jax.sharding import PartitionSpec as P

HEADS = 25
GROUPS = 5
HEAD = 64
INNER = 3200
STATE = 16
CONV = 4
FF = 5504
META = 128
SHEAD = 64


eps = 1e-05
highest = lax.Precision.HIGHEST


MESH = pl.DeviceIdType.MESH
MIB = 2**20


def cost(microseconds):
    return pl.CostEstimate(
        flops=0, transcendentals=0, bytes_accessed=int(microseconds * 3_000_000)
    )


def flipped(v, k):
    bit = 1 << k
    return jnp.where(lax.rem(v // bit, 2) == 0, v + bit, v - bit)


def flips_of(v, bits):
    out = [v]
    for k in bits:
        out = out + [flipped(o, k) for o in out]
    return out


def thirds(rows):
    most = (rows // 3 + 15) // 16 * 16
    return [(0, most), (most, most), (2 * most, rows - 2 * most)]


def parts_of(rows):
    return [part for part in thirds(rows) if part[1] > 0] if rows >= 48 else [(0, rows)]


def greet(partners):
    barrier = pltpu.get_barrier_semaphore()
    for partner in partners:
        pl.semaphore_signal(barrier, inc=1, device_id=(partner,), device_id_type=MESH)
    pl.semaphore_wait(barrier, len(partners))


def remote(src, dst, send, recv, device):
    return pltpu.make_async_remote_copy(
        src_ref=src,
        dst_ref=dst,
        send_sem=send,
        recv_sem=recv,
        device_id=(device,),
        device_id_type=MESH,
    )


def gather_kernel(arrays, half, *refs):
    ins, out = refs[:arrays], refs[arrays]
    send, recv, core_send, core_recv, local_sem = refs[arrays + 1 :]
    me = lax.axis_index("seq")
    place = lax.rem(me, half)
    bits = half.bit_length() - 1
    greet([flipped(me, k) for k in range(bits)])
    parts = thirds(ins[0].shape[0])
    links = bits - 1
    orders = [[1 + (c + s) % links for s in range(links)] for c in range(3)]
    local = [
        pltpu.make_async_copy(ins[a], out.at[a * half + place], local_sem.at[a])
        for a in range(arrays)
    ]
    for copy in local:
        copy.start()
    sent, handed = [], []
    for step in range(links + 1):
        arriving = []
        for c, (first, count) in enumerate(parts):
            rows = pl.ds(first, count)
            held = flips_of(place, orders[c][:step])
            for a in range(arrays):
                if step < links:
                    for i, b in enumerate(held):
                        place_at = out.at[a * half + b, rows]
                        at = (1 << step) - 1 + i
                        copy = remote(
                            ins[a].at[rows] if i == 0 else place_at,
                            place_at,
                            send.at[a, c, at],
                            recv.at[a, c, at],
                            flipped(me, orders[c][step]),
                        )
                        copy.start()
                        arriving.append(copy)
                new = held if step == 0 else held[len(held) // 2 :]
                for i, b in enumerate(new):
                    place_at = out.at[a * half + b, rows]
                    at = 0 if step == 0 else (1 << (step - 1)) + i
                    copy = remote(
                        ins[a].at[rows] if step == 0 else place_at,
                        place_at,
                        core_send.at[a, c, at],
                        core_recv.at[a, c, at],
                        flipped(me, 0),
                    )
                    copy.start()
                    handed.append(copy)
        for copy in arriving:
            copy.wait_recv()
        sent += arriving
    for copy in sent:
        copy.wait_send()
    for copy in handed:
        copy.wait()
    for copy in local:
        copy.wait()


def gather_half(arrays, half, collective_id):
    count = len(arrays)
    shape = arrays[0].shape
    semaphores = pltpu.SemaphoreType.DMA((count, 3, half // 2))
    return pl.pallas_call(
        partial(gather_kernel, count, half),
        out_shape=jax.ShapeDtypeStruct((count * half,) + shape, arrays[0].dtype),
        in_specs=[pl.BlockSpec(memory_space=pl.ANY)] * count,
        out_specs=pl.BlockSpec(memory_space=pl.ANY),
        scratch_shapes=[semaphores] * 4 + [pltpu.SemaphoreType.DMA((count,))],
        compiler_params=pltpu.CompilerParams(collective_id=collective_id, has_side_effects=True),
        cost_estimate=cost(40),
        name="gather_half",
    )(*arrays)


def gather_both_kernel(arrays, half, *refs):
    ins, outs = refs[:arrays], refs[arrays : 2 * arrays]
    send, recv, core_send, core_recv, flip_send, flip_recv, local_sem = refs[2 * arrays :]
    me = lax.axis_index("seq")
    place = lax.rem(me, half)
    twin = jnp.where(me < half, me + half, me - half)
    bits = half.bit_length() - 1
    greet([flipped(me, k) for k in range(bits)] + [twin])
    links = bits - 1
    orders = [[1 + (c + s) % links for s in range(links)] for c in range(3)]
    parts = [parts_of(ref.shape[0]) for ref in ins]
    local, sent, handed, twins = [], [], [], []
    for a in range(arrays):
        copy = remote(ins[a], outs[a].at[place], flip_send.at[a], flip_recv.at[a], twin)
        copy.start()
        twins.append(copy)
        copy = pltpu.make_async_copy(ins[a], outs[a].at[half + place], local_sem.at[a])
        copy.start()
        local.append(copy)
    for time in range(links + 2):
        arriving = []
        for own in (1, 0):
            step = time - (1 - own)
            if step < 0 or step > links:
                continue
            for a in range(arrays):
                for c, (first, count) in enumerate(parts[a]):
                    rows = pl.ds(first, count)
                    slot = own * arrays + a
                    held = flips_of(place, orders[c][:step])
                    if step < links:
                        for i, b in enumerate(held):
                            place_at = outs[a].at[own * half + b, rows]
                            at = (1 << step) - 1 + i
                            copy = remote(
                                ins[a].at[rows] if i == 0 and own else place_at,
                                place_at,
                                send.at[slot, c, at],
                                recv.at[slot, c, at],
                                flipped(me, orders[c][step]),
                            )
                            copy.start()
                            arriving.append(copy)
                    new = held if step == 0 else held[len(held) // 2 :]
                    for i, b in enumerate(new):
                        place_at = outs[a].at[own * half + b, rows]
                        at = 0 if step == 0 else (1 << (step - 1)) + i
                        copy = remote(
                            ins[a].at[rows] if step == 0 and own else place_at,
                            place_at,
                            core_send.at[slot, c, at],
                            core_recv.at[slot, c, at],
                            flipped(me, 0),
                        )
                        copy.start()
                        handed.append(copy)
        if time == 0:
            for copy in twins:
                copy.wait_recv()
        for copy in arriving:
            copy.wait_recv()
        sent += arriving
    for copy in sent + twins:
        copy.wait_send()
    for copy in handed:
        copy.wait()
    for copy in local:
        copy.wait()


def gather_both(arrays, half, collective_id):
    count = len(arrays)
    semaphores = pltpu.SemaphoreType.DMA((2 * count, 3, half // 2))
    single = pltpu.SemaphoreType.DMA((count,))
    return pl.pallas_call(
        partial(gather_both_kernel, count, half),
        out_shape=[jax.ShapeDtypeStruct((2 * half,) + a.shape, a.dtype) for a in arrays],
        in_specs=[pl.BlockSpec(memory_space=pl.ANY)] * count,
        out_specs=[pl.BlockSpec(memory_space=pl.ANY)] * count,
        scratch_shapes=[semaphores] * 4 + [single] * 3,
        compiler_params=pltpu.CompilerParams(collective_id=collective_id, has_side_effects=True),
        cost_estimate=cost(50),
        name="gather_both",
    )(*arrays)


def total_kernel(devices, terms, out, mine, core_in, link_in, send, recv, send_back, recv_back):
    me = lax.axis_index("seq")
    bits = devices.bit_length() - 1
    greet([flipped(me, k) for k in range(bits)])
    pairs = devices // 2
    columns = terms.shape[2]
    third = columns // 3 // 128 * 128
    parts = [(0, third), (third, third), (2 * third, columns - 2 * third)]
    turned = min(3, bits - 1)
    orders = [
        [1 + (c + s) % turned for s in range(turned)] + list(range(1 + turned, bits))
        for c in range(3)
    ]
    everything = pl.ds(0, columns)
    copies = []
    first = []
    for i in range(pairs):
        block = 2 * i + 1 - lax.rem(me, 2)
        copy = remote(
            terms.at[block], core_in.at[i], send.at[0, i], recv.at[0, i], flipped(me, 0)
        )
        copy.start()
        first.append(copy)
    copies += first
    for i in range(pairs):
        first[i].wait_recv()
        mine[i] = terms[2 * i + lax.rem(me, 2)] + core_in[i]
    for step in range(bits - 1):
        arriving = []
        for c, (start, count) in enumerate(parts):
            lanes = pl.ds(start, count)
            for i, b in enumerate(flips_of(me, orders[c][step + 1 :])):
                away = flipped(b, orders[c][step])
                at = pairs - (pairs >> step) + i
                copy = remote(
                    mine.at[away // 2, :, lanes],
                    link_in.at[at, :, lanes],
                    send.at[1 + c, at],
                    recv.at[1 + c, at],
                    flipped(me, orders[c][step]),
                )
                copy.start()
                arriving.append((copy, b, at, lanes))
        for copy, b, at, lanes in arriving:
            copy.wait_recv()
            mine[b // 2, :, lanes] = mine[b // 2, :, lanes] + link_in[at, :, lanes]
            copies.append(copy)
    out[me] = mine[me // 2]
    for step in range(bits - 1):
        arriving = []
        for c, (start, count) in enumerate(parts):
            lanes = pl.ds(start, count)
            order = orders[c][::-1]
            for i, b in enumerate(flips_of(me, order[:step])):
                at = (1 << step) - 1 + i
                copy = remote(
                    out.at[b, :, lanes],
                    out.at[b, :, lanes],
                    send_back.at[1 + c, at],
                    recv_back.at[1 + c, at],
                    flipped(me, order[step]),
                )
                copy.start()
                arriving.append(copy)
        for copy in arriving:
            copy.wait_recv()
        copies += arriving
    last = []
    for i, b in enumerate(flips_of(me, range(1, bits))):
        copy = remote(
            out.at[b], out.at[b], send_back.at[0, i], recv_back.at[0, i], flipped(me, 0)
        )
        copy.start()
        last.append(copy)
    for copy in last:
        copy.wait()
    for copy in copies:
        copy.wait_send()


def total_of(terms, devices, collective_id, *early):
    pairs = devices // 2
    half_shape = (pairs,) + terms.shape[1:]
    semaphores = pltpu.SemaphoreType.DMA((4, pairs))
    return pl.pallas_call(
        lambda terms, *refs: total_kernel(devices, terms, *refs[len(early) :]),
        out_shape=jax.ShapeDtypeStruct(terms.shape, terms.dtype),
        in_specs=[pl.BlockSpec(memory_space=pltpu.VMEM)]
        + [pl.BlockSpec(memory_space=pl.ANY)] * len(early),
        out_specs=pl.BlockSpec(memory_space=pltpu.VMEM),
        scratch_shapes=[pltpu.VMEM(half_shape, terms.dtype)] * 3 + [semaphores] * 4,
        compiler_params=pltpu.CompilerParams(
            collective_id=collective_id, has_side_effects=True, vmem_limit_bytes=48 * MIB
        ),
        cost_estimate=cost(40),
        name="total_of",
    )(terms, *early)


def sum_kernel(arrays, half, *refs):
    terms, out = refs[:2]
    mine, core_in, link_in, load_sem, send, recv, core_send, core_recv, flip_in, flip_sem = refs[2:]
    me = lax.axis_index("seq")
    place = lax.rem(me, half)
    bits = half.bit_length() - 1
    twin = jnp.where(me < half, me + half, me - half)
    greet([flipped(me, k) for k in range(bits)] + ([twin] if arrays == 2 else []))
    parts = thirds(terms.shape[1])
    links = bits - 1
    orders = [[1 + (c + s) % links for s in range(links)] for c in range(3)]
    loads = []
    pairs = half // 2
    for a in range(arrays):
        for i in range(pairs):
            block = 2 * i + lax.rem(place, 2)
            copy = pltpu.make_async_copy(
                terms.at[a * half + block], mine.at[a, i], load_sem.at[a, i]
            )
            copy.start()
            loads.append(copy)
    handed = {}
    for wanted in range(2):
        for c, (first, count) in enumerate(parts):
            rows = pl.ds(first, count)
            kept = flips_of(place, orders[c][1:])
            blocks = kept if wanted else [flipped(b, orders[c][0]) for b in kept]
            for a in range(arrays):
                for i, b in enumerate(blocks):
                    at = wanted * (pairs // 2) + i
                    copy = remote(
                        terms.at[a * half + flipped(b, 0), rows],
                        core_in.at[a, at, rows],
                        core_send.at[a, c, at],
                        core_recv.at[a, c, at],
                        flipped(me, 0),
                    )
                    copy.start()
                    handed[a, c, at] = copy
    for copy in loads:
        copy.wait()
    sent = []
    arriving = {}

    def add(ref, slot, rows, other):
        ref[slot, rows] = (
            ref[slot, rows].astype(jnp.float32) + other[...].astype(jnp.float32)
        ).astype(ref.dtype)

    for step in range(links):
        for c, (first, count) in enumerate(parts):
            rows = pl.ds(first, count)
            kept = flips_of(place, orders[c][step + 1 :])
            for a in range(arrays):
                for i, b in enumerate(kept):
                    out_block = flipped(b, orders[c][step])
                    if step == 0:
                        handed[a, c, i].wait_recv()
                        add(mine.at[a], out_block // 2, rows, core_in.at[a, i, rows])
                    at = pairs - (pairs >> step) + i
                    copy = remote(
                        mine.at[a, out_block // 2, rows],
                        link_in.at[a, at, rows],
                        send.at[a, c, at],
                        recv.at[a, c, at],
                        flipped(me, orders[c][step]),
                    )
                    copy.start()
                    arriving[a, c, at] = copy
                    sent.append(copy)
        if step == 0:
            for c, (first, count) in enumerate(parts):
                rows = pl.ds(first, count)
                for a in range(arrays):
                    for i, b in enumerate(flips_of(place, orders[c][1:])):
                        at = pairs // 2 + i
                        handed[a, c, at].wait_recv()
                        add(mine.at[a], b // 2, rows, core_in.at[a, at, rows])
        for c, (first, count) in enumerate(parts):
            rows = pl.ds(first, count)
            kept = flips_of(place, orders[c][step + 1 :])
            for a in range(arrays):
                for i, b in enumerate(kept):
                    at = pairs - (pairs >> step) + i
                    arriving[a, c, at].wait_recv()
                    add(mine.at[a], b // 2, rows, link_in.at[a, at, rows])
    if arrays == 2:
        flip = remote(mine.at[0, place // 2], flip_in, flip_sem.at[0], flip_sem.at[1], twin)
        flip.start()
        flip.wait_recv()
        out[...] = mine[1, place // 2].astype(jnp.float32) + flip_in[...].astype(jnp.float32)
        sent.append(flip)
    else:
        out[...] = mine[0, place // 2].astype(jnp.float32)
    for copy in sent:
        copy.wait_send()
    for copy in handed.values():
        copy.wait_send()


def sum_half(terms, arrays, half, collective_id, *early):
    rows, columns = terms.shape[1:]
    pairs = half // 2
    block = (rows, columns)
    semaphores = pltpu.SemaphoreType.DMA((arrays, 3, pairs))
    return pl.pallas_call(
        lambda terms, *refs: sum_kernel(arrays, half, terms, *refs[len(early) :]),
        out_shape=jax.ShapeDtypeStruct(block, jnp.float32),
        in_specs=[pl.BlockSpec(memory_space=pl.ANY)] * (1 + len(early)),
        out_specs=pl.BlockSpec(memory_space=pltpu.VMEM),
        scratch_shapes=[
            pltpu.VMEM((arrays, pairs) + block, terms.dtype),
            pltpu.VMEM((arrays, pairs) + block, terms.dtype),
            pltpu.VMEM((arrays, pairs) + block, terms.dtype),
            pltpu.SemaphoreType.DMA((arrays, pairs)),
        ]
        + [semaphores] * 4
        + [
            pltpu.VMEM(block if arrays == 2 else (16, 128), terms.dtype),
            pltpu.SemaphoreType.DMA((2,)),
        ],
        compiler_params=pltpu.CompilerParams(
            collective_id=collective_id, has_side_effects=True, vmem_limit_bytes=60 * MIB
        ),
        cost_estimate=cost(50),
        name="sum_half",
    )(terms, *early)


def ffn_kernel(x_ref, cot_ref, in_ref, down_ref, out_ref, grad_in_ref, grad_w_ref, grad_d_ref):
    wide = down_ref.shape[0]
    x, cot = x_ref[...], cot_ref[...]
    low = jnp.bfloat16

    def dot(a, b, contract):
        return lax.dot_general(a, b, (contract, ((), ())), preferred_element_type=jnp.float32)

    vals = dot(x, in_ref[...], ((1,), (0,)))
    gate, up = vals[:, :wide], vals[:, wide:]
    sigma = jax.nn.sigmoid(gate)
    act = gate * sigma
    hidden = (act * up).astype(low)
    out_ref[...] = dot(hidden, down_ref[...], ((1,), (0,))).astype(low)
    grad_hidden = dot(cot, down_ref[...], ((1,), (1,))).astype(low).astype(jnp.float32)
    slope = sigma * (1.0 + gate * (1.0 - sigma))
    grads = jnp.concatenate([grad_hidden * up * slope, grad_hidden * act], 1).astype(low)
    grad_in_ref[...] = dot(grads, in_ref[...], ((1,), (1,))).astype(low)

    @pl.when(pl.program_id(0) == 0)
    def _():
        grad_w_ref[...] = jnp.zeros_like(grad_w_ref)
        grad_d_ref[...] = jnp.zeros_like(grad_d_ref)

    grad_w_ref[...] += dot(grads, x, ((0,), (0,)))
    grad_d_ref[...] += dot(hidden, cot, ((0,), (0,)))


def ffn(x, cot, in_weight, down_weight):
    rows, model = x.shape
    block = min(256, rows)
    wide = down_weight.shape[0]
    moving = pl.BlockSpec((block, model), lambda i: (i, 0))
    fixed = lambda shape: pl.BlockSpec(shape, lambda i: (0, 0))
    return pl.pallas_call(
        ffn_kernel,
        grid=(rows // block,),
        out_shape=[
            jax.ShapeDtypeStruct(x.shape, jnp.bfloat16),
            jax.ShapeDtypeStruct(x.shape, jnp.bfloat16),
            jax.ShapeDtypeStruct((2 * wide, model), jnp.float32),
            jax.ShapeDtypeStruct((wide, model), jnp.float32),
        ],
        in_specs=[moving, moving, fixed(in_weight.shape), fixed(down_weight.shape)],
        out_specs=[moving, moving, fixed((2 * wide, model)), fixed((wide, model))],
        compiler_params=pltpu.CompilerParams(vmem_limit_bytes=56 * MIB),
        cost_estimate=cost(35),
        name="ffn",
    )(x, cot, in_weight, down_weight)


def masked_block(at, first_ref, device_index, rows):
    key = lax.broadcasted_iota(jnp.int32, (rows, rows), 0) + at * rows
    query = lax.broadcasted_iota(jnp.int32, (rows, rows), 1) + device_index * rows
    seen = ((key >= first_ref[...]) & (key <= query)).astype(jnp.float32)
    return jnp.concatenate([seen] * (HEADS // GROUPS), 1) > 0.0


def side_by_side(ref, g):
    return jnp.concatenate([ref[g, j] for j in range(HEADS // GROUPS)], 1)


def over_shards(steps_ref, body):
    body(0)

    @pl.loop(1, steps_ref[1] + 1)
    def _(hop):
        body(hop)


def attend_kernel(half, steps_ref, q_ref, kv_ref, first_ref, out_ref, log_ref, top, total, acc):
    device_index, newest = steps_ref[0], half + lax.rem(steps_ref[0], half)
    rows = kv_ref.shape[1]
    top[...] = jnp.full_like(top, -1e30)
    total[...] = jnp.zeros_like(total)
    acc[...] = jnp.zeros_like(acc)

    def body(hop):
        block = kv_ref[newest - hop]
        seen = masked_block(device_index - hop, first_ref, device_index, rows)
        for g in range(GROUPS):
            keys = block[:, g * HEAD : (g + 1) * HEAD]
            values = block[:, (GROUPS + g) * HEAD : (GROUPS + g + 1) * HEAD]
            scores = jnp.dot(keys, side_by_side(q_ref, g), preferred_element_type=jnp.float32)
            scores = jnp.where(seen, scores, -1e30)
            now = jnp.maximum(top[g], jnp.max(scores, axis=0, keepdims=True))
            probs = jnp.exp(scores - now)
            fade = jnp.exp(top[g] - now)
            top[g] = now
            total[g] = total[g] * fade + jnp.sum(probs, axis=0, keepdims=True)
            acc[g] = acc[g] * fade + lax.dot_general(
                values,
                probs.astype(jnp.bfloat16),
                (((0,), (0,)), ((), ())),
                preferred_element_type=jnp.float32,
            )

    over_shards(steps_ref, body)
    for g in range(GROUPS):
        done = acc[g] / total[g]
        for j in range(HEADS // GROUPS):
            out_ref[g, j] = done[:, j * rows : (j + 1) * rows]
        log_ref[g] = top[g] + jnp.log(total[g])


def attend(steps, queries, kv, first, half):
    rows = kv.shape[1]
    per_group = HEADS // GROUPS
    wide = per_group * rows
    return pl.pallas_call(
        partial(attend_kernel, half),
        out_shape=[
            jax.ShapeDtypeStruct((GROUPS, per_group, HEAD, rows), jnp.float32),
            jax.ShapeDtypeStruct((GROUPS, 1, wide), jnp.float32),
        ],
        in_specs=[pl.BlockSpec(memory_space=pltpu.SMEM)]
        + [pl.BlockSpec(memory_space=pltpu.VMEM)] * 3,
        out_specs=[pl.BlockSpec(memory_space=pltpu.VMEM)] * 2,
        scratch_shapes=[
            pltpu.VMEM((GROUPS, 1, wide), jnp.float32),
            pltpu.VMEM((GROUPS, 1, wide), jnp.float32),
            pltpu.VMEM((GROUPS, HEAD, wide), jnp.float32),
        ],
        compiler_params=pltpu.CompilerParams(vmem_limit_bytes=56 * MIB),
        cost_estimate=cost(15),
        name="attend",
    )(steps, queries, kv, first)


def attend_back_kernel(
    half,
    steps_ref,
    q_ref,
    kv_ref,
    first_ref,
    out_ref,
    log_ref,
    grad_ref,
    grad_q_ref,
    grad_kv_ref,
    dots,
    acc,
):
    device_index, newest = steps_ref[0], half + lax.rem(steps_ref[0], half)
    rows = kv_ref.shape[1]
    contract = lambda a, b, i: lax.dot_general(
        a, b, (((i,), (i,)), ((), ())), preferred_element_type=jnp.float32
    )
    for g in range(GROUPS):
        product = side_by_side(out_ref, g) * side_by_side(grad_ref, g).astype(jnp.float32)
        dots[g] = jnp.sum(product, axis=0, keepdims=True)
    acc[...] = jnp.zeros_like(acc)

    @pl.loop(0, 2 * half)
    def _(i):
        grad_kv_ref[i] = jnp.zeros(grad_kv_ref.shape[1:], grad_kv_ref.dtype)

    def body(hop):
        block = kv_ref[newest - hop]
        seen = masked_block(device_index - hop, first_ref, device_index, rows)
        grad_keys, grad_values = [], []
        for g in range(GROUPS):
            keys = block[:, g * HEAD : (g + 1) * HEAD]
            values = block[:, (GROUPS + g) * HEAD : (GROUPS + g + 1) * HEAD]
            queries, grads = side_by_side(q_ref, g), side_by_side(grad_ref, g)
            scores = jnp.dot(keys, queries, preferred_element_type=jnp.float32)
            probs = jnp.where(seen, jnp.exp(scores - log_ref[g]), 0.0)
            grad_probs = jnp.dot(values, grads, preferred_element_type=jnp.float32)
            grad_values.append(contract(probs.astype(jnp.bfloat16), grads, 1))
            grad_scores = (probs * (grad_probs - dots[g])).astype(jnp.bfloat16)
            grad_keys.append(contract(grad_scores, queries, 1))
            acc[g] += contract(keys, grad_scores, 0)
        grad_kv_ref[newest - hop] = jnp.concatenate(grad_keys + grad_values, 1).astype(
            grad_kv_ref.dtype
        )

    over_shards(steps_ref, body)
    for g in range(GROUPS):
        for j in range(HEADS // GROUPS):
            grad_q_ref[g, j] = (acc[g, :, j * rows : (j + 1) * rows] * (HEAD**-0.5)).astype(
                grad_q_ref.dtype
            )


def attend_back(steps, queries, kv, first, out, log_sum, grads, half):
    rows = kv.shape[1]
    wide = HEADS // GROUPS * rows
    return pl.pallas_call(
        partial(attend_back_kernel, half),
        out_shape=[
            jax.ShapeDtypeStruct(queries.shape, jnp.bfloat16),
            jax.ShapeDtypeStruct(kv.shape, jnp.bfloat16),
        ],
        in_specs=[pl.BlockSpec(memory_space=pltpu.SMEM)]
        + [pl.BlockSpec(memory_space=pltpu.VMEM)] * 6,
        out_specs=[pl.BlockSpec(memory_space=pltpu.VMEM)] * 2,
        scratch_shapes=[
            pltpu.VMEM((GROUPS, 1, wide), jnp.float32),
            pltpu.VMEM((GROUPS, HEAD, wide), jnp.float32),
        ],
        compiler_params=pltpu.CompilerParams(vmem_limit_bytes=60 * MIB),
        cost_estimate=cost(20),
        name="attend_back",
    )(steps, queries, kv, first, out, log_sum, grads)


def spread_heads(ref, tile, rows):
    first_half = lax.broadcasted_iota(jnp.int32, (rows, 128), 1) < SHEAD
    return jnp.where(
        first_half, ref[:, 2 * tile : 2 * tile + 1], ref[:, 2 * tile + 1 : 2 * tile + 2]
    )


def conv_tile(proj_ref, tail_ref, taps_ref, place, extended, at, rows):
    extended[8 : 8 + rows] = proj_ref[:, at]
    extended[0:8] = tail_ref[:, at]
    lagged = []
    summed = jnp.zeros((rows, 128), jnp.float32)
    for lag in range(taps_ref.shape[0]):
        moved = extended[8 - lag : 8 - lag + rows]
        moved = moved if lag == 0 else jnp.where(place >= lag, moved, 0.0)
        lagged.append(moved)
        summed = summed + taps_ref[lag : lag + 1, at] * moved
    return summed, lagged


def ssm_state_kernel(
    proj_ref,
    tail_ref,
    taps_ref,
    place_ref,
    items_ref,
    select_ref,
    bias_ref,
    rate_ref,
    state_ref,
    b_ref,
    c_ref,
    raw_ref,
    step_ref,
    cum_ref,
    cum_t_ref,
    last_ref,
    carry_ref,
    all_ref,
    extended,
):
    rows, inner = proj_ref.shape[0], taps_ref.shape[1]
    heads = step_ref.shape[1]
    low = jnp.bfloat16
    b_ref[...] = select_ref[:, :STATE].astype(low)
    c_ref[...] = select_ref[:, STATE : 2 * STATE].astype(low)
    raw = select_ref[:, 2 * STATE :] + bias_ref[...]
    raw_ref[...] = raw
    step = jnp.maximum(raw, 0.0) + jnp.log1p(jnp.exp(-jnp.abs(raw)))
    step_ref[...] = step
    lower = (
        lax.broadcasted_iota(jnp.int32, (rows, rows), 0)
        >= lax.broadcasted_iota(jnp.int32, (rows, rows), 1)
    ).astype(jnp.float32)
    cum = jnp.dot(
        lower, -step * rate_ref[...], precision=highest, preferred_element_type=jnp.float32
    )
    cum_ref[...] = cum
    wide = jnp.concatenate([cum, jnp.zeros((rows, 128 - heads), jnp.float32)], 1)
    cum_t_ref[...] = wide.T[:heads]
    items = items_ref[...]
    final = items_ref[rows - 1 : rows, :]
    total = cum[rows - 1 : rows, :]
    last_ref[...] = jnp.where(items == final, jnp.exp(total - cum), 0.0)
    carry_ref[...] = jnp.where(items == 0, jnp.exp(cum), 0.0)
    all_ref[...] = jnp.where(final == 0, jnp.exp(total), 0.0)
    place = place_ref[...]
    b = b_ref[...]
    for tile in range(inner // 128):
        at = slice(tile * 128, (tile + 1) * 128)
        summed, _ = conv_tile(proj_ref, tail_ref, taps_ref, place, extended, at, rows)
        x = summed * jax.nn.sigmoid(summed)
        taken = x * spread_heads(step_ref, tile, rows) * spread_heads(last_ref, tile, rows)
        state_ref[:, at] = lax.dot_general(
            b, taken.astype(low), (((0,), (0,)), ((), ())), preferred_element_type=jnp.float32
        ).astype(low)


def whole_call(kernel, operands, outs, scratch, microseconds, name):
    return pl.pallas_call(
        kernel,
        out_shape=[jax.ShapeDtypeStruct(dims, kind) for dims, kind in outs],
        in_specs=[pl.BlockSpec(memory_space=pltpu.VMEM)] * len(operands),
        out_specs=[pl.BlockSpec(memory_space=pltpu.VMEM)] * len(outs),
        scratch_shapes=scratch,
        compiler_params=pltpu.CompilerParams(vmem_limit_bytes=48 * MIB),
        cost_estimate=cost(microseconds),
        name=name,
    )(*operands)


def ssm_state(proj, tail, taps, place, items, select, bias, rate):
    rows, inner, heads = proj.shape[0], taps.shape[1], bias.shape[1]
    low, full = jnp.bfloat16, jnp.float32
    by_head = ((rows, heads), full)
    outs = [((STATE, inner), low), ((rows, STATE), low), ((rows, STATE), low)]
    outs += [by_head, by_head, by_head, ((heads, rows), full), by_head, by_head]
    outs += [((1, heads), full)]
    operands = (proj, tail, taps, place, items, select, bias, rate)
    scratch = [pltpu.VMEM((rows + 8, 128), full)]
    return whole_call(ssm_state_kernel, operands, outs, scratch, 8, "ssm_state")


def ssm_output_kernel(
    proj_ref,
    tail_ref,
    taps_ref,
    place_ref,
    b_ref,
    c_ref,
    cum_ref,
    cum_t_ref,
    step_ref,
    skip_ref,
    carry_ref,
    same_ref,
    held_ref,
    scanned_ref,
    gated_ref,
    extended,
):
    rows, inner = proj_ref.shape[0], taps_ref.shape[1]
    low = jnp.bfloat16
    place, c = place_ref[...], c_ref[...]
    both = lax.dot_general(
        c, b_ref[...], (((1,), (1,)), ((), ())), preferred_element_type=jnp.float32
    )
    same = same_ref[...] > 0.0
    first_half = lax.broadcasted_iota(jnp.int32, (rows, 128), 1) < SHEAD
    for tile in range(inner // 128):
        at = slice(tile * 128, (tile + 1) * 128)
        summed, _ = conv_tile(proj_ref, tail_ref, taps_ref, place, extended, at, rows)
        x = summed * jax.nn.sigmoid(summed)
        scaled = (x * spread_heads(step_ref, tile, rows)).astype(low)
        halves = []
        for k in range(2):
            head = 2 * tile + k
            exponent = jnp.where(
                same, cum_ref[:, head : head + 1] - cum_t_ref[head : head + 1, :], -1e30
            )
            weights = (jnp.exp(exponent) * both).astype(low)
            halves.append(jnp.dot(weights, scaled, preferred_element_type=jnp.float32))
        carried = jnp.dot(c, held_ref[:, at].astype(low), preferred_element_type=jnp.float32)
        out = (
            jnp.where(first_half, halves[0], halves[1])
            + carried * spread_heads(carry_ref, tile, rows)
            + spread_heads(skip_ref, tile, rows) * x
        )
        scanned_ref[:, at] = out
        z = proj_ref[:, inner + tile * 128 : inner + (tile + 1) * 128]
        gated_ref[:, at] = (out * z * jax.nn.sigmoid(z)).astype(low)


def ssm_output(*operands):
    rows, inner = operands[0].shape[0], operands[2].shape[1]
    outs = [((rows, inner), jnp.float32), ((rows, inner), jnp.bfloat16)]
    scratch = [pltpu.VMEM((rows + 8, 128), jnp.float32)]
    return whole_call(ssm_output_kernel, operands, outs, scratch, 8, "ssm_output")


def held_grad_kernel(proj_ref, grad_ref, carry_ref, c_ref, out_ref):
    rows, inner = grad_ref.shape
    for tile in range(inner // 128):
        at = slice(tile * 128, (tile + 1) * 128)
        z = proj_ref[:, inner + tile * 128 : inner + (tile + 1) * 128]
        grad = grad_ref[:, at].astype(jnp.float32) * z * jax.nn.sigmoid(z)
        grad = (grad * spread_heads(carry_ref, tile, rows)).astype(jnp.bfloat16)
        out_ref[:, at] = lax.dot_general(
            c_ref[...], grad, (((0,), (0,)), ((), ())), preferred_element_type=jnp.float32
        ).astype(jnp.bfloat16)


def held_grad(proj, grad, carry, c):
    outs = [((STATE, grad.shape[1]), jnp.bfloat16)]
    return whole_call(held_grad_kernel, (proj, grad, carry, c), outs, [], 4, "held_grad")[0]


def ssm_back_kernel(
    proj_ref,
    tail_ref,
    taps_ref,
    place_ref,
    grad_ref,
    scanned_ref,
    b_ref,
    c_ref,
    cum_ref,
    cum_t_ref,
    step_ref,
    raw_ref,
    rate_ref,
    skip_ref,
    last_ref,
    carry_ref,
    same_ref,
    held_ref,
    later_ref,
    grad_all_ref,
    grad_conv_ref,
    grad_z_ref,
    end_ref,
    grad_tail_ref,
    grad_b_ref,
    grad_c_ref,
    grad_raw_ref,
    grad_taps_ref,
    grad_heads_ref,
    extended,
    sums,
    columns,
):
    rows = b_ref.shape[0]
    inner = taps_ref.shape[1]
    tap_count = taps_ref.shape[0]
    heads = step_ref.shape[1]
    low = jnp.bfloat16

    def dot(a, b, left=1, right=0):
        return lax.dot_general(
            a, b, (((left,), (right,)), ((), ())), preferred_element_type=jnp.float32
        )

    lane = lax.broadcasted_iota(jnp.int32, (rows, 128), 1)
    first_half = lane < SHEAD
    place = place_ref[...]
    b, c = b_ref[...], c_ref[...]
    both = dot(c, b, 1, 1)
    same = same_ref[...] > 0.0
    sums[...] = jnp.zeros_like(sums)
    columns[...] = jnp.zeros_like(columns)
    grad_b = jnp.zeros((rows, STATE), jnp.float32)
    grad_c = jnp.zeros((rows, STATE), jnp.float32)
    grad_both = jnp.zeros((rows, rows), jnp.float32)
    grad_skip = jnp.zeros((1, 128), jnp.float32)
    picker_row = lax.broadcasted_iota(jnp.int32, (128, 128), 0)
    picker_lane = lax.broadcasted_iota(jnp.int32, (128, 128), 1)

    def head_sums(values, tile):
        pick = (picker_lane == 2 * tile + picker_row // SHEAD).astype(low)
        high = values.astype(low)
        rest = (values - high.astype(jnp.float32)).astype(low)
        return dot(high, pick) + dot(rest, pick)

    def spread(ref, tile):
        return jnp.where(
            first_half,
            ref[:, 2 * tile : 2 * tile + 1],
            ref[:, 2 * tile + 1 : 2 * tile + 2],
        )

    for tile in range(inner // 128):
        at = slice(tile * 128, (tile + 1) * 128)
        z_at = slice(inner + tile * 128, inner + (tile + 1) * 128)
        extended[8 : 8 + rows] = proj_ref[:, at]
        extended[0:8] = tail_ref[:, at]
        lagged = []
        summed = jnp.zeros((rows, 128), jnp.float32)
        for lag in range(tap_count):
            moved = extended[8 - lag : 8 - lag + rows]
            moved = moved if lag == 0 else jnp.where(place >= lag, moved, 0.0)
            lagged.append(moved)
            summed = summed + taps_ref[lag : lag + 1, at] * moved
        sigma = jax.nn.sigmoid(summed)
        x = summed * sigma
        step = spread(step_ref, tile)
        scaled = x * step
        z = proj_ref[:, z_at]
        z_sigma = jax.nn.sigmoid(z)
        grad_gated = grad_ref[:, at].astype(jnp.float32)
        grad_y = grad_gated * z * z_sigma
        grad_z_ref[:, at] = (
            grad_gated * scanned_ref[:, at] * (z_sigma * (1.0 + z * (1.0 - z_sigma)))
        ).astype(low)
        held, later = held_ref[:, at].astype(low), later_ref[:, at].astype(low)
        last, carry = spread(last_ref, tile), spread(carry_ref, tile)
        from_later = dot(b, later)
        from_held = dot(c, held)
        grad_b = grad_b + dot((scaled * last).astype(low), later, 1, 1)
        carried_grad = grad_y * carry
        grad_c = grad_c + dot(carried_grad.astype(low), held, 1, 1)
        cum_grad = head_sums(carried_grad * from_held - scaled * last * from_later, tile)
        last_total = head_sums(
            jnp.sum(scaled * last * from_later, axis=0, keepdims=True), tile
        )
        grad_scaled = last * from_later
        grad_skip = grad_skip + head_sums(jnp.sum(grad_y * x, axis=0, keepdims=True), tile)
        grad_low, scaled_low = grad_y.astype(low), scaled.astype(low)
        halves = []
        for k in range(2):
            head = 2 * tile + k
            mine = first_half if k == 0 else ~first_half
            exponent = jnp.where(
                same, cum_ref[:, head : head + 1] - cum_t_ref[head : head + 1, :], -1e30
            )
            fade = jnp.exp(exponent)
            weights = fade * both
            halves.append(dot(weights.astype(low), grad_low, 0, 0))
            grad_weights = dot(jnp.where(mine, grad_y, 0.0).astype(low), scaled_low, 1, 1)
            grad_both = grad_both + grad_weights * fade
            grad_exponent = grad_weights * weights
            columns[head : head + 1, :] = jnp.sum(grad_exponent, axis=0, keepdims=True)
            pick = (picker_lane == head).astype(low)
            high = grad_exponent.astype(low)
            rest = (grad_exponent - high.astype(jnp.float32)).astype(low)
            cum_grad = cum_grad + dot(high, pick) + dot(rest, pick)
        grad_scaled = grad_scaled + jnp.where(first_half, halves[0], halves[1])
        sums[0] += cum_grad
        sums[1] += head_sums(grad_scaled * x, tile)
        sums[2] += last_total
        grad_x = grad_scaled * step + spread(skip_ref, tile) * grad_y
        grad_summed = grad_x * (sigma * (1.0 + summed * (1.0 - sigma)))
        for lag in range(tap_count):
            grad_taps_ref[lag : lag + 1, at] = jnp.sum(
                grad_summed * lagged[lag], axis=0, keepdims=True
            )
        extended[...] = jnp.zeros_like(extended)
        for lag in range(tap_count):
            moved = taps_ref[lag : lag + 1, at] * grad_summed
            moved = moved if lag == 0 else jnp.where(place >= lag, moved, 0.0)
            extended[8 - lag : 8 - lag + rows] += moved
        grad_conv_ref[:, at] = extended[8 : 8 + rows].astype(low)
        end_ref[:, at] = extended[rows : 8 + rows]
        grad_tail_ref[:, at] = extended[0:8]

    grad_c_ref[...] = grad_c + dot(grad_both.astype(low), b)
    grad_b_ref[...] = grad_b + dot(grad_both.astype(low), c, 0, 0)
    row_at = lax.broadcasted_iota(jnp.int32, (rows, 128), 0)
    cum_grad = sums[0] - columns[...].T
    cum_grad = cum_grad + jnp.where(row_at == rows - 1, sums[2] + grad_all_ref[...], 0.0)
    upper = (
        lax.broadcasted_iota(jnp.int32, (rows, rows), 0)
        <= lax.broadcasted_iota(jnp.int32, (rows, rows), 1)
    ).astype(jnp.float32)
    log_grad = jnp.dot(upper, cum_grad, precision=highest, preferred_element_type=jnp.float32)
    log_grad = log_grad[:, :heads]
    rate = rate_ref[...]
    step = step_ref[...]
    raw_grad = (sums[1][:, :heads] - rate * log_grad) * jax.nn.sigmoid(raw_ref[...])
    grad_raw_ref[...] = raw_grad
    grad_heads_ref[0:1, :] = jnp.sum(raw_grad, axis=0, keepdims=True)
    grad_heads_ref[1:2, :] = jnp.sum(-rate * step * log_grad, axis=0, keepdims=True)
    grad_heads_ref[2:3, :] = grad_skip[:, :heads]
    grad_heads_ref[3:8, :] = jnp.zeros((5, heads), jnp.float32)


def ssm_back(*operands):
    proj, taps, b, step = operands[0], operands[2], operands[6], operands[10]
    rows, inner = proj.shape[0], taps.shape[1]
    heads = step.shape[1]
    shape = lambda dims, kind: jax.ShapeDtypeStruct(dims, kind)
    outs = [
        shape((rows, inner), jnp.bfloat16),
        shape((rows, inner), jnp.bfloat16),
        shape((8, inner), jnp.float32),
        shape((8, inner), jnp.float32),
        shape((rows, STATE), jnp.float32),
        shape((rows, STATE), jnp.float32),
        shape((rows, heads), jnp.float32),
        shape(taps.shape, jnp.float32),
        shape((8, heads), jnp.float32),
    ]
    return pl.pallas_call(
        ssm_back_kernel,
        out_shape=outs,
        in_specs=[pl.BlockSpec(memory_space=pltpu.VMEM)] * len(operands),
        out_specs=[pl.BlockSpec(memory_space=pltpu.VMEM)] * len(outs),
        scratch_shapes=[
            pltpu.VMEM((rows + 8, 128), jnp.float32),
            pltpu.VMEM((3, rows, 128), jnp.float32),
            pltpu.VMEM((128, rows), jnp.float32),
        ],
        compiler_params=pltpu.CompilerParams(vmem_limit_bytes=48 * MIB),
        cost_estimate=cost(20),
        name="ssm_back",
    )(*operands)


def from_behind(x, axis, by):
    count = lax.axis_size(axis)
    pairs = [(i, i + by) for i in range(count) if 0 <= i + by < count]
    return lax.ppermute(x, axis, pairs)


def as_sent(x):
    return jax.tree.map(lambda a: a.astype(jnp.bfloat16) if a.dtype == jnp.float32 else a, x)


def gathered(x, groups):
    return lax.all_gather(x, "seq", axis_index_groups=groups, tiled=True)


def summed_rows(x, groups):
    return lax.psum_scatter(x, "seq", scatter_dimension=0, axis_index_groups=groups, tiled=True)


def behind(x, late):
    return x + (0.0 * late.reshape(-1)[0].astype(jnp.float32)).astype(x.dtype)


def corner(x):
    return x[:16, :128]


def after(x, late):
    return lax.optimization_barrier((x, late))[0]


def exchanged(first, second, side, half, late=None):
    send = jnp.where(side == 0, second, first).astype(jnp.bfloat16)
    keep = jnp.where(side == 0, first, second)
    if late is not None:
        send = after(send, late)
    pairs = [(d, (d + half) % (2 * half)) for d in range(2 * half)]
    return keep, lax.ppermute(send, "seq", pairs), send


def swapped(arrays, half, groups, late=None):
    widths = [a.shape[1] // (2 * half) for a in arrays]
    rows = arrays[0].shape[0]
    packed = jnp.concatenate([a.reshape(rows, 2, half, -1) for a in arrays], 3)
    packed = jnp.transpose(packed, (2, 0, 1, 3))
    packed = lax.all_to_all(packed, "seq", 0, 0, axis_index_groups=groups, tiled=True)
    if late is not None:
        packed = behind(packed, late)
    packed = packed.reshape(half * rows, 2, -1)
    out, at = [], 0
    for width in widths:
        out.append([packed[:, k, at : at + width] for k in range(2)])
        at += width
    return out


def rms_scale(entries):
    return entries * lax.rsqrt(jnp.mean(entries * entries, axis=-1, keepdims=True) + eps)


def scaled_norm(entries, gain):
    return rms_scale(entries) * gain


def branch_mix(attn_proj, ssm_proj_out, attn_beta, ssm_beta):
    return attn_beta * rms_scale(attn_proj) + ssm_beta * rms_scale(ssm_proj_out)


def per_device(
    tokens,
    seg_ids,
    meta_index,
    meta_table,
    mixer_gain,
    attn_weight,
    ssm_weight,
    select_weight,
    conv_weight,
    step_bias,
    decay_log,
    skip_gain,
    ssm_down,
    attn_beta,
    ssm_beta,
    ffn_gain,
    gate_up,
    ffn_down,
    cotangent,
):
    row_count = tokens.shape[0]
    model_width = tokens.shape[1]
    kv_width = GROUPS * HEAD
    per_group = HEADS // GROUPS
    qkv_cols = model_width + 2 * kv_width
    score_scale = 1.0 / math.sqrt(HEAD)
    devices = lax.axis_size("seq")
    device_index = lax.axis_index("seq")
    half = devices // 2
    side, place = device_index // half, device_index % half
    groups = [[h * half + q for q in range(half)] for h in range(2)]
    one_hot = (meta_index[:, None] == jnp.arange(META, dtype=jnp.int32)[None, :]).astype(
        jnp.float32
    )
    is_meta = (meta_index < META)[:, None]
    layer_in = jnp.where(
        is_meta,
        jnp.dot(one_hot.astype(jnp.bfloat16), meta_table, preferred_element_type=jnp.float32),
        tokens.astype(jnp.float32),
    )
    normed = scaled_norm(layer_in, mixer_gain).astype(jnp.bfloat16)
    query_weight = attn_weight[:, :model_width]
    kv_weight = attn_weight[:, model_width:qkv_cols]
    cot_rows = gathered(cotangent, groups)
    kv = jnp.dot(normed, kv_weight, preferred_element_type=jnp.float32).astype(jnp.bfloat16)
    kv = after(kv, cot_rows)
    queries = lax.dot_general(
        query_weight, normed, (((0,), (1,)), ((), ())), preferred_element_type=jnp.float32
    )
    queries = (queries.astype(jnp.bfloat16) * score_scale).reshape(
        GROUPS, per_group, HEAD, row_count
    )
    ssm_proj = jnp.dot(normed, ssm_weight, preferred_element_type=jnp.float32)
    select = jnp.dot(normed, select_weight, preferred_element_type=jnp.float32)
    last_rows = ssm_proj[row_count - CONV + 1 :, :INNER].astype(jnp.bfloat16)
    tail_x = jnp.pad(
        from_behind(last_rows, "seq", 1).astype(jnp.float32), ((8 - CONV + 1, 0), (0, 0))
    )
    row = jnp.arange(row_count, dtype=jnp.int32)
    starts = jnp.where((meta_index == 0)[None, :] & (row[None, :] <= row[:, None]), 1, 0)
    items = jnp.sum(starts, axis=1)
    own_start = jnp.max(starts * (row[None, :] + 1), axis=1) - 1 + device_index * row_count
    same_item = ((items[:, None] == items[None, :]) & (row[None, :] <= row[:, None])).astype(
        jnp.float32
    )
    sheads = INNER // SHEAD
    place_in_item = meta_index[:, None]
    rate = jnp.exp(decay_log)[None, :]
    state, b_proj, c_proj, raw, step_size, cum, cum_t, last_weight, carry_weight, decay_all = (
        ssm_state(
            ssm_proj,
            tail_x,
            conv_weight,
            place_in_item,
            items[:, None],
            select,
            step_bias[None, :],
            rate,
        )
    )
    states = lax.all_gather(state, "seq")
    last_start = jnp.where(items[-1] > 0, own_start[-1], -1).astype(jnp.float32)
    facts = jnp.concatenate(
        [decay_all[0], jnp.full((128 - sheads,), 1.0) * last_start]
    )
    facts = jnp.broadcast_to(facts[None, :], (8, 128))
    kv_all, facts = gather_both([kv, facts], half, 0)
    ordered = facts[:, 0].reshape(2, half, 128)
    ordered = jnp.where(side == 0, ordered[::-1], ordered).reshape(devices, 128)
    shard = jnp.arange(devices, dtype=jnp.int32)
    earlier_start = jnp.max(jnp.where(shard < device_index, ordered[:, sheads], -1.0)).astype(
        jnp.int32
    )
    first = jnp.where(items > 0, own_start, earlier_start)
    steps = jnp.stack([device_index, device_index - first[0] // row_count])
    attn_full, log_sum = attend(steps, queries, kv_all, first[None, :], half)
    attended = attn_full.reshape(model_width, row_count).astype(jnp.bfloat16).T
    out_weight = attn_weight[:, qkv_cols:]
    attn_proj = jnp.dot(attended, out_weight.T, preferred_element_type=jnp.float32)
    decays = ordered[:, :sheads]
    between_before = (shard[None, :] > shard[:, None]) & (shard[None, :] < device_index)
    weight_before = jnp.where(
        (shard < device_index)[:, None],
        jnp.prod(jnp.where(between_before[:, :, None], decays[None], 1.0), axis=1),
        0.0,
    )
    between_after = (shard[None, :] < shard[:, None]) & (shard[None, :] > device_index)
    weight_after = jnp.where(
        (shard > device_index)[:, None],
        jnp.prod(jnp.where(between_after[:, :, None], decays[None], 1.0), axis=1),
        0.0,
    )
    per_channel = lambda weight: jnp.repeat(weight, SHEAD, axis=1)[:, None, :]
    held_in = jnp.sum(per_channel(weight_before) * states.astype(jnp.float32), axis=0)
    scanned, gated = ssm_output(
        ssm_proj,
        tail_x,
        conv_weight,
        place_in_item,
        b_proj,
        c_proj,
        cum,
        cum_t,
        step_size,
        skip_gain[None, :],
        carry_weight,
        same_item,
        held_in,
    )
    ssm_proj_out = jnp.dot(gated, ssm_down, preferred_element_type=jnp.float32)
    mixed_terms, mix_pull = jax.vjp(branch_mix, attn_proj, ssm_proj_out, attn_beta, ssm_beta)
    hidden1 = layer_in + mixed_terms
    ffn_in_f, ffn_norm_pull = jax.vjp(scaled_norm, hidden1, ffn_gain)
    normed_rows = gathered(after(normed, state), groups)
    ffn_in = after(ffn_in_f.astype(jnp.bfloat16), normed_rows)
    ffn_rows = gather_half([ffn_in], half, 2).reshape(half * row_count, model_width)
    units = FF // half
    wide = (units + 127) // 128 * 128
    in_weight = jnp.concatenate(
        [
            jnp.pad(
                lax.dynamic_slice_in_dim(gate_up, first_unit + place * units, units, 1),
                ((0, 0), (0, wide - units)),
            )
            for first_unit in (0, FF)
        ],
        1,
    )
    down_weight = jnp.pad(
        lax.dynamic_slice_in_dim(ffn_down, place * units, units, 0), ((0, wide - units), (0, 0))
    )
    out_terms, in_terms, in_weight_terms, down_terms = ffn(
        ffn_rows, cot_rows, in_weight, down_weight
    )
    in_terms = in_terms.reshape(half, row_count, model_width)
    grad_ffn_in = sum_half(in_terms, 1, half, 3)
    gate_keep, gate_sent, _ = exchanged(
        in_weight_terms[:units], in_weight_terms[wide : wide + units], side, half
    )
    down_low = down_terms[:units].astype(jnp.bfloat16).reshape(2, units // 2, model_width)
    down_low = jnp.where(side == 0, down_low, down_low[::-1])
    grad_from_ffn, grad_ffn_gain = ffn_norm_pull(grad_ffn_in)
    grad_hidden1 = cotangent.astype(jnp.float32) + grad_from_ffn
    grad_attn_proj, grad_ssm_proj_out, grad_attn_beta, grad_ssm_beta = mix_pull(grad_hidden1)
    attn_grad_low = grad_attn_proj.astype(jnp.bfloat16)
    ssm_grad_low = grad_ssm_proj_out.astype(jnp.bfloat16)
    grad_gated = jnp.dot(ssm_grad_low, ssm_down.T, preferred_element_type=jnp.float32).astype(
        jnp.bfloat16
    )
    out_grad = (
        lax.dot_general(
            out_weight, attn_grad_low, (((0,), (1,)), ((), ())), preferred_element_type=jnp.float32
        )
        .astype(jnp.bfloat16)
        .reshape(GROUPS, per_group, HEAD, row_count)
    )
    grad_queries, kv_terms = attend_back(
        steps, queries, kv_all, first[None, :], attn_full, log_sum, out_grad, half
    )
    def complete(keep, sent, late):
        return keep + behind(sent.astype(jnp.float32), late)

    gated_columns = swapped([gated], half, groups)[0]
    grad_kv = sum_half(kv_terms, 2, half, 1, corner(gated_columns[0]))
    out_sum = summed_rows(after(out_terms, grad_kv), groups)
    grad_gate_up = complete(gate_keep, gate_sent, grad_queries)
    down_sent = [
        lax.ppermute(
            after(down_low[k], grad_kv),
            "seq",
            [(h * half + q, 2 * q + (h + k) % 2) for h in range(2) for q in range(half)],
        )
        for k in range(2)
    ]
    grad_kv = after(grad_kv, grad_gate_up)
    qkv_grad = jnp.concatenate(
        [grad_queries.reshape(model_width, row_count).T, grad_kv.astype(jnp.bfloat16)], 1
    )
    held_grads = lax.all_gather(held_grad(ssm_proj, grad_gated, carry_weight, c_proj), "seq")
    later_grad = jnp.sum(
        per_channel(behind(weight_after, grad_kv)) * held_grads.astype(jnp.float32), axis=0
    )
    grad_decay_all = jnp.sum((later_grad * held_in).reshape(STATE, sheads, SHEAD), axis=(0, 2))
    grad_all = jnp.pad((grad_decay_all * decay_all[0])[None, :], ((0, 0), (0, 128 - sheads)))
    conv_grad, z_grad, end_rows, grad_tail, grad_b, grad_c, grad_raw, grad_conv, grad_heads = (
        ssm_back(
            ssm_proj,
            tail_x,
            conv_weight,
            place_in_item,
            grad_gated,
            scanned,
            b_proj,
            c_proj,
            cum,
            cum_t,
            step_size,
            raw,
            rate,
            skip_gain[None, :],
            last_weight,
            carry_weight,
            same_item,
            held_in,
            later_grad,
            grad_all,
        )
    )
    attn_columns = swapped(
        [jnp.concatenate([qkv_grad, attended], 1)], half, groups, grad_raw
    )[0]
    attn_grad_rows = gathered(attn_grad_low, groups)
    ssm_grad_rows = gathered(ssm_grad_low, groups)
    attn_terms = []
    for k in range(2):
        block = attn_columns[k]
        width = block.shape[1]
        column = (k * half + place) * width + jnp.arange(width, dtype=jnp.int32)
        attn_terms.append(
            jnp.where(
                (column < qkv_cols)[:, None],
                jnp.dot(block.T, normed_rows, preferred_element_type=jnp.float32),
                jnp.dot(block.T, attn_grad_rows, preferred_element_type=jnp.float32),
            )
        )
    grad_step_bias, grad_decay, grad_skip = grad_heads[0], grad_heads[1], grad_heads[2]
    grad_ffn_down = sum(after(sent, grad_raw).astype(jnp.float32) for sent in down_sent)
    tail_back = from_behind(grad_tail[8 - CONV + 1 :].astype(jnp.bfloat16), "seq", -1)
    end_rows = end_rows[8 - CONV + 1 :] + tail_back.astype(jnp.float32)
    grad_select_in = jnp.concatenate([grad_b, grad_c, grad_raw], 1).astype(jnp.bfloat16)
    attn_keep, attn_sent, attn_send = exchanged(
        attn_terms[0], attn_terms[1], side, half, tail_back
    )
    ssm_down_keep, ssm_down_sent, ssm_down_send = exchanged(
        jnp.dot(gated_columns[0].T, ssm_grad_rows, preferred_element_type=jnp.float32),
        jnp.dot(gated_columns[1].T, ssm_grad_rows, preferred_element_type=jnp.float32),
        side,
        half,
        tail_back,
    )
    conv_grad = jnp.concatenate(
        [conv_grad[: row_count - CONV + 1], end_rows.astype(jnp.bfloat16)], 0
    )
    proj_grad = jnp.concatenate([conv_grad, z_grad], 1)
    ssm_columns = swapped([proj_grad], half, groups)[0]
    grad_normed = jnp.dot(qkv_grad, attn_weight[:, :qkv_cols].T, preferred_element_type=jnp.float32)
    grad_normed = grad_normed + jnp.dot(proj_grad, ssm_weight.T, preferred_element_type=jnp.float32)
    grad_normed = grad_normed + jnp.dot(
        grad_select_in, select_weight.T, preferred_element_type=jnp.float32
    )
    ssm_keep, ssm_sent, ssm_send = exchanged(
        jnp.dot(ssm_columns[0].T, normed_rows, preferred_element_type=jnp.float32),
        jnp.dot(ssm_columns[1].T, normed_rows, preferred_element_type=jnp.float32),
        side,
        half,
    )
    grad_select = jnp.dot(grad_select_in.T, normed, preferred_element_type=jnp.float32)
    mixer_norm_pull = jax.vjp(scaled_norm, layer_in, mixer_gain)[1]
    grad_from_mixer, grad_mixer_gain = mixer_norm_pull(grad_normed)
    grad_layer_in = grad_hidden1 + grad_from_mixer
    grad_tokens = jnp.where(is_meta, 0.0, grad_layer_in).astype(jnp.bfloat16)
    grad_meta = jnp.dot(one_hot.T, jnp.where(is_meta, grad_layer_in, 0.0), precision=highest)
    pieces = [
        grad_meta,
        grad_select,
        grad_conv.reshape(-1, model_width),
        jnp.stack([grad_mixer_gain, grad_attn_beta, grad_ssm_beta, grad_ffn_gain]),
        jnp.pad(
            jnp.concatenate([grad_step_bias, grad_decay, grad_skip])[None, :],
            ((0, 0), (0, model_width - 3 * sheads)),
        ),
    ]
    counts = [piece.shape[0] for piece in pieces]
    share = -(-sum(counts) // (8 * devices)) * 8
    packed = jnp.concatenate(
        pieces + [jnp.zeros((share * devices - sum(counts), model_width), jnp.float32)], 0
    )
    packed = after(
        packed, (attn_send, ssm_down_send, ssm_send, grad_ffn_down)
    )
    packed = total_of(
        packed.reshape(devices, share, model_width),
        devices,
        4,
        corner(ssm_send),
        corner(attn_send),
        corner(ssm_down_send),
    )
    packed = packed.reshape(devices * share, model_width)
    at = [sum(counts[:i]) for i in range(len(counts))]
    gains = packed[at[3] : at[4]]
    little = packed[at[4]]
    small = (
        packed[: counts[0]],
        gains[0],
        packed[at[1] : at[2]].T,
        packed[at[2] : at[3]].reshape(grad_conv.shape),
        little[:sheads],
        little[sheads : 2 * sheads],
        little[2 * sheads : 3 * sheads],
        gains[1],
        gains[2],
        gains[3],
    )
    grad_ssm = complete(ssm_keep, ssm_sent, little)
    late = grad_ssm[0]
    layer_out = (hidden1 + after(out_sum, late).astype(jnp.float32)).astype(jnp.bfloat16)
    shares = (
        complete(attn_keep, attn_sent, late).T,
        grad_ssm.T,
        complete(ssm_down_keep, ssm_down_sent, late),
        grad_gate_up.T,
        grad_ffn_down,
    )
    return (
        layer_out,
        grad_tokens,
        small[0],
        small[1],
        shares[0],
        shares[1],
        small[2],
        small[3],
        small[4],
        small[5],
        small[6],
        shares[2],
        small[7],
        small[8],
        small[9],
        shares[3],
        shares[4],
    )


def solution(mesh):
    placed = (
        P("seq", None),
        P("seq"),
        P("seq"),
        P(),
        P(),
        P(),
        P(),
        P(),
        P(),
        P(),
        P(),
        P(),
        P(),
        P(),
        P(),
        P(),
        P(),
        P(),
        P("seq", None),
    )
    return jax.shard_map(
        per_device,
        mesh=mesh,
        in_specs=placed,
        out_specs=(
            P("seq", None),
            P("seq", None),
            P(),
            P(),
            P(None, "seq"),
            P(None, "seq"),
            P(),
            P(),
            P(),
            P(),
            P(),
            P("seq", None),
            P(),
            P(),
            P(),
            P(None, "seq"),
            P("seq", None),
        ),
        check_vma=False,
    )
```

```python
from functools import partial
import math

import jax
import jax.numpy as jnp
from jax import lax
from jax.experimental import pallas as pl
from jax.experimental.pallas import tpu as pltpu
from jax.sharding import PartitionSpec as P

HEADS = 25
GROUPS = 5
HEAD = 64
INNER = 3200
STATE = 16
CONV = 4
FF = 5504
META = 128
SHEAD = 64


eps = 1e-05
highest = lax.Precision.HIGHEST


MESH = pl.DeviceIdType.MESH
MIB = 2**20


def cost(microseconds):
    return pl.CostEstimate(
        flops=0, transcendentals=0, bytes_accessed=int(microseconds * 3_000_000)
    )


def flipped(v, k):
    bit = 1 << k
    return jnp.where(lax.rem(v // bit, 2) == 0, v + bit, v - bit)


def flips_of(v, bits):
    out = [v]
    for k in bits:
        out = out + [flipped(o, k) for o in out]
    return out


def thirds(rows):
    most = (rows // 3 + 15) // 16 * 16
    return [(0, most), (most, most), (2 * most, rows - 2 * most)]


def parts_of(rows):
    return [part for part in thirds(rows) if part[1] > 0] if rows >= 48 else [(0, rows)]


def greet(partners):
    barrier = pltpu.get_barrier_semaphore()
    for partner in partners:
        pl.semaphore_signal(barrier, inc=1, device_id=(partner,), device_id_type=MESH)
    pl.semaphore_wait(barrier, len(partners))


def remote(src, dst, send, recv, device):
    return pltpu.make_async_remote_copy(
        src_ref=src,
        dst_ref=dst,
        send_sem=send,
        recv_sem=recv,
        device_id=(device,),
        device_id_type=MESH,
    )


def gather_kernel(arrays, half, *refs):
    ins, out = refs[:arrays], refs[arrays]
    send, recv, core_send, core_recv, local_sem = refs[arrays + 1 :]
    me = lax.axis_index("seq")
    place = lax.rem(me, half)
    bits = half.bit_length() - 1
    greet([flipped(me, k) for k in range(bits)])
    parts = thirds(ins[0].shape[0])
    links = bits - 1
    orders = [[1 + (c + s) % links for s in range(links)] for c in range(3)]
    local = [
        pltpu.make_async_copy(ins[a], out.at[a * half + place], local_sem.at[a])
        for a in range(arrays)
    ]
    for copy in local:
        copy.start()
    sent, handed = [], []
    for step in range(links + 1):
        arriving = []
        for c, (first, count) in enumerate(parts):
            rows = pl.ds(first, count)
            held = flips_of(place, orders[c][:step])
            for a in range(arrays):
                if step < links:
                    for i, b in enumerate(held):
                        place_at = out.at[a * half + b, rows]
                        at = (1 << step) - 1 + i
                        copy = remote(
                            ins[a].at[rows] if i == 0 else place_at,
                            place_at,
                            send.at[a, c, at],
                            recv.at[a, c, at],
                            flipped(me, orders[c][step]),
                        )
                        copy.start()
                        arriving.append(copy)
                new = held if step == 0 else held[len(held) // 2 :]
                for i, b in enumerate(new):
                    place_at = out.at[a * half + b, rows]
                    at = 0 if step == 0 else (1 << (step - 1)) + i
                    copy = remote(
                        ins[a].at[rows] if step == 0 else place_at,
                        place_at,
                        core_send.at[a, c, at],
                        core_recv.at[a, c, at],
                        flipped(me, 0),
                    )
                    copy.start()
                    handed.append(copy)
        for copy in arriving:
            copy.wait_recv()
        sent += arriving
    for copy in sent:
        copy.wait_send()
    for copy in handed:
        copy.wait()
    for copy in local:
        copy.wait()


def gather_half(arrays, half, collective_id):
    count = len(arrays)
    shape = arrays[0].shape
    semaphores = pltpu.SemaphoreType.DMA((count, 3, half // 2))
    return pl.pallas_call(
        partial(gather_kernel, count, half),
        out_shape=jax.ShapeDtypeStruct((count * half,) + shape, arrays[0].dtype),
        in_specs=[pl.BlockSpec(memory_space=pl.ANY)] * count,
        out_specs=pl.BlockSpec(memory_space=pl.ANY),
        scratch_shapes=[semaphores] * 4 + [pltpu.SemaphoreType.DMA((count,))],
        compiler_params=pltpu.CompilerParams(collective_id=collective_id, has_side_effects=True),
        cost_estimate=cost(40),
        name="gather_half",
    )(*arrays)


def gather_both_kernel(arrays, half, *refs):
    ins, outs = refs[:arrays], refs[arrays : 2 * arrays]
    send, recv, core_send, core_recv, flip_send, flip_recv, local_sem = refs[2 * arrays :]
    me = lax.axis_index("seq")
    place = lax.rem(me, half)
    twin = jnp.where(me < half, me + half, me - half)
    bits = half.bit_length() - 1
    greet([flipped(me, k) for k in range(bits)] + [twin])
    links = bits - 1
    orders = [[1 + (c + s) % links for s in range(links)] for c in range(3)]
    parts = [parts_of(ref.shape[0]) for ref in ins]
    local, sent, handed, twins = [], [], [], []
    for a in range(arrays):
        copy = remote(ins[a], outs[a].at[place], flip_send.at[a], flip_recv.at[a], twin)
        copy.start()
        twins.append(copy)
        copy = pltpu.make_async_copy(ins[a], outs[a].at[half + place], local_sem.at[a])
        copy.start()
        local.append(copy)
    for time in range(links + 2):
        arriving = []
        for own in (1, 0):
            step = time - (1 - own)
            if step < 0 or step > links:
                continue
            for a in range(arrays):
                for c, (first, count) in enumerate(parts[a]):
                    rows = pl.ds(first, count)
                    slot = own * arrays + a
                    held = flips_of(place, orders[c][:step])
                    if step < links:
                        for i, b in enumerate(held):
                            place_at = outs[a].at[own * half + b, rows]
                            at = (1 << step) - 1 + i
                            copy = remote(
                                ins[a].at[rows] if i == 0 and own else place_at,
                                place_at,
                                send.at[slot, c, at],
                                recv.at[slot, c, at],
                                flipped(me, orders[c][step]),
                            )
                            copy.start()
                            arriving.append(copy)
                    new = held if step == 0 else held[len(held) // 2 :]
                    for i, b in enumerate(new):
                        place_at = outs[a].at[own * half + b, rows]
                        at = 0 if step == 0 else (1 << (step - 1)) + i
                        copy = remote(
                            ins[a].at[rows] if step == 0 and own else place_at,
                            place_at,
                            core_send.at[slot, c, at],
                            core_recv.at[slot, c, at],
                            flipped(me, 0),
                        )
                        copy.start()
                        handed.append(copy)
        if time == 0:
            for copy in twins:
                copy.wait_recv()
        for copy in arriving:
            copy.wait_recv()
        sent += arriving
    for copy in sent + twins:
        copy.wait_send()
    for copy in handed:
        copy.wait()
    for copy in local:
        copy.wait()


def gather_both(arrays, half, collective_id):
    count = len(arrays)
    semaphores = pltpu.SemaphoreType.DMA((2 * count, 3, half // 2))
    single = pltpu.SemaphoreType.DMA((count,))
    return pl.pallas_call(
        partial(gather_both_kernel, count, half),
        out_shape=[jax.ShapeDtypeStruct((2 * half,) + a.shape, a.dtype) for a in arrays],
        in_specs=[pl.BlockSpec(memory_space=pl.ANY)] * count,
        out_specs=[pl.BlockSpec(memory_space=pl.ANY)] * count,
        scratch_shapes=[semaphores] * 4 + [single] * 3,
        compiler_params=pltpu.CompilerParams(collective_id=collective_id, has_side_effects=True),
        cost_estimate=cost(50),
        name="gather_both",
    )(*arrays)


def total_kernel(devices, terms, out, mine, core_in, link_in, send, recv, send_back, recv_back):
    me = lax.axis_index("seq")
    bits = devices.bit_length() - 1
    greet([flipped(me, k) for k in range(bits)])
    pairs = devices // 2
    columns = terms.shape[2]
    third = columns // 3 // 128 * 128
    parts = [(0, third), (third, third), (2 * third, columns - 2 * third)]
    turned = min(3, bits - 1)
    orders = [
        [1 + (c + s) % turned for s in range(turned)] + list(range(1 + turned, bits))
        for c in range(3)
    ]
    everything = pl.ds(0, columns)
    copies = []
    first = []
    for i in range(pairs):
        block = 2 * i + 1 - lax.rem(me, 2)
        copy = remote(
            terms.at[block], core_in.at[i], send.at[0, i], recv.at[0, i], flipped(me, 0)
        )
        copy.start()
        first.append(copy)
    copies += first
    for i in range(pairs):
        first[i].wait_recv()
        mine[i] = terms[2 * i + lax.rem(me, 2)] + core_in[i]
    for step in range(bits - 1):
        arriving = []
        for c, (start, count) in enumerate(parts):
            lanes = pl.ds(start, count)
            for i, b in enumerate(flips_of(me, orders[c][step + 1 :])):
                away = flipped(b, orders[c][step])
                at = pairs - (pairs >> step) + i
                copy = remote(
                    mine.at[away // 2, :, lanes],
                    link_in.at[at, :, lanes],
                    send.at[1 + c, at],
                    recv.at[1 + c, at],
                    flipped(me, orders[c][step]),
                )
                copy.start()
                arriving.append((copy, b, at, lanes))
        for copy, b, at, lanes in arriving:
            copy.wait_recv()
            mine[b // 2, :, lanes] = mine[b // 2, :, lanes] + link_in[at, :, lanes]
            copies.append(copy)
    out[me] = mine[me // 2]
    for step in range(bits - 1):
        arriving = []
        for c, (start, count) in enumerate(parts):
            lanes = pl.ds(start, count)
            order = orders[c][::-1]
            for i, b in enumerate(flips_of(me, order[:step])):
                at = (1 << step) - 1 + i
                copy = remote(
                    out.at[b, :, lanes],
                    out.at[b, :, lanes],
                    send_back.at[1 + c, at],
                    recv_back.at[1 + c, at],
                    flipped(me, order[step]),
                )
                copy.start()
                arriving.append(copy)
        for copy in arriving:
            copy.wait_recv()
        copies += arriving
    last = []
    for i, b in enumerate(flips_of(me, range(1, bits))):
        copy = remote(
            out.at[b], out.at[b], send_back.at[0, i], recv_back.at[0, i], flipped(me, 0)
        )
        copy.start()
        last.append(copy)
    for copy in last:
        copy.wait()
    for copy in copies:
        copy.wait_send()


def total_of(terms, devices, collective_id, *early):
    pairs = devices // 2
    half_shape = (pairs,) + terms.shape[1:]
    semaphores = pltpu.SemaphoreType.DMA((4, pairs))
    return pl.pallas_call(
        lambda terms, *refs: total_kernel(devices, terms, *refs[len(early) :]),
        out_shape=jax.ShapeDtypeStruct(terms.shape, terms.dtype),
        in_specs=[pl.BlockSpec(memory_space=pltpu.VMEM)]
        + [pl.BlockSpec(memory_space=pl.ANY)] * len(early),
        out_specs=pl.BlockSpec(memory_space=pltpu.VMEM),
        scratch_shapes=[pltpu.VMEM(half_shape, terms.dtype)] * 3 + [semaphores] * 4,
        compiler_params=pltpu.CompilerParams(
            collective_id=collective_id, has_side_effects=True, vmem_limit_bytes=48 * MIB
        ),
        cost_estimate=cost(40),
        name="total_of",
    )(terms, *early)


def sum_kernel(arrays, half, *refs):
    terms, out = refs[:2]
    mine, core_in, link_in, load_sem, send, recv, core_send, core_recv, flip_in, flip_sem = refs[2:]
    me = lax.axis_index("seq")
    place = lax.rem(me, half)
    bits = half.bit_length() - 1
    twin = jnp.where(me < half, me + half, me - half)
    greet([flipped(me, k) for k in range(bits)] + ([twin] if arrays == 2 else []))
    parts = thirds(terms.shape[1])
    links = bits - 1
    orders = [[1 + (c + s) % links for s in range(links)] for c in range(3)]
    loads = []
    pairs = half // 2
    for a in range(arrays):
        for i in range(pairs):
            block = 2 * i + lax.rem(place, 2)
            copy = pltpu.make_async_copy(
                terms.at[a * half + block], mine.at[a, i], load_sem.at[a, i]
            )
            copy.start()
            loads.append(copy)
    handed = {}
    for wanted in range(2):
        for c, (first, count) in enumerate(parts):
            rows = pl.ds(first, count)
            kept = flips_of(place, orders[c][1:])
            blocks = kept if wanted else [flipped(b, orders[c][0]) for b in kept]
            for a in range(arrays):
                for i, b in enumerate(blocks):
                    at = wanted * (pairs // 2) + i
                    copy = remote(
                        terms.at[a * half + flipped(b, 0), rows],
                        core_in.at[a, at, rows],
                        core_send.at[a, c, at],
                        core_recv.at[a, c, at],
                        flipped(me, 0),
                    )
                    copy.start()
                    handed[a, c, at] = copy
    for copy in loads:
        copy.wait()
    sent = []
    arriving = {}

    def add(ref, slot, rows, other):
        ref[slot, rows] = (
            ref[slot, rows].astype(jnp.float32) + other[...].astype(jnp.float32)
        ).astype(ref.dtype)

    for step in range(links):
        for c, (first, count) in enumerate(parts):
            rows = pl.ds(first, count)
            kept = flips_of(place, orders[c][step + 1 :])
            for a in range(arrays):
                for i, b in enumerate(kept):
                    out_block = flipped(b, orders[c][step])
                    if step == 0:
                        handed[a, c, i].wait_recv()
                        add(mine.at[a], out_block // 2, rows, core_in.at[a, i, rows])
                    at = pairs - (pairs >> step) + i
                    copy = remote(
                        mine.at[a, out_block // 2, rows],
                        link_in.at[a, at, rows],
                        send.at[a, c, at],
                        recv.at[a, c, at],
                        flipped(me, orders[c][step]),
                    )
                    copy.start()
                    arriving[a, c, at] = copy
                    sent.append(copy)
        if step == 0:
            for c, (first, count) in enumerate(parts):
                rows = pl.ds(first, count)
                for a in range(arrays):
                    for i, b in enumerate(flips_of(place, orders[c][1:])):
                        at = pairs // 2 + i
                        handed[a, c, at].wait_recv()
                        add(mine.at[a], b // 2, rows, core_in.at[a, at, rows])
        for c, (first, count) in enumerate(parts):
            rows = pl.ds(first, count)
            kept = flips_of(place, orders[c][step + 1 :])
            for a in range(arrays):
                for i, b in enumerate(kept):
                    at = pairs - (pairs >> step) + i
                    arriving[a, c, at].wait_recv()
                    add(mine.at[a], b // 2, rows, link_in.at[a, at, rows])
    if arrays == 2:
        flip = remote(mine.at[0, place // 2], flip_in, flip_sem.at[0], flip_sem.at[1], twin)
        flip.start()
        flip.wait_recv()
        out[...] = mine[1, place // 2].astype(jnp.float32) + flip_in[...].astype(jnp.float32)
        sent.append(flip)
    else:
        out[...] = mine[0, place // 2].astype(jnp.float32)
    for copy in sent:
        copy.wait_send()
    for copy in handed.values():
        copy.wait_send()


def sum_half(terms, arrays, half, collective_id, *early):
    rows, columns = terms.shape[1:]
    pairs = half // 2
    block = (rows, columns)
    semaphores = pltpu.SemaphoreType.DMA((arrays, 3, pairs))
    return pl.pallas_call(
        lambda terms, *refs: sum_kernel(arrays, half, terms, *refs[len(early) :]),
        out_shape=jax.ShapeDtypeStruct(block, jnp.float32),
        in_specs=[pl.BlockSpec(memory_space=pl.ANY)] * (1 + len(early)),
        out_specs=pl.BlockSpec(memory_space=pltpu.VMEM),
        scratch_shapes=[
            pltpu.VMEM((arrays, pairs) + block, terms.dtype),
            pltpu.VMEM((arrays, pairs) + block, terms.dtype),
            pltpu.VMEM((arrays, pairs) + block, terms.dtype),
            pltpu.SemaphoreType.DMA((arrays, pairs)),
        ]
        + [semaphores] * 4
        + [
            pltpu.VMEM(block if arrays == 2 else (16, 128), terms.dtype),
            pltpu.SemaphoreType.DMA((2,)),
        ],
        compiler_params=pltpu.CompilerParams(
            collective_id=collective_id, has_side_effects=True, vmem_limit_bytes=60 * MIB
        ),
        cost_estimate=cost(50),
        name="sum_half",
    )(terms, *early)


def ffn_kernel(x_ref, cot_ref, in_ref, down_ref, out_ref, grad_in_ref, grad_w_ref, grad_d_ref):
    wide = down_ref.shape[0]
    x, cot = x_ref[...], cot_ref[...]
    low = jnp.bfloat16

    def dot(a, b, contract):
        return lax.dot_general(a, b, (contract, ((), ())), preferred_element_type=jnp.float32)

    vals = dot(x, in_ref[...], ((1,), (0,)))
    gate, up = vals[:, :wide], vals[:, wide:]
    sigma = jax.nn.sigmoid(gate)
    act = gate * sigma
    hidden = (act * up).astype(low)
    out_ref[...] = dot(hidden, down_ref[...], ((1,), (0,))).astype(low)
    grad_hidden = dot(cot, down_ref[...], ((1,), (1,))).astype(low).astype(jnp.float32)
    slope = sigma * (1.0 + gate * (1.0 - sigma))
    grads = jnp.concatenate([grad_hidden * up * slope, grad_hidden * act], 1).astype(low)
    grad_in_ref[...] = dot(grads, in_ref[...], ((1,), (1,))).astype(low)

    @pl.when(pl.program_id(0) == 0)
    def _():
        grad_w_ref[...] = jnp.zeros_like(grad_w_ref)
        grad_d_ref[...] = jnp.zeros_like(grad_d_ref)

    grad_w_ref[...] += dot(grads, x, ((0,), (0,)))
    grad_d_ref[...] += dot(hidden, cot, ((0,), (0,)))


def ffn(x, cot, in_weight, down_weight):
    rows, model = x.shape
    block = min(256, rows)
    wide = down_weight.shape[0]
    moving = pl.BlockSpec((block, model), lambda i: (i, 0))
    fixed = lambda shape: pl.BlockSpec(shape, lambda i: (0, 0))
    return pl.pallas_call(
        ffn_kernel,
        grid=(rows // block,),
        out_shape=[
            jax.ShapeDtypeStruct(x.shape, jnp.bfloat16),
            jax.ShapeDtypeStruct(x.shape, jnp.bfloat16),
            jax.ShapeDtypeStruct((2 * wide, model), jnp.float32),
            jax.ShapeDtypeStruct((wide, model), jnp.float32),
        ],
        in_specs=[moving, moving, fixed(in_weight.shape), fixed(down_weight.shape)],
        out_specs=[moving, moving, fixed((2 * wide, model)), fixed((wide, model))],
        compiler_params=pltpu.CompilerParams(vmem_limit_bytes=56 * MIB),
        cost_estimate=cost(35),
        name="ffn",
    )(x, cot, in_weight, down_weight)


def masked_block(at, first_ref, device_index, rows):
    key = lax.broadcasted_iota(jnp.int32, (rows, rows), 0) + at * rows
    query = lax.broadcasted_iota(jnp.int32, (rows, rows), 1) + device_index * rows
    seen = ((key >= first_ref[...]) & (key <= query)).astype(jnp.float32)
    return jnp.concatenate([seen] * (HEADS // GROUPS), 1) > 0.0


def side_by_side(ref, g):
    return jnp.concatenate([ref[g, j] for j in range(HEADS // GROUPS)], 1)


def over_shards(steps_ref, body):
    body(0)

    @pl.loop(1, steps_ref[1] + 1)
    def _(hop):
        body(hop)


def attend_kernel(half, steps_ref, q_ref, kv_ref, first_ref, out_ref, log_ref, top, total, acc):
    device_index, newest = steps_ref[0], half + lax.rem(steps_ref[0], half)
    rows = kv_ref.shape[1]
    top[...] = jnp.full_like(top, -1e30)
    total[...] = jnp.zeros_like(total)
    acc[...] = jnp.zeros_like(acc)

    def body(hop):
        block = kv_ref[newest - hop]
        seen = masked_block(device_index - hop, first_ref, device_index, rows)
        for g in range(GROUPS):
            keys = block[:, g * HEAD : (g + 1) * HEAD]
            values = block[:, (GROUPS + g) * HEAD : (GROUPS + g + 1) * HEAD]
            scores = jnp.dot(keys, side_by_side(q_ref, g), preferred_element_type=jnp.float32)
            scores = jnp.where(seen, scores, -1e30)
            now = jnp.maximum(top[g], jnp.max(scores, axis=0, keepdims=True))
            probs = jnp.exp(scores - now)
            fade = jnp.exp(top[g] - now)
            top[g] = now
            total[g] = total[g] * fade + jnp.sum(probs, axis=0, keepdims=True)
            acc[g] = acc[g] * fade + lax.dot_general(
                values,
                probs.astype(jnp.bfloat16),
                (((0,), (0,)), ((), ())),
                preferred_element_type=jnp.float32,
            )

    over_shards(steps_ref, body)
    for g in range(GROUPS):
        done = acc[g] / total[g]
        for j in range(HEADS // GROUPS):
            out_ref[g, j] = done[:, j * rows : (j + 1) * rows]
        log_ref[g] = top[g] + jnp.log(total[g])


def attend(steps, queries, kv, first, half):
    rows = kv.shape[1]
    per_group = HEADS // GROUPS
    wide = per_group * rows
    return pl.pallas_call(
        partial(attend_kernel, half),
        out_shape=[
            jax.ShapeDtypeStruct((GROUPS, per_group, HEAD, rows), jnp.float32),
            jax.ShapeDtypeStruct((GROUPS, 1, wide), jnp.float32),
        ],
        in_specs=[pl.BlockSpec(memory_space=pltpu.SMEM)]
        + [pl.BlockSpec(memory_space=pltpu.VMEM)] * 3,
        out_specs=[pl.BlockSpec(memory_space=pltpu.VMEM)] * 2,
        scratch_shapes=[
            pltpu.VMEM((GROUPS, 1, wide), jnp.float32),
            pltpu.VMEM((GROUPS, 1, wide), jnp.float32),
            pltpu.VMEM((GROUPS, HEAD, wide), jnp.float32),
        ],
        compiler_params=pltpu.CompilerParams(vmem_limit_bytes=56 * MIB),
        cost_estimate=cost(15),
        name="attend",
    )(steps, queries, kv, first)


def attend_back_kernel(
    half,
    steps_ref,
    q_ref,
    kv_ref,
    first_ref,
    out_ref,
    log_ref,
    grad_ref,
    grad_q_ref,
    grad_kv_ref,
    dots,
    acc,
):
    device_index, newest = steps_ref[0], half + lax.rem(steps_ref[0], half)
    rows = kv_ref.shape[1]
    contract = lambda a, b, i: lax.dot_general(
        a, b, (((i,), (i,)), ((), ())), preferred_element_type=jnp.float32
    )
    for g in range(GROUPS):
        product = side_by_side(out_ref, g) * side_by_side(grad_ref, g).astype(jnp.float32)
        dots[g] = jnp.sum(product, axis=0, keepdims=True)
    acc[...] = jnp.zeros_like(acc)

    @pl.loop(0, 2 * half)
    def _(i):
        grad_kv_ref[i] = jnp.zeros(grad_kv_ref.shape[1:], grad_kv_ref.dtype)

    def body(hop):
        block = kv_ref[newest - hop]
        seen = masked_block(device_index - hop, first_ref, device_index, rows)
        grad_keys, grad_values = [], []
        for g in range(GROUPS):
            keys = block[:, g * HEAD : (g + 1) * HEAD]
            values = block[:, (GROUPS + g) * HEAD : (GROUPS + g + 1) * HEAD]
            queries, grads = side_by_side(q_ref, g), side_by_side(grad_ref, g)
            scores = jnp.dot(keys, queries, preferred_element_type=jnp.float32)
            probs = jnp.where(seen, jnp.exp(scores - log_ref[g]), 0.0)
            grad_probs = jnp.dot(values, grads, preferred_element_type=jnp.float32)
            grad_values.append(contract(probs.astype(jnp.bfloat16), grads, 1))
            grad_scores = (probs * (grad_probs - dots[g])).astype(jnp.bfloat16)
            grad_keys.append(contract(grad_scores, queries, 1))
            acc[g] += contract(keys, grad_scores, 0)
        grad_kv_ref[newest - hop] = jnp.concatenate(grad_keys + grad_values, 1).astype(
            grad_kv_ref.dtype
        )

    over_shards(steps_ref, body)
    for g in range(GROUPS):
        for j in range(HEADS // GROUPS):
            grad_q_ref[g, j] = (acc[g, :, j * rows : (j + 1) * rows] * (HEAD**-0.5)).astype(
                grad_q_ref.dtype
            )


def attend_back(steps, queries, kv, first, out, log_sum, grads, half):
    rows = kv.shape[1]
    wide = HEADS // GROUPS * rows
    return pl.pallas_call(
        partial(attend_back_kernel, half),
        out_shape=[
            jax.ShapeDtypeStruct(queries.shape, jnp.bfloat16),
            jax.ShapeDtypeStruct(kv.shape, jnp.bfloat16),
        ],
        in_specs=[pl.BlockSpec(memory_space=pltpu.SMEM)]
        + [pl.BlockSpec(memory_space=pltpu.VMEM)] * 6,
        out_specs=[pl.BlockSpec(memory_space=pltpu.VMEM)] * 2,
        scratch_shapes=[
            pltpu.VMEM((GROUPS, 1, wide), jnp.float32),
            pltpu.VMEM((GROUPS, HEAD, wide), jnp.float32),
        ],
        compiler_params=pltpu.CompilerParams(vmem_limit_bytes=60 * MIB),
        cost_estimate=cost(20),
        name="attend_back",
    )(steps, queries, kv, first, out, log_sum, grads)


def spread_heads(ref, tile, rows):
    first_half = lax.broadcasted_iota(jnp.int32, (rows, 128), 1) < SHEAD
    return jnp.where(
        first_half, ref[:, 2 * tile : 2 * tile + 1], ref[:, 2 * tile + 1 : 2 * tile + 2]
    )


def conv_tile(proj_ref, tail_ref, taps_ref, place, extended, at, rows):
    extended[8 : 8 + rows] = proj_ref[:, at]
    extended[0:8] = tail_ref[:, at]
    lagged = []
    summed = jnp.zeros((rows, 128), jnp.float32)
    for lag in range(taps_ref.shape[0]):
        moved = extended[8 - lag : 8 - lag + rows]
        moved = moved if lag == 0 else jnp.where(place >= lag, moved, 0.0)
        lagged.append(moved)
        summed = summed + taps_ref[lag : lag + 1, at] * moved
    return summed, lagged


def ssm_state_kernel(
    proj_ref,
    tail_ref,
    taps_ref,
    place_ref,
    items_ref,
    select_ref,
    bias_ref,
    rate_ref,
    state_ref,
    b_ref,
    c_ref,
    raw_ref,
    step_ref,
    cum_ref,
    cum_t_ref,
    last_ref,
    carry_ref,
    all_ref,
    extended,
):
    rows, inner = proj_ref.shape[0], taps_ref.shape[1]
    heads = step_ref.shape[1]
    low = jnp.bfloat16
    b_ref[...] = select_ref[:, :STATE].astype(low)
    c_ref[...] = select_ref[:, STATE : 2 * STATE].astype(low)
    raw = select_ref[:, 2 * STATE :] + bias_ref[...]
    raw_ref[...] = raw
    step = jnp.maximum(raw, 0.0) + jnp.log1p(jnp.exp(-jnp.abs(raw)))
    step_ref[...] = step
    lower = (
        lax.broadcasted_iota(jnp.int32, (rows, rows), 0)
        >= lax.broadcasted_iota(jnp.int32, (rows, rows), 1)
    ).astype(jnp.float32)
    cum = jnp.dot(
        lower, -step * rate_ref[...], precision=highest, preferred_element_type=jnp.float32
    )
    cum_ref[...] = cum
    wide = jnp.concatenate([cum, jnp.zeros((rows, 128 - heads), jnp.float32)], 1)
    cum_t_ref[...] = wide.T[:heads]
    items = items_ref[...]
    final = items_ref[rows - 1 : rows, :]
    total = cum[rows - 1 : rows, :]
    last_ref[...] = jnp.where(items == final, jnp.exp(total - cum), 0.0)
    carry_ref[...] = jnp.where(items == 0, jnp.exp(cum), 0.0)
    all_ref[...] = jnp.where(final == 0, jnp.exp(total), 0.0)
    place = place_ref[...]
    b = b_ref[...]
    for tile in range(inner // 128):
        at = slice(tile * 128, (tile + 1) * 128)
        summed, _ = conv_tile(proj_ref, tail_ref, taps_ref, place, extended, at, rows)
        x = summed * jax.nn.sigmoid(summed)
        taken = x * spread_heads(step_ref, tile, rows) * spread_heads(last_ref, tile, rows)
        state_ref[:, at] = lax.dot_general(
            b, taken.astype(low), (((0,), (0,)), ((), ())), preferred_element_type=jnp.float32
        ).astype(low)


def whole_call(kernel, operands, outs, scratch, microseconds, name):
    return pl.pallas_call(
        kernel,
        out_shape=[jax.ShapeDtypeStruct(dims, kind) for dims, kind in outs],
        in_specs=[pl.BlockSpec(memory_space=pltpu.VMEM)] * len(operands),
        out_specs=[pl.BlockSpec(memory_space=pltpu.VMEM)] * len(outs),
        scratch_shapes=scratch,
        compiler_params=pltpu.CompilerParams(vmem_limit_bytes=48 * MIB),
        cost_estimate=cost(microseconds),
        name=name,
    )(*operands)


def ssm_state(proj, tail, taps, place, items, select, bias, rate):
    rows, inner, heads = proj.shape[0], taps.shape[1], bias.shape[1]
    low, full = jnp.bfloat16, jnp.float32
    by_head = ((rows, heads), full)
    outs = [((STATE, inner), low), ((rows, STATE), low), ((rows, STATE), low)]
    outs += [by_head, by_head, by_head, ((heads, rows), full), by_head, by_head]
    outs += [((1, heads), full)]
    operands = (proj, tail, taps, place, items, select, bias, rate)
    scratch = [pltpu.VMEM((rows + 8, 128), full)]
    return whole_call(ssm_state_kernel, operands, outs, scratch, 8, "ssm_state")


def ssm_output_kernel(
    proj_ref,
    tail_ref,
    taps_ref,
    place_ref,
    b_ref,
    c_ref,
    cum_ref,
    cum_t_ref,
    step_ref,
    skip_ref,
    carry_ref,
    same_ref,
    held_ref,
    scanned_ref,
    gated_ref,
    extended,
):
    rows, inner = proj_ref.shape[0], taps_ref.shape[1]
    low = jnp.bfloat16
    place, c = place_ref[...], c_ref[...]
    both = lax.dot_general(
        c, b_ref[...], (((1,), (1,)), ((), ())), preferred_element_type=jnp.float32
    )
    same = same_ref[...] > 0.0
    first_half = lax.broadcasted_iota(jnp.int32, (rows, 128), 1) < SHEAD
    for tile in range(inner // 128):
        at = slice(tile * 128, (tile + 1) * 128)
        summed, _ = conv_tile(proj_ref, tail_ref, taps_ref, place, extended, at, rows)
        x = summed * jax.nn.sigmoid(summed)
        scaled = (x * spread_heads(step_ref, tile, rows)).astype(low)
        halves = []
        for k in range(2):
            head = 2 * tile + k
            exponent = jnp.where(
                same, cum_ref[:, head : head + 1] - cum_t_ref[head : head + 1, :], -1e30
            )
            weights = (jnp.exp(exponent) * both).astype(low)
            halves.append(jnp.dot(weights, scaled, preferred_element_type=jnp.float32))
        carried = jnp.dot(c, held_ref[:, at].astype(low), preferred_element_type=jnp.float32)
        out = (
            jnp.where(first_half, halves[0], halves[1])
            + carried * spread_heads(carry_ref, tile, rows)
            + spread_heads(skip_ref, tile, rows) * x
        )
        scanned_ref[:, at] = out
        z = proj_ref[:, inner + tile * 128 : inner + (tile + 1) * 128]
        gated_ref[:, at] = (out * z * jax.nn.sigmoid(z)).astype(low)


def ssm_output(*operands):
    rows, inner = operands[0].shape[0], operands[2].shape[1]
    outs = [((rows, inner), jnp.float32), ((rows, inner), jnp.bfloat16)]
    scratch = [pltpu.VMEM((rows + 8, 128), jnp.float32)]
    return whole_call(ssm_output_kernel, operands, outs, scratch, 8, "ssm_output")


def held_grad_kernel(proj_ref, grad_ref, carry_ref, c_ref, out_ref):
    rows, inner = grad_ref.shape
    for tile in range(inner // 128):
        at = slice(tile * 128, (tile + 1) * 128)
        z = proj_ref[:, inner + tile * 128 : inner + (tile + 1) * 128]
        grad = grad_ref[:, at].astype(jnp.float32) * z * jax.nn.sigmoid(z)
        grad = (grad * spread_heads(carry_ref, tile, rows)).astype(jnp.bfloat16)
        out_ref[:, at] = lax.dot_general(
            c_ref[...], grad, (((0,), (0,)), ((), ())), preferred_element_type=jnp.float32
        ).astype(jnp.bfloat16)


def held_grad(proj, grad, carry, c):
    outs = [((STATE, grad.shape[1]), jnp.bfloat16)]
    return whole_call(held_grad_kernel, (proj, grad, carry, c), outs, [], 4, "held_grad")[0]


def ssm_back_kernel(
    proj_ref,
    tail_ref,
    taps_ref,
    place_ref,
    grad_ref,
    scanned_ref,
    b_ref,
    c_ref,
    cum_ref,
    cum_t_ref,
    step_ref,
    raw_ref,
    rate_ref,
    skip_ref,
    last_ref,
    carry_ref,
    same_ref,
    held_ref,
    later_ref,
    grad_all_ref,
    grad_conv_ref,
    grad_z_ref,
    end_ref,
    grad_tail_ref,
    grad_b_ref,
    grad_c_ref,
    grad_raw_ref,
    grad_taps_ref,
    grad_heads_ref,
    extended,
    sums,
    columns,
):
    rows = b_ref.shape[0]
    inner = taps_ref.shape[1]
    tap_count = taps_ref.shape[0]
    heads = step_ref.shape[1]
    low = jnp.bfloat16

    def dot(a, b, left=1, right=0):
        return lax.dot_general(
            a, b, (((left,), (right,)), ((), ())), preferred_element_type=jnp.float32
        )

    lane = lax.broadcasted_iota(jnp.int32, (rows, 128), 1)
    first_half = lane < SHEAD
    place = place_ref[...]
    b, c = b_ref[...], c_ref[...]
    both = dot(c, b, 1, 1)
    same = same_ref[...] > 0.0
    sums[...] = jnp.zeros_like(sums)
    columns[...] = jnp.zeros_like(columns)
    grad_b = jnp.zeros((rows, STATE), jnp.float32)
    grad_c = jnp.zeros((rows, STATE), jnp.float32)
    grad_both = jnp.zeros((rows, rows), jnp.float32)
    grad_skip = jnp.zeros((1, 128), jnp.float32)
    picker_row = lax.broadcasted_iota(jnp.int32, (128, 128), 0)
    picker_lane = lax.broadcasted_iota(jnp.int32, (128, 128), 1)

    def head_sums(values, tile):
        pick = (picker_lane == 2 * tile + picker_row // SHEAD).astype(low)
        high = values.astype(low)
        rest = (values - high.astype(jnp.float32)).astype(low)
        return dot(high, pick) + dot(rest, pick)

    def spread(ref, tile):
        return jnp.where(
            first_half,
            ref[:, 2 * tile : 2 * tile + 1],
            ref[:, 2 * tile + 1 : 2 * tile + 2],
        )

    for tile in range(inner // 128):
        at = slice(tile * 128, (tile + 1) * 128)
        z_at = slice(inner + tile * 128, inner + (tile + 1) * 128)
        extended[8 : 8 + rows] = proj_ref[:, at]
        extended[0:8] = tail_ref[:, at]
        lagged = []
        summed = jnp.zeros((rows, 128), jnp.float32)
        for lag in range(tap_count):
            moved = extended[8 - lag : 8 - lag + rows]
            moved = moved if lag == 0 else jnp.where(place >= lag, moved, 0.0)
            lagged.append(moved)
            summed = summed + taps_ref[lag : lag + 1, at] * moved
        sigma = jax.nn.sigmoid(summed)
        x = summed * sigma
        step = spread(step_ref, tile)
        scaled = x * step
        z = proj_ref[:, z_at]
        z_sigma = jax.nn.sigmoid(z)
        grad_gated = grad_ref[:, at].astype(jnp.float32)
        grad_y = grad_gated * z * z_sigma
        grad_z_ref[:, at] = (
            grad_gated * scanned_ref[:, at] * (z_sigma * (1.0 + z * (1.0 - z_sigma)))
        ).astype(low)
        held, later = held_ref[:, at].astype(low), later_ref[:, at].astype(low)
        last, carry = spread(last_ref, tile), spread(carry_ref, tile)
        from_later = dot(b, later)
        from_held = dot(c, held)
        grad_b = grad_b + dot((scaled * last).astype(low), later, 1, 1)
        carried_grad = grad_y * carry
        grad_c = grad_c + dot(carried_grad.astype(low), held, 1, 1)
        cum_grad = head_sums(carried_grad * from_held - scaled * last * from_later, tile)
        last_total = head_sums(
            jnp.sum(scaled * last * from_later, axis=0, keepdims=True), tile
        )
        grad_scaled = last * from_later
        grad_skip = grad_skip + head_sums(jnp.sum(grad_y * x, axis=0, keepdims=True), tile)
        grad_low, scaled_low = grad_y.astype(low), scaled.astype(low)
        halves = []
        for k in range(2):
            head = 2 * tile + k
            mine = first_half if k == 0 else ~first_half
            exponent = jnp.where(
                same, cum_ref[:, head : head + 1] - cum_t_ref[head : head + 1, :], -1e30
            )
            fade = jnp.exp(exponent)
            weights = fade * both
            halves.append(dot(weights.astype(low), grad_low, 0, 0))
            grad_weights = dot(jnp.where(mine, grad_y, 0.0).astype(low), scaled_low, 1, 1)
            grad_both = grad_both + grad_weights * fade
            grad_exponent = grad_weights * weights
            columns[head : head + 1, :] = jnp.sum(grad_exponent, axis=0, keepdims=True)
            pick = (picker_lane == head).astype(low)
            high = grad_exponent.astype(low)
            rest = (grad_exponent - high.astype(jnp.float32)).astype(low)
            cum_grad = cum_grad + dot(high, pick) + dot(rest, pick)
        grad_scaled = grad_scaled + jnp.where(first_half, halves[0], halves[1])
        sums[0] += cum_grad
        sums[1] += head_sums(grad_scaled * x, tile)
        sums[2] += last_total
        grad_x = grad_scaled * step + spread(skip_ref, tile) * grad_y
        grad_summed = grad_x * (sigma * (1.0 + summed * (1.0 - sigma)))
        for lag in range(tap_count):
            grad_taps_ref[lag : lag + 1, at] = jnp.sum(
                grad_summed * lagged[lag], axis=0, keepdims=True
            )
        extended[...] = jnp.zeros_like(extended)
        for lag in range(tap_count):
            moved = taps_ref[lag : lag + 1, at] * grad_summed
            moved = moved if lag == 0 else jnp.where(place >= lag, moved, 0.0)
            extended[8 - lag : 8 - lag + rows] += moved
        grad_conv_ref[:, at] = extended[8 : 8 + rows].astype(low)
        end_ref[:, at] = extended[rows : 8 + rows]
        grad_tail_ref[:, at] = extended[0:8]

    grad_c_ref[...] = grad_c + dot(grad_both.astype(low), b)
    grad_b_ref[...] = grad_b + dot(grad_both.astype(low), c, 0, 0)
    row_at = lax.broadcasted_iota(jnp.int32, (rows, 128), 0)
    cum_grad = sums[0] - columns[...].T
    cum_grad = cum_grad + jnp.where(row_at == rows - 1, sums[2] + grad_all_ref[...], 0.0)
    upper = (
        lax.broadcasted_iota(jnp.int32, (rows, rows), 0)
        <= lax.broadcasted_iota(jnp.int32, (rows, rows), 1)
    ).astype(jnp.float32)
    log_grad = jnp.dot(upper, cum_grad, precision=highest, preferred_element_type=jnp.float32)
    log_grad = log_grad[:, :heads]
    rate = rate_ref[...]
    step = step_ref[...]
    raw_grad = (sums[1][:, :heads] - rate * log_grad) * jax.nn.sigmoid(raw_ref[...])
    grad_raw_ref[...] = raw_grad
    grad_heads_ref[0:1, :] = jnp.sum(raw_grad, axis=0, keepdims=True)
    grad_heads_ref[1:2, :] = jnp.sum(-rate * step * log_grad, axis=0, keepdims=True)
    grad_heads_ref[2:3, :] = grad_skip[:, :heads]
    grad_heads_ref[3:8, :] = jnp.zeros((5, heads), jnp.float32)


def ssm_back(*operands):
    proj, taps, b, step = operands[0], operands[2], operands[6], operands[10]
    rows, inner = proj.shape[0], taps.shape[1]
    heads = step.shape[1]
    shape = lambda dims, kind: jax.ShapeDtypeStruct(dims, kind)
    outs = [
        shape((rows, inner), jnp.bfloat16),
        shape((rows, inner), jnp.bfloat16),
        shape((8, inner), jnp.float32),
        shape((8, inner), jnp.float32),
        shape((rows, STATE), jnp.float32),
        shape((rows, STATE), jnp.float32),
        shape((rows, heads), jnp.float32),
        shape(taps.shape, jnp.float32),
        shape((8, heads), jnp.float32),
    ]
    return pl.pallas_call(
        ssm_back_kernel,
        out_shape=outs,
        in_specs=[pl.BlockSpec(memory_space=pltpu.VMEM)] * len(operands),
        out_specs=[pl.BlockSpec(memory_space=pltpu.VMEM)] * len(outs),
        scratch_shapes=[
            pltpu.VMEM((rows + 8, 128), jnp.float32),
            pltpu.VMEM((3, rows, 128), jnp.float32),
            pltpu.VMEM((128, rows), jnp.float32),
        ],
        compiler_params=pltpu.CompilerParams(vmem_limit_bytes=48 * MIB),
        cost_estimate=cost(20),
        name="ssm_back",
    )(*operands)


def from_behind(x, axis, by):
    count = lax.axis_size(axis)
    pairs = [(i, i + by) for i in range(count) if 0 <= i + by < count]
    return lax.ppermute(x, axis, pairs)


def as_sent(x):
    return jax.tree.map(lambda a: a.astype(jnp.bfloat16) if a.dtype == jnp.float32 else a, x)


def gathered(x, groups):
    return lax.all_gather(x, "seq", axis_index_groups=groups, tiled=True)


def summed_rows(x, groups):
    return lax.psum_scatter(x, "seq", scatter_dimension=0, axis_index_groups=groups, tiled=True)


def behind(x, late):
    return x + (0.0 * late.reshape(-1)[0].astype(jnp.float32)).astype(x.dtype)


def corner(x):
    return x[:16, :128]


def after(x, late):
    return lax.optimization_barrier((x, late))[0]


def exchanged(first, second, side, half, late=None):
    send = jnp.where(side == 0, second, first).astype(jnp.bfloat16)
    keep = jnp.where(side == 0, first, second)
    if late is not None:
        send = after(send, late)
    pairs = [(d, (d + half) % (2 * half)) for d in range(2 * half)]
    return keep, lax.ppermute(send, "seq", pairs), send


def swapped(arrays, half, groups, late=None):
    widths = [a.shape[1] // (2 * half) for a in arrays]
    rows = arrays[0].shape[0]
    packed = jnp.concatenate([a.reshape(rows, 2, half, -1) for a in arrays], 3)
    packed = jnp.transpose(packed, (2, 0, 1, 3))
    packed = lax.all_to_all(packed, "seq", 0, 0, axis_index_groups=groups, tiled=True)
    if late is not None:
        packed = behind(packed, late)
    packed = packed.reshape(half * rows, 2, -1)
    out, at = [], 0
    for width in widths:
        out.append([packed[:, k, at : at + width] for k in range(2)])
        at += width
    return out


def rms_scale(entries):
    return entries * lax.rsqrt(jnp.mean(entries * entries, axis=-1, keepdims=True) + eps)


def scaled_norm(entries, gain):
    return rms_scale(entries) * gain


def branch_mix(attn_proj, ssm_proj_out, attn_beta, ssm_beta):
    return attn_beta * rms_scale(attn_proj) + ssm_beta * rms_scale(ssm_proj_out)


def per_device(
    tokens,
    seg_ids,
    meta_index,
    meta_table,
    mixer_gain,
    attn_weight,
    ssm_weight,
    select_weight,
    conv_weight,
    step_bias,
    decay_log,
    skip_gain,
    ssm_down,
    attn_beta,
    ssm_beta,
    ffn_gain,
    gate_up,
    ffn_down,
    cotangent,
):
    row_count = tokens.shape[0]
    model_width = tokens.shape[1]
    kv_width = GROUPS * HEAD
    per_group = HEADS // GROUPS
    qkv_cols = model_width + 2 * kv_width
    score_scale = 1.0 / math.sqrt(HEAD)
    devices = lax.axis_size("seq")
    device_index = lax.axis_index("seq")
    half = devices // 2
    side, place = device_index // half, device_index % half
    groups = [[h * half + q for q in range(half)] for h in range(2)]
    one_hot = (meta_index[:, None] == jnp.arange(META, dtype=jnp.int32)[None, :]).astype(
        jnp.float32
    )
    is_meta = (meta_index < META)[:, None]
    layer_in = jnp.where(
        is_meta,
        jnp.dot(one_hot.astype(jnp.bfloat16), meta_table, preferred_element_type=jnp.float32),
        tokens.astype(jnp.float32),
    )
    normed = scaled_norm(layer_in, mixer_gain).astype(jnp.bfloat16)
    query_weight = attn_weight[:, :model_width]
    kv_weight = attn_weight[:, model_width:qkv_cols]
    cot_rows = gathered(cotangent, groups)
    kv = jnp.dot(normed, kv_weight, preferred_element_type=jnp.float32).astype(jnp.bfloat16)
    kv = after(kv, cot_rows)
    queries = lax.dot_general(
        query_weight, normed, (((0,), (1,)), ((), ())), preferred_element_type=jnp.float32
    )
    queries = (queries.astype(jnp.bfloat16) * score_scale).reshape(
        GROUPS, per_group, HEAD, row_count
    )
    ssm_proj = jnp.dot(normed, ssm_weight, preferred_element_type=jnp.float32)
    select = jnp.dot(normed, select_weight, preferred_element_type=jnp.float32)
    last_rows = ssm_proj[row_count - CONV + 1 :, :INNER].astype(jnp.bfloat16)
    tail_x = jnp.pad(
        from_behind(last_rows, "seq", 1).astype(jnp.float32), ((8 - CONV + 1, 0), (0, 0))
    )
    row = jnp.arange(row_count, dtype=jnp.int32)
    starts = jnp.where((meta_index == 0)[None, :] & (row[None, :] <= row[:, None]), 1, 0)
    items = jnp.sum(starts, axis=1)
    own_start = jnp.max(starts * (row[None, :] + 1), axis=1) - 1 + device_index * row_count
    same_item = ((items[:, None] == items[None, :]) & (row[None, :] <= row[:, None])).astype(
        jnp.float32
    )
    sheads = INNER // SHEAD
    place_in_item = meta_index[:, None]
    rate = jnp.exp(decay_log)[None, :]
    state, b_proj, c_proj, raw, step_size, cum, cum_t, last_weight, carry_weight, decay_all = (
        ssm_state(
            ssm_proj,
            tail_x,
            conv_weight,
            place_in_item,
            items[:, None],
            select,
            step_bias[None, :],
            rate,
        )
    )
    states = lax.all_gather(state, "seq")
    last_start = jnp.where(items[-1] > 0, own_start[-1], -1).astype(jnp.float32)
    facts = jnp.concatenate(
        [decay_all[0], jnp.full((128 - sheads,), 1.0) * last_start]
    )
    facts = jnp.broadcast_to(facts[None, :], (8, 128))
    kv_all, facts = gather_both([kv, facts], half, 0)
    ordered = facts[:, 0].reshape(2, half, 128)
    ordered = jnp.where(side == 0, ordered[::-1], ordered).reshape(devices, 128)
    shard = jnp.arange(devices, dtype=jnp.int32)
    earlier_start = jnp.max(jnp.where(shard < device_index, ordered[:, sheads], -1.0)).astype(
        jnp.int32
    )
    first = jnp.where(items > 0, own_start, earlier_start)
    steps = jnp.stack([device_index, device_index - first[0] // row_count])
    attn_full, log_sum = attend(steps, queries, kv_all, first[None, :], half)
    attended = attn_full.reshape(model_width, row_count).astype(jnp.bfloat16).T
    out_weight = attn_weight[:, qkv_cols:]
    attn_proj = jnp.dot(attended, out_weight.T, preferred_element_type=jnp.float32)
    decays = ordered[:, :sheads]
    between_before = (shard[None, :] > shard[:, None]) & (shard[None, :] < device_index)
    weight_before = jnp.where(
        (shard < device_index)[:, None],
        jnp.prod(jnp.where(between_before[:, :, None], decays[None], 1.0), axis=1),
        0.0,
    )
    between_after = (shard[None, :] < shard[:, None]) & (shard[None, :] > device_index)
    weight_after = jnp.where(
        (shard > device_index)[:, None],
        jnp.prod(jnp.where(between_after[:, :, None], decays[None], 1.0), axis=1),
        0.0,
    )
    per_channel = lambda weight: jnp.repeat(weight, SHEAD, axis=1)[:, None, :]
    held_in = jnp.sum(per_channel(weight_before) * states.astype(jnp.float32), axis=0)
    scanned, gated = ssm_output(
        ssm_proj,
        tail_x,
        conv_weight,
        place_in_item,
        b_proj,
        c_proj,
        cum,
        cum_t,
        step_size,
        skip_gain[None, :],
        carry_weight,
        same_item,
        held_in,
    )
    ssm_proj_out = jnp.dot(gated, ssm_down, preferred_element_type=jnp.float32)
    mixed_terms, mix_pull = jax.vjp(branch_mix, attn_proj, ssm_proj_out, attn_beta, ssm_beta)
    hidden1 = layer_in + mixed_terms
    ffn_in_f, ffn_norm_pull = jax.vjp(scaled_norm, hidden1, ffn_gain)
    normed_rows = gathered(after(normed, state), groups)
    ffn_in = after(ffn_in_f.astype(jnp.bfloat16), normed_rows)
    ffn_rows = gather_half([ffn_in], half, 2).reshape(half * row_count, model_width)
    units = FF // half
    wide = (units + 127) // 128 * 128
    in_weight = jnp.concatenate(
        [
            jnp.pad(
                lax.dynamic_slice_in_dim(gate_up, first_unit + place * units, units, 1),
                ((0, 0), (0, wide - units)),
            )
            for first_unit in (0, FF)
        ],
        1,
    )
    down_weight = jnp.pad(
        lax.dynamic_slice_in_dim(ffn_down, place * units, units, 0), ((0, wide - units), (0, 0))
    )
    out_terms, in_terms, in_weight_terms, down_terms = ffn(
        ffn_rows, cot_rows, in_weight, down_weight
    )
    in_terms = in_terms.reshape(half, row_count, model_width)
    grad_ffn_in = sum_half(in_terms, 1, half, 3)
    gate_keep, gate_sent, _ = exchanged(
        in_weight_terms[:units], in_weight_terms[wide : wide + units], side, half
    )
    down_low = down_terms[:units].astype(jnp.bfloat16).reshape(2, units // 2, model_width)
    down_low = jnp.where(side == 0, down_low, down_low[::-1])
    grad_from_ffn, grad_ffn_gain = ffn_norm_pull(grad_ffn_in)
    grad_hidden1 = cotangent.astype(jnp.float32) + grad_from_ffn
    grad_attn_proj, grad_ssm_proj_out, grad_attn_beta, grad_ssm_beta = mix_pull(grad_hidden1)
    attn_grad_low = grad_attn_proj.astype(jnp.bfloat16)
    ssm_grad_low = grad_ssm_proj_out.astype(jnp.bfloat16)
    grad_gated = jnp.dot(ssm_grad_low, ssm_down.T, preferred_element_type=jnp.float32).astype(
        jnp.bfloat16
    )
    out_grad = (
        lax.dot_general(
            out_weight, attn_grad_low, (((0,), (1,)), ((), ())), preferred_element_type=jnp.float32
        )
        .astype(jnp.bfloat16)
        .reshape(GROUPS, per_group, HEAD, row_count)
    )
    grad_queries, kv_terms = attend_back(
        steps, queries, kv_all, first[None, :], attn_full, log_sum, out_grad, half
    )
    def complete(keep, sent, late):
        return keep + behind(sent.astype(jnp.float32), late)

    gated_columns = swapped([gated], half, groups)[0]
    grad_kv = sum_half(kv_terms, 2, half, 1, corner(gated_columns[0]))
    out_sum = summed_rows(after(out_terms, grad_kv), groups)
    grad_gate_up = complete(gate_keep, gate_sent, grad_queries)
    down_sent = [
        lax.ppermute(
            after(down_low[k], grad_kv),
            "seq",
            [(h * half + q, 2 * q + (h + k) % 2) for h in range(2) for q in range(half)],
        )
        for k in range(2)
    ]
    grad_kv = after(grad_kv, grad_gate_up)
    qkv_grad = jnp.concatenate(
        [grad_queries.reshape(model_width, row_count).T, grad_kv.astype(jnp.bfloat16)], 1
    )
    held_grads = lax.all_gather(held_grad(ssm_proj, grad_gated, carry_weight, c_proj), "seq")
    later_grad = jnp.sum(
        per_channel(behind(weight_after, grad_kv)) * held_grads.astype(jnp.float32), axis=0
    )
    grad_decay_all = jnp.sum((later_grad * held_in).reshape(STATE, sheads, SHEAD), axis=(0, 2))
    grad_all = jnp.pad((grad_decay_all * decay_all[0])[None, :], ((0, 0), (0, 128 - sheads)))
    conv_grad, z_grad, end_rows, grad_tail, grad_b, grad_c, grad_raw, grad_conv, grad_heads = (
        ssm_back(
            ssm_proj,
            tail_x,
            conv_weight,
            place_in_item,
            grad_gated,
            scanned,
            b_proj,
            c_proj,
            cum,
            cum_t,
            step_size,
            raw,
            rate,
            skip_gain[None, :],
            last_weight,
            carry_weight,
            same_item,
            held_in,
            later_grad,
            grad_all,
        )
    )
    attn_columns = swapped(
        [jnp.concatenate([qkv_grad, attended], 1)], half, groups, grad_raw
    )[0]
    attn_grad_rows = gathered(attn_grad_low, groups)
    ssm_grad_rows = gathered(ssm_grad_low, groups)
    attn_terms = []
    for k in range(2):
        block = attn_columns[k]
        width = block.shape[1]
        column = (k * half + place) * width + jnp.arange(width, dtype=jnp.int32)
        attn_terms.append(
            jnp.where(
                (column < qkv_cols)[:, None],
                jnp.dot(block.T, normed_rows, preferred_element_type=jnp.float32),
                jnp.dot(block.T, attn_grad_rows, preferred_element_type=jnp.float32),
            )
        )
    grad_step_bias, grad_decay, grad_skip = grad_heads[0], grad_heads[1], grad_heads[2]
    grad_ffn_down = sum(after(sent, grad_raw).astype(jnp.float32) for sent in down_sent)
    tail_back = from_behind(grad_tail[8 - CONV + 1 :].astype(jnp.bfloat16), "seq", -1)
    end_rows = end_rows[8 - CONV + 1 :] + tail_back.astype(jnp.float32)
    grad_select_in = jnp.concatenate([grad_b, grad_c, grad_raw], 1).astype(jnp.bfloat16)
    attn_keep, attn_sent, attn_send = exchanged(
        attn_terms[0], attn_terms[1], side, half, tail_back
    )
    conv_grad = jnp.concatenate(
        [conv_grad[: row_count - CONV + 1], end_rows.astype(jnp.bfloat16)], 0
    )
    proj_grad = jnp.concatenate([conv_grad, z_grad], 1)
    proj_grad = behind(proj_grad, attn_send)
    ssm_columns = swapped([proj_grad], half, groups)[0]
    gated_columns = [behind(block, ssm_columns[0]) for block in gated_columns]
    ssm_down_keep, ssm_down_sent, ssm_down_send = exchanged(
        jnp.dot(gated_columns[0].T, ssm_grad_rows, preferred_element_type=jnp.float32),
        jnp.dot(gated_columns[1].T, ssm_grad_rows, preferred_element_type=jnp.float32),
        side,
        half,
        tail_back,
    )
    grad_normed = jnp.dot(qkv_grad, attn_weight[:, :qkv_cols].T, preferred_element_type=jnp.float32)
    grad_normed = grad_normed + jnp.dot(proj_grad, ssm_weight.T, preferred_element_type=jnp.float32)
    grad_normed = grad_normed + jnp.dot(
        grad_select_in, select_weight.T, preferred_element_type=jnp.float32
    )
    ssm_keep, ssm_sent, ssm_send = exchanged(
        jnp.dot(ssm_columns[0].T, normed_rows, preferred_element_type=jnp.float32),
        jnp.dot(ssm_columns[1].T, normed_rows, preferred_element_type=jnp.float32),
        side,
        half,
    )
    grad_select = jnp.dot(grad_select_in.T, normed, preferred_element_type=jnp.float32)
    mixer_norm_pull = jax.vjp(scaled_norm, layer_in, mixer_gain)[1]
    grad_from_mixer, grad_mixer_gain = mixer_norm_pull(grad_normed)
    grad_layer_in = grad_hidden1 + grad_from_mixer
    grad_tokens = jnp.where(is_meta, 0.0, grad_layer_in).astype(jnp.bfloat16)
    grad_meta = jnp.dot(one_hot.T, jnp.where(is_meta, grad_layer_in, 0.0), precision=highest)
    pieces = [
        grad_meta,
        grad_select,
        grad_conv.reshape(-1, model_width),
        jnp.stack([grad_mixer_gain, grad_attn_beta, grad_ssm_beta, grad_ffn_gain]),
        jnp.pad(
            jnp.concatenate([grad_step_bias, grad_decay, grad_skip])[None, :],
            ((0, 0), (0, model_width - 3 * sheads)),
        ),
    ]
    counts = [piece.shape[0] for piece in pieces]
    share = -(-sum(counts) // (8 * devices)) * 8
    packed = jnp.concatenate(
        pieces + [jnp.zeros((share * devices - sum(counts), model_width), jnp.float32)], 0
    )
    packed = after(
        packed, (attn_send, ssm_down_send, ssm_send, grad_ffn_down)
    )
    packed = total_of(
        packed.reshape(devices, share, model_width),
        devices,
        4,
        corner(ssm_send),
        corner(attn_send),
        corner(ssm_down_send),
    )
    packed = packed.reshape(devices * share, model_width)
    at = [sum(counts[:i]) for i in range(len(counts))]
    gains = packed[at[3] : at[4]]
    little = packed[at[4]]
    small = (
        packed[: counts[0]],
        gains[0],
        packed[at[1] : at[2]].T,
        packed[at[2] : at[3]].reshape(grad_conv.shape),
        little[:sheads],
        little[sheads : 2 * sheads],
        little[2 * sheads : 3 * sheads],
        gains[1],
        gains[2],
        gains[3],
    )
    grad_ssm = complete(ssm_keep, ssm_sent, little)
    late = grad_ssm[0]
    layer_out = (hidden1 + behind(out_sum.astype(jnp.float32), late)).astype(jnp.bfloat16)
    shares = (
        complete(attn_keep, attn_sent, late).T,
        grad_ssm.T,
        complete(ssm_down_keep, ssm_down_sent, late),
        grad_gate_up.T,
        grad_ffn_down,
    )
    return (
        layer_out,
        grad_tokens,
        small[0],
        small[1],
        shares[0],
        shares[1],
        small[2],
        small[3],
        small[4],
        small[5],
        small[6],
        shares[2],
        small[7],
        small[8],
        small[9],
        shares[3],
        shares[4],
    )


def solution(mesh):
    placed = (
        P("seq", None),
        P("seq"),
        P("seq"),
        P(),
        P(),
        P(),
        P(),
        P(),
        P(),
        P(),
        P(),
        P(),
        P(),
        P(),
        P(),
        P(),
        P(),
        P(),
        P("seq", None),
    )
    return jax.shard_map(
        per_device,
        mesh=mesh,
        in_specs=placed,
        out_specs=(
            P("seq", None),
            P("seq", None),
            P(),
            P(),
            P(None, "seq"),
            P(None, "seq"),
            P(),
            P(),
            P(),
            P(),
            P(),
            P("seq", None),
            P(),
            P(),
            P(),
            P(None, "seq"),
            P("seq", None),
        ),
        check_vma=False,
    )
```
